256 devices in a mesh: gx: 8 (over z), gy: 32 (over y, x, core).
Axes of the slice: x: 4, y: 4, z: 8, core: 2. Of those that a mesh axis runs over, the one named last changes fastest.
Arguments:
- right_side: float32 [64, 64, 4096], P(None, 'gx', 'gy'), may hold values from -4 to 4
- alpha: float32 [64, 64, 4096], P(None, 'gx', 'gy'), may hold values from 0.0001 to 1
- beta: float32 [64, 64, 4096], P(None, 'gx', 'gy'), may hold values from 0.5 to 2
Outputs:
- solution_field: float32 [64, 64, 4096], P(None, 'gx', 'gy')
- residual: float32 [64, 64, 4096], P(None, 'gx', 'gy')
The draws below stay inside these ranges and needn't reach their ends.
All inputs are finite; a program needn't handle non-finite values.
Results may differ from the reference program's by a relative error of at most 0.0003.
Values sent between devices are 32-bit elements; how exact they have to be, the bound alone decides.
No kernel may reach another device: no remote copies, remote signals or barrier semaphores. Data moves between devices by JAX's collectives and lax.ppermute only.
A program may use at most 128 MiB of HBM per device.

```python
import math
import jax
import jax.numpy as jnp

NZ = 64
LEVELS = 4
SMOOTHS = 3
BOTTOM = 12
NX = 64
NY = 4096


def draw_right_side(key, part):
    key = jax.random.fold_in(key, 11)
    first_key = jax.random.fold_in(key, 0)
    extent = (NZ, NX, NY)
    return jnp.clip(jax.random.normal(first_key, extent, jnp.float32), -4.0, 4.0)


def draw_alpha(key, part):
    key = jax.random.fold_in(key, 23)
    first_key = jax.random.fold_in(key, 0)
    extent = (NZ, NX, NY)
    return 0.01 * jnp.exp(jax.random.uniform(first_key, extent, jnp.float32, 0.0, math.log(100.0)))


def block_levels(own_key, shape, shards, smallest, top_value):
    factor_of, own = 1.0, jax.random.fold_in(own_key, 6)
    for dim, parts in shards:
        steps = jnp.exp(jax.random.uniform(jax.random.fold_in(own, dim), (parts,), jnp.float32, smallest / len(shards), top_value / len(shards)))
        factor_of = factor_of * jnp.repeat(steps, shape[dim] // parts).reshape([-1 if axis == dim else 1 for axis in range(len(shape))])
    return factor_of


def setup_inputs(seed: int = 0) -> dict:
    splits = jax.random.split(jax.random.key(seed), 4)
    return {
        "right_side": draw_right_side(jax.random.fold_in(splits[3], 71), 0),
        "alpha": draw_alpha(jax.random.fold_in(splits[3], 71), 0),
        "beta": jnp.clip(jnp.exp(math.log(2.0) - 1.3862944 * jax.random.uniform(splits[2], (NZ, NX, NY), jnp.float32) ** block_levels(splits[2], (NZ, NX, NY), ((1, 8), (2, 32)), -0.2, 0.2)), 0.5, 2.0),
    }


def face_weights(padded_beta, factor):
    centre = padded_beta[:, 1:-1, 1:-1]
    along_z = jnp.pad(centre, ((1, 1), (0, 0), (0, 0)))
    face_z = factor * (0.5 * (along_z[1:] + along_z[:-1]))
    face_x = factor * (0.5 * (padded_beta[:, 1:, 1:-1] + padded_beta[:, :-1, 1:-1]))
    face_y = factor * (0.5 * (padded_beta[:, 1:-1, 1:] + padded_beta[:, 1:-1, :-1]))
    return face_z, face_x, face_y


def build_level(alpha_level, padded_beta, factor):
    face_z, face_x, face_y = face_weights(padded_beta, factor)
    diagonal = alpha_level + (face_z[1:] + face_z[:-1] + face_x[:, 1:] + face_x[:, :-1] + face_y[:, :, 1:] + face_y[:, :, :-1])
    return diagonal, face_z, face_x, face_y


def apply_rims(padded, operator):
    diagonal, face_z, face_x, face_y = operator
    centre = padded[:, 1:-1, 1:-1]
    along_z = jnp.pad(centre, ((1, 1), (0, 0), (0, 0)))
    beside = face_z[:-1] * along_z[:-2] + face_z[1:] * along_z[2:]
    beside = beside + face_x[:, :-1] * padded[:, :-2, 1:-1] + face_x[:, 1:] * padded[:, 2:, 1:-1]
    beside = beside + face_y[:, :, :-1] * padded[:, 1:-1, :-2] + face_y[:, :, 1:] * padded[:, 1:-1, 2:]
    return diagonal * centre - beside


def zero_rims(field):
    return jnp.pad(field, ((0, 0), (1, 1), (1, 1)))


def coarsen(field):
    planes, across, along = field.shape
    return field.reshape(planes // 2, 2, across // 2, 2, along // 2, 2).mean(axis=(1, 3, 5))


def refine(field):
    planes, across, along = field.shape
    wide = jnp.broadcast_to(field[:, None, :, None, :, None], (planes, 2, across, 2, along, 2))
    return wide.reshape(2 * planes, 2 * across, 2 * along)


def relax_once(iterate, source, operator, weight, rims_fn):
    return iterate + (weight * (source - apply_rims(rims_fn(iterate), operator))) / operator[0]


def reference(right_side, alpha, beta):
    alpha_levels = [alpha]
    beta_levels = [beta]
    for height in range(1, LEVELS):
        alpha_levels.append(coarsen(alpha_levels[-1]))
        beta_levels.append(coarsen(beta_levels[-1]))
    operators = [build_level(alpha_levels[height], zero_rims(beta_levels[height]), 0.25 ** height) for height in range(LEVELS)]
    sources = []
    smoothed = []
    source = right_side
    for height in range(LEVELS - 1):
        iterate = jnp.zeros_like(source)
        for turn in range(SMOOTHS):
            iterate = relax_once(iterate, source, operators[height], 0.6 + 0.15 * (turn % 3), zero_rims)
        sources.append(source)
        smoothed.append(iterate)
        source = coarsen(source - apply_rims(zero_rims(iterate), operators[height]))
    iterate = jnp.zeros_like(source)
    for turn in range(BOTTOM):
        iterate = relax_once(iterate, source, operators[-1], 0.8, zero_rims)
    for height in reversed(range(LEVELS - 1)):
        iterate = smoothed[height] + refine(iterate)
        source = sources[height]
        for turn in range(SMOOTHS):
            iterate = relax_once(iterate, source, operators[height], 0.6 + 0.15 * (turn % 3), zero_rims)
    residual = right_side - apply_rims(zero_rims(iterate), operators[0])
    return iterate, residual
```

```python
import functools

import jax
import jax.numpy as jnp
from jax import lax
from jax.experimental import pallas as pl
from jax.experimental.pallas import tpu as pltpu
from jax.sharding import PartitionSpec as P

F32 = jnp.float32
WEIGHTS = (0.6, 0.75, 0.9)
BOTTOM_WEIGHT = 0.8
BOTTOM = 12
YH = 20


def roll(x, shift, axis):
    shift %= x.shape[axis]
    return x if shift == 0 else pltpu.roll(x, shift, axis)


def iota(shape, axis):
    return lax.broadcasted_iota(jnp.int32, shape, axis)


def either(flag, a, b):
    return jnp.where(flag, a, b)


def only(flag, a):
    return jnp.where(flag, a, 0.0)


def matmul(a, b):
    return jnp.dot(a, b, precision=lax.Precision.HIGHEST, preferred_element_type=F32)


def indicator(mask):
    return jnp.where(mask, 1.0, 0.0).astype(F32)


def half_wrapped(i, low, high):
    return jnp.where(i < high, i // 2, jnp.where(i >= low, 64 + i // 2, -1))


class Level:
    def __init__(self, refs, factor, circular, unroll):
        self.f, self.a, self.b, self.ws, self.wl, self.wm, self.inv, self.diag, self.u, self.v = refs
        self.half = 0.5 * factor
        self.circular = circular
        self.planes, self.rows, self.lanes = self.f.shape
        self.unroll = unroll

    def build(self):
        shape = (self.rows, self.lanes)
        sub = iota(shape, 0)
        half = self.half
        self.b[self.planes] = jnp.zeros(shape, F32)
        self.u[self.planes] = jnp.zeros(shape, F32)
        self.v[self.planes] = jnp.zeros(shape, F32)

        def step(m, carry):
            before, b = carry
            after = self.b[m + 1]
            wl = half * (b + roll(b, -1, 1))
            beside = roll(b, -1, 0)
            if not self.circular:
                beside = only(sub < self.rows - 1, beside)
            ws = half * (b + beside)
            wm = half * (b + after)
            below = roll(ws, 1, 0)
            if not self.circular:
                below = jnp.where(sub == 0, half * b, below)
            diag = self.a[m] + (wl + roll(wl, 1, 1) + ws + below + wm + before)
            inv = jnp.where(b > 0.0, 1.0 / diag, 0.0)
            self.ws[m] = ws if self.circular else only(sub < self.rows - 1, ws)
            self.wl[m] = wl
            self.wm[m] = wm
            self.diag[m] = diag
            self.inv[m] = inv
            return wm, after

        first = self.b[0]
        lax.fori_loop(0, self.planes, step, (half * first, first), unroll=self.unroll)

    def start(self, weight):
        def step(m, carry):
            self.u[m] = (weight * self.f[m]) * self.inv[m]
            return carry

        lax.fori_loop(0, self.planes, step, 0, unroll=self.unroll)

    def beside(self, m, u, after, flow):
        wl, ws, wm = self.wl[m], self.ws[m], self.wm[m]
        along = wl * roll(u, -1, 1) + roll(wl * u, 1, 1)
        across = ws * roll(u, -1, 0) + roll(ws * u, 1, 0)
        return self.f[m] + (along + across + (wm * after + flow)), wm * u

    def sweep(self, weight, src, dst):
        def step(m, carry):
            flow, u = carry
            after = src[m + 1]
            total, flow = self.beside(m, u, after, flow)
            dst[m] = (1.0 - weight) * u + (weight * self.inv[m]) * total
            return flow, after

        first = src[0]
        lax.fori_loop(0, self.planes, step, (jnp.zeros_like(first), first), unroll=self.unroll)

    def sweeps_down(self):
        self.start(WEIGHTS[0])
        self.sweep(WEIGHTS[1], self.u, self.v)
        self.sweep(WEIGHTS[2], self.v, self.u)

    def sweeps_up(self):
        self.sweep(WEIGHTS[0], self.u, self.v)
        self.sweep(WEIGHTS[1], self.v, self.u)
        self.sweep(WEIGHTS[2], self.u, self.v)

    def residual_pairs(self, src, dst, rows):
        def step(m, carry):
            flow, u = carry
            total = None
            for k in (2 * m, 2 * m + 1):
                after = src[k + 1]
                part, flow = self.beside(k, u, after, flow)
                part = (part - self.diag[k] * u)[:rows]
                total = part if total is None else total + part
                u = after
            dst[m] = total
            return flow, u

        first = src[0]
        lax.fori_loop(0, self.planes // 2, step, (jnp.zeros_like(first), first), unroll=max(self.unroll // 2, 1))

    def residual(self, src, dst, rows, lanes):
        def step(m, carry):
            flow, u = carry
            after = src[m + 1]
            part, flow = self.beside(m, u, after, flow)
            dst[m] = (part - self.diag[m] * u)[:rows, :lanes]
            return flow, after

        first = src[0]
        lax.fori_loop(0, self.planes, step, (jnp.zeros_like(first), first), unroll=self.unroll)


def sum_planes(src, dst, rows):
    def step(m, carry):
        dst[m] = src[2 * m][:rows] + src[2 * m + 1][:rows]
        return carry

    lax.fori_loop(0, dst.shape[0], step, 0, unroll=4)


def places():
    ix, iy = lax.axis_index("gx"), lax.axis_index("gy")
    nx, ny = lax.axis_size("gx"), lax.axis_size("gy")
    return ix, iy, ix % 2 == 0, iy % 2 == 0, ix < nx - 1, ix > 0, iy < ny - 1, iy > 0


def pack_kernel(f, a, b, ya, yb, xa, xb):
    ix, iy, even_x, even_y, *_ = places()
    lane, sub = iota((8, 128), 1), iota((8, 128), 0)

    def y_side(z, shift):
        return jnp.where(
            lane < YH,
            roll(f[z], shift, 1),
            jnp.where(lane < 2 * YH, roll(a[z], shift + YH, 1), roll(b[z], shift + 2 * YH, 1)),
        )

    def y_step(z, carry):
        low = jnp.where(lane < 64, y_side(z, 0), roll(y_side(z + 32, 0), 64, 1))
        high = jnp.where(lane < 64, y_side(z, YH), roll(y_side(z + 32, YH), 64, 1))
        ya[z] = either(even_y, high, low)
        yb[z] = either(even_y, low, high)
        return carry

    lax.fori_loop(0, 32, y_step, 0, unroll=2)

    def x_step(q, carry):
        extra_low = extra_high = jnp.zeros((8, 128), F32)
        for j in range(4):
            z = 4 * q + j
            fz, az, bz = f[z], a[z], b[z]
            low = jnp.where(sub < 3, fz, jnp.where(sub < 6, roll(az, 3, 0), roll(bz, 6, 0)))
            high = jnp.where(sub < 3, roll(fz, 3, 0), jnp.where(sub < 6, roll(az, 6, 0), roll(bz, 2, 0)))
            here = sub // 2 == j
            extra_low = jnp.where(here, roll(bz, 2 * j - 2, 0), extra_low)
            extra_high = jnp.where(here, roll(bz, 2 * j - 6, 0), extra_high)
            xa[z] = either(even_x, high, low)
            xb[z] = either(even_x, low, high)
        xa[64 + q] = either(even_x, extra_high, extra_low)
        xb[64 + q] = either(even_x, extra_low, extra_high)
        return carry

    lax.fori_loop(0, 16, x_step, 0)


def corner_kernel(ya, yb, ca, cb):
    ix, iy, even_x, even_y, *_ = places()
    sub = iota((8, 128), 0)

    def step(z, carry):
        right, left = either(even_y, ya[z], yb[z]), either(even_y, yb[z], ya[z])
        low = jnp.where(sub < 4, left, roll(right, 4, 0))
        high = jnp.where(sub < 4, roll(left, 4, 0), right)
        ca[z] = either(even_x, high, low)
        cb[z] = either(even_x, low, high)
        return carry

    lax.fori_loop(0, 32, step, 0, unroll=4)


def fine_down_kernel(
    f, a, b, xa, xb, ya, yb, ca, cb,
    pack, ra, rb, own_u, f_out, ws_out, wl_out, wm_out, inv_out, diag_out,
    fx, ax, bx, ws, wl, wm, inv, diag, u, v, pairs, wide, sems,
):
    ix, iy, even_x, even_y, has_right, has_left, has_above, has_below = places()
    lane, sub = iota((8, 128), 1), iota((8, 128), 0)

    def unpack(q, carry):
        for j in range(4):
            zz = 4 * q + j
            up = only(has_above, either(even_y, ya[zz], yb[zz]))
            down = only(has_below, either(even_y, yb[zz], ya[zz]))
            corner_r = only(has_right, either(even_x, ca[zz], cb[zz]))
            corner_l = only(has_left, either(even_x, cb[zz], ca[zz]))
            up_c = only(has_above, jnp.where(sub < 4, roll(corner_r, 4, 0), corner_l))
            down_c = only(has_below, jnp.where(sub < 4, corner_r, roll(corner_l, 4, 0)))
            for h in range(2):
                z, e = zz + 32 * h, 64 + q + 8 * h
                main_r = only(has_right, either(even_x, xa[z], xb[z]))
                main_l = only(has_left, either(even_x, xb[z], xa[z]))
                extra_r = only(has_right, either(even_x, xa[e], xb[e]))
                extra_l = only(has_left, either(even_x, xb[e], xa[e]))
                beside = (
                    jnp.where(sub < 3, main_r, only(sub >= 5, roll(main_l, 5, 0))),
                    jnp.where(sub < 3, roll(main_r, -3, 0), only(sub >= 5, roll(main_l, 2, 0))),
                    jnp.where(
                        sub < 2,
                        roll(main_r, 2, 0),
                        jnp.where(
                            sub < 4,
                            roll(extra_r, 2 - 2 * j, 0),
                            jnp.where(sub < 6, roll(main_l, 6, 0), roll(extra_l, 6 - 2 * j, 0)),
                        ),
                    ),
                )
                for n, (own, full) in enumerate(((f, fx), (a, ax), (b, bx))):
                    at = 64 * h + YH * n
                    full[z, 0:8, 0:128] = own[z]
                    full[z, 8:16, 0:128] = beside[n]
                    for rows, hi, lo in (((0, 8), up, down), ((8, 16), up_c, down_c)):
                        full[z, rows[0] : rows[1], 128:256] = jnp.where(
                            lane < YH, roll(hi, -at, 1), only(lane >= 128 - YH, roll(lo, 128 - YH - at, 1))
                        )
        return carry

    lax.fori_loop(0, 8, unpack, 0)
    level = Level((fx, ax, bx, ws, wl, wm, inv, diag, u, v), 1.0, True, 4)
    level.build()
    copies = [
        pltpu.make_async_copy(src, dst, sems.at[n])
        for n, (src, dst) in enumerate(
            ((fx, f_out), (ws, ws_out), (wl, wl_out), (wm, wm_out), (inv, inv_out), (diag, diag_out))
        )
    ]
    for copy in copies:
        copy.start()

    half = indicator(iota((256, 128), 0) // 2 == iota((256, 128), 1))

    def coarse():
        wide[...] = matmul(pairs[...].reshape(256, 256), half)
        return 0.125 * (wide[pl.ds(0, 128, stride=2), :] + wide[pl.ds(1, 128, stride=2), :])

    sum_planes(ax, pairs, 8)
    alpha = coarse()
    sum_planes(bx, pairs, 8)
    beta = coarse()
    level.sweeps_down()
    level.residual_pairs(u, pairs, 8)
    source = coarse()

    at = iota((128, 128), 1)
    pack[0:16] = jnp.where(at < 64, source, roll(alpha, 64, 1)).reshape(16, 8, 128)
    second = jnp.zeros((128, 128), F32)
    for end, part in (
        (112, roll(beta, -16, 1)),
        (104, roll(beta, 32, 1)),
        (96, roll(alpha, -32, 1)),
        (88, roll(alpha, 16, 1)),
        (80, roll(source, -48, 1)),
        (72, source),
        (64, beta),
    ):
        second = jnp.where(at < end, part, second)
    pack[16:32] = second.reshape(16, 8, 128)

    for z in range(32):
        own_u[z] = u[z, 0:8, :]
        own_u[z + 32] = u[z + 32, 0:8, :]
        one, two = u[z, 0:8, 0:128], u[z + 32, 0:8, 0:128]
        low = jnp.where(sub < 4, one, roll(two, 4, 0))
        high = jnp.where(sub < 4, roll(one, 4, 0), two)
        ra[z] = either(even_x, high, low)
        rb[z] = either(even_x, low, high)
    for t in range(2):
        low = high = jnp.zeros((8, 128), F32)
        for g in range(2):
            for k in range(16):
                edge = u[16 * (2 * t + g) + k, 0:8, 128:256]
                edge = roll(jnp.where(lane < 4, edge, roll(edge, 8, 1)), 8 * k, 1)
                here = (lane // 8 == k) & (sub // 4 == g)
                turned = roll(edge, 4, 0)
                low = jnp.where(here, turned if g else edge, low)
                high = jnp.where(here, edge if g else turned, high)
        ra[32 + t] = either(even_x, high, low)
        rb[32 + t] = either(even_x, low, high)
    for copy in copies:
        copy.wait()


def middle_down_kernel(
    pack, ga, gb, ra, rb,
    copies, sa, sb, f1, a1, b1, u1,
    b, ws, wl, wm, inv, diag, u, v, pairs, wide,
):
    ix, iy, even_x, even_y, has_right, has_left, has_above, has_below = places()
    lane, sub = iota((8, 128), 1), iota((8, 128), 0)

    def fields(one, two):
        def halo(right, left):
            return jnp.where(lane < 72, roll(two, right, 1), only(lane >= 120, roll(two, left, 1)))

        return (
            jnp.where(lane < 64, one, halo(0, 48)),
            jnp.where(lane < 64, roll(one, 64, 1), halo(-16, 32)),
            jnp.where(lane < 64, two, halo(-32, 16)),
        )

    def unpack(t, carry):
        own = fields(pack[t], pack[16 + t])
        right = fields(
            only(has_right, either(even_x, ga[t], gb[t])), only(has_right, either(even_x, ga[16 + t], gb[16 + t]))
        )
        left = fields(
            only(has_left, either(even_x, gb[t], ga[t])), only(has_left, either(even_x, gb[16 + t], ga[16 + t]))
        )
        for n, full in enumerate((f1, a1, b)):
            full[2 * t, 0:8] = jnp.where(sub < 4, own[n], roll(right[n], 4, 0))
            full[2 * t, 8:16] = only(sub >= 4, roll(left[n], 4, 0))
            full[2 * t + 1, 0:8] = jnp.where(sub < 4, roll(own[n], 4, 0), right[n])
            full[2 * t + 1, 8:16] = only(sub >= 4, left[n])
        return carry

    lax.fori_loop(0, 16, unpack, 0)
    level = Level((f1, a1, b, ws, wl, wm, inv, diag, u, v), 0.25, True, 4)
    level.build()
    level.sweeps_down()

    lanes_in, lanes_out = iota((128, 128), 0), iota((128, 128), 1)
    half = indicator((lanes_in // 2 == lanes_out) & (lanes_out < 32))

    def coarse():
        wide[...] = matmul(pairs[...].reshape(128, 128), half)
        rows = [wide[pl.ds(k, 16, stride=8), :] for k in range(4)]
        return 0.125 * (rows[0] + rows[1]), 0.125 * (rows[2] + rows[3])

    sum_planes(a1, pairs, 8)
    alpha = coarse()
    sum_planes(b, pairs, 8)
    beta = coarse()
    level.residual_pairs(u, pairs, 8)
    source = coarse()
    for k in range(2):
        block = source[k] + roll(alpha[k], 32, 1) + roll(beta[k], 64, 1)
        for d in range(8):
            copies[2 * d + k] = block

    def edges(z, carry):
        b1[z] = b[z]
        u1[z] = u[z]
        mine, far = u[z, 0:8], u[z, 8:16]
        turned = roll(mine, 4, 0)
        high = jnp.where(
            sub >= 4, turned, jnp.where(sub == 3, roll(far, 4, 0), roll(b[z, 8:16], 1, 0))
        )
        low = jnp.where(sub == 1, roll(b[z, 0:8], 5, 0), turned)
        sa[z] = either(even_x, high, low)
        sb[z] = either(even_x, low, high)
        return carry

    lax.fori_loop(0, 32, edges, 0, unroll=2)
    sa[32:66] = ra[...]
    sb[32:66] = rb[...]


def up_kernel(
    own, ya, yb, xa, xb, f1, a1, b1, u1, own_u,
    f0_in, ws0_in, wl0_in, wm0_in, inv0_in, diag0_in,
    field_out, residual_out,
    f0, ws0, wl0, wm0, inv0, diag0, u0, v0,
    bx1, ws1, wl1, wm1, inv1, diag1, ux1, v1,
    f2, a2, b2, ws2, wl2, wm2, inv2, diag2, u2, v2,
    f3, a3, b3, ws3, wl3, wm3, inv3, diag3, u3, v3,
    pairs, wide, spread, sems,
):
    ix, iy, even_x, even_y, has_right, has_left, has_above, has_below = places()
    lane, sub = iota((8, 128), 1), iota((8, 128), 0)
    copies = [
        pltpu.make_async_copy(src, dst, sems.at[n])
        for n, (src, dst) in enumerate(
            ((f0_in, f0), (ws0_in, ws0), (wl0_in, wl0), (wm0_in, wm0), (inv0_in, inv0), (diag0_in, diag0))
        )
    ]
    for copy in copies:
        copy.start()

    at = iota((16, 128), 1)
    for x in range(16):
        mine = own[x]
        up = only(has_above, either(even_y, ya[x], yb[x]))
        down = only(has_below, either(even_y, yb[x], ya[x]))
        for n, full in enumerate((f2, a2, b2)):
            full[x] = jnp.where(
                at < 32,
                roll(mine, -32 * n, 1),
                jnp.where(at < 64, roll(up, 32 - 32 * n, 1), only(at >= 96, roll(down, 96 - 32 * n, 1))),
            )
    level2 = Level((f2, a2, b2, ws2, wl2, wm2, inv2, diag2, u2, v2), 0.0625, False, 4)
    level2.build()
    level2.sweeps_down()

    lanes_in, lanes_out = iota((128, 128), 0), iota((128, 128), 1)
    half = indicator(half_wrapped(lanes_in, 96, 64) == lanes_out)
    twice = indicator(lanes_in == half_wrapped(lanes_out, 96, 64))

    def coarse():
        wide[0:128, :] = matmul(pairs[...].reshape(128, 128), half)
        halves = wide[pl.ds(0, 64, stride=2), :] + wide[pl.ds(1, 64, stride=2), :]
        return (0.125 * halves).reshape(8, 8, 128)

    sum_planes(a2, pairs, 16)
    a3[...] = coarse()
    sum_planes(b2, pairs, 16)
    b3[0:8] = coarse()
    level2.residual_pairs(u2, pairs, 16)
    f3[...] = coarse()
    level3 = Level((f3, a3, b3, ws3, wl3, wm3, inv3, diag3, u3, v3), 0.015625, False, 8)
    level3.build()
    level3.start(BOTTOM_WEIGHT)

    def two_sweeps(_, carry):
        level3.sweep(BOTTOM_WEIGHT, u3, v3)
        level3.sweep(BOTTOM_WEIGHT, v3, u3)
        return carry

    lax.fori_loop(0, (BOTTOM - 2) // 2, two_sweeps, 0)
    level3.sweep(BOTTOM_WEIGHT, u3, v3)

    fine = matmul(v3[0:8].reshape(64, 128), twice)
    wide[pl.ds(0, 64, stride=2), :] = fine
    wide[pl.ds(1, 64, stride=2), :] = fine
    for x in range(16):
        u2[x] = u2[x] + only(inv2[x] > 0.0, wide[16 * (x // 2) : 16 * (x // 2) + 16, :])
    level2.sweeps_up()

    def fill_1(z, carry):
        right = only(has_right, either(even_x, xa[z], xb[z]))
        left = only(has_left, either(even_x, xb[z], xa[z]))
        ux1[z, 0:8] = jnp.where(sub < 4, u1[z, 0:8], right)
        ux1[z, 8:16] = jnp.where(sub == 0, right, only(sub >= 3, left))
        bx1[z, 0:8] = b1[z, 0:8]
        bx1[z, 8:16] = jnp.where(
            sub == 0, roll(right, -1, 0), jnp.where(sub == 3, roll(left, 3, 0), b1[z, 8:16])
        )
        return carry

    lax.fori_loop(0, 32, fill_1, 0, unroll=2)
    level1 = Level((f1, a1, bx1, ws1, wl1, wm1, inv1, diag1, ux1, v1), 0.25, True, 4)
    level1.build()
    double = indicator(lanes_in == jnp.where(lanes_out < 96, lanes_out // 2, 64 + lanes_out // 2))
    for k in range(-3, 5):
        column = jnp.clip(2 * ix + k, 0, 15)
        fine = matmul(v2[column], double)
        for e in range(2):
            for x in range(2):
                spread[pl.ds(e * 16 + (2 * k + x) % 16, 16, stride=32), :] = fine

    def correct_1(z, carry):
        rows = spread[pl.ds(pl.multiple_of(16 * z, 16), 16), :]
        ux1[z] = ux1[z] + only(inv1[z] > 0.0, rows)
        return carry

    lax.fori_loop(0, 32, correct_1, 0, unroll=2)
    level1.sweeps_up()

    for z in range(32):
        parts = v1[z, 0:8], v1[z, 8:16]
        rows = jnp.where(sub < 6, parts[0], parts[1])
        spread[pl.ds(16 * z, 8, stride=2), :] = rows
        spread[pl.ds(16 * z + 1, 8, stride=2), :] = rows
    for copy in copies:
        copy.wait()
    for z in range(64):
        t, e = z % 32, z // 32
        right = only(has_right, either(even_x, xa[32 + t], xb[32 + t]))
        left = only(has_left, either(even_x, xb[32 + t], xa[32 + t]))
        u0[z, 0:8, :] = own_u[z]
        u0[z, 8:16, 0:128] = jnp.where(
            sub < 4, roll(right, 4, 0) if e else right, left if e else roll(left, 4, 0)
        )
        g, k = z // 16, z % 16
        t, e = 64 + g // 2, g % 2
        right = only(has_right, either(even_x, xa[t], xb[t]))
        left = only(has_left, either(even_x, xb[t], xa[t]))
        edge = jnp.where(sub < 4, roll(right, 4, 0) if e else right, left if e else roll(left, 4, 0))
        u0[z, 8:16, 128:256] = jnp.where(
            lane < 4, roll(edge, -8 * k, 1), only(lane >= 124, roll(edge, 120 - 8 * k, 1))
        )
    lanes_in, lanes_out = iota((128, 256), 0), iota((128, 256), 1)
    double = indicator(lanes_in == lanes_out // 2)

    def correct_0(z, carry):
        fine = matmul(spread[pl.ds(pl.multiple_of(64 * z, 64), 64), :], double)
        for k in range(4):
            rows = fine[16 * k : 16 * k + 16]
            for e in range(2):
                m = 8 * z + 2 * k + e
                u0[m] = u0[m] + only(inv0[m] > 0.0, rows)
        return carry

    lax.fori_loop(0, 8, correct_0, 0)
    level0 = Level((f0, None, u0, ws0, wl0, wm0, inv0, diag0, u0, v0), 1.0, True, 4)
    u0[64] = jnp.zeros((16, 256), F32)
    v0[64] = jnp.zeros((16, 256), F32)
    level0.sweeps_up()
    level0.residual(v0, residual_out, 8, 128)

    def out(z, carry):
        field_out[z] = v0[z, 0:8, 0:128]
        return carry

    lax.fori_loop(0, 64, out, 0, unroll=4)


def call(kernel, outs, scratch, any_in=0, any_out=0, n_in=0, sems=0):
    vmem = pl.BlockSpec(memory_space=pltpu.VMEM)
    anywhere = pl.BlockSpec(memory_space=pl.ANY)
    out_specs = [vmem] * (len(outs) - any_out) + [anywhere] * any_out
    scratch_shapes = [pltpu.VMEM(shape, F32) for shape in scratch]
    if sems:
        scratch_shapes.append(pltpu.SemaphoreType.DMA((sems,)))
    return pl.pallas_call(
        kernel,
        out_shape=[jax.ShapeDtypeStruct(shape, F32) for shape in outs],
        in_specs=[vmem] * (n_in - any_in) + [anywhere] * any_in,
        out_specs=out_specs,
        scratch_shapes=scratch_shapes,
        compiler_params=pltpu.CompilerParams(vmem_limit_bytes=48 * 1024 * 1024),
    )


def swaps(axis):
    size = lax.axis_size(axis)
    first = [(i, i ^ 1) for i in range(size)]
    second = [(i, i + 1 if i % 2 else i - 1) for i in range(size)]
    if axis == "gx":
        second = [(i, j % size) for i, j in second]
    else:
        second = [(i, j) for i, j in second if 0 <= j < size]
    return first, second


def swap(a, b, axis):
    first, second = swaps(axis)
    return lax.ppermute(a, axis, first), lax.ppermute(b, axis, second)


def body(right_side, alpha, beta):
    tiles = lambda n: (n, 8, 128)
    ya, yb, xa, xb = call(pack_kernel, [tiles(32), tiles(32), tiles(80), tiles(80)], [], n_in=3)(
        right_side, alpha, beta
    )
    ya, yb = swap(ya, yb, "gy")
    xa, xb = swap(xa, xb, "gx")
    ca, cb = call(corner_kernel, [tiles(32), tiles(32)], [], n_in=2)(ya, yb)
    ca, cb = swap(ca, cb, "gx")

    full, more = (64, 16, 256), (65, 16, 256)
    pack, ra, rb, own_u, *fine = call(
        fine_down_kernel,
        [tiles(32), tiles(34), tiles(34), (64, 8, 256)] + [full] * 6,
        [full, full, more, full, full, full, full, full, more, more, (32, 8, 256), (256, 128)],
        n_in=9,
        any_out=6,
        sems=6,
    )(right_side, alpha, beta, xa, xb, ya, yb, ca, cb)
    ga, gb = swap(pack, pack, "gx")

    full, more = (32, 16, 128), (33, 16, 128)
    copies, sa, sb, f1, a1, b1, u1 = call(
        middle_down_kernel,
        [(16, 16, 128), tiles(66), tiles(66)] + [full] * 4,
        [more, full, full, full, full, full, more, more, tiles(16), (128, 128)],
        n_in=5,
    )(pack, ga, gb, ra, rb)
    own = lax.all_to_all(copies, "gx", 0, 0, tiled=True)
    ya, yb = swap(own, own, "gy")
    xa, xb = swap(sa, sb, "gx")

    def level(planes, rows, lanes):
        one, two = (planes, rows, lanes), (planes + 1, rows, lanes)
        return [one, one, two, one, one, one, one, one, two, two]

    zero, first = level(64, 16, 256), level(32, 16, 128)
    return tuple(
        call(
            up_kernel,
            [tiles(64), tiles(64)],
            [zero[0]]
            + zero[3:]
            + first[2:]
            + level(16, 16, 128)
            + level(8, 8, 128)
            + [(8, 16, 128), (128, 128), (512, 128)],
            n_in=16,
            any_in=6,
            sems=6,
        )(own, ya, yb, xa, xb, f1, a1, b1, u1, own_u, *fine)
    )


def solution(mesh):
    return jax.shard_map(
        body,
        mesh=mesh,
        in_specs=(P(None, "gx", "gy"),) * 3,
        out_specs=(P(None, "gx", "gy"),) * 2,
        check_vma=False,
    )
```

```python
import functools

import jax
import jax.numpy as jnp
from jax import lax
from jax.experimental import pallas as pl
from jax.experimental.pallas import tpu as pltpu
from jax.sharding import PartitionSpec as P

F32 = jnp.float32
WEIGHTS = (0.6, 0.75, 0.9)
BOTTOM_WEIGHT = 0.8
BOTTOM = 12
YH = 20


def roll(x, shift, axis):
    shift %= x.shape[axis]
    return x if shift == 0 else pltpu.roll(x, shift, axis)


def iota(shape, axis):
    return lax.broadcasted_iota(jnp.int32, shape, axis)


def either(flag, a, b):
    return jnp.where(flag, a, b)


def only(flag, a):
    return jnp.where(flag, a, 0.0)


def matmul(a, chooser):
    total = None
    for _ in range(3):
        part = a.astype(jnp.bfloat16)
        product = jnp.dot(part, chooser, preferred_element_type=F32)
        total = product if total is None else total + product
        a = a - part.astype(F32)
    return total


def indicator(mask):
    return jnp.where(mask, 1.0, 0.0).astype(jnp.bfloat16)


def half_wrapped(i, low, high):
    return jnp.where(i < high, i // 2, jnp.where(i >= low, 64 + i // 2, -1))


class Level:
    def __init__(self, refs, factor, circular, unroll):
        self.f, self.a, self.b, self.ws, self.wl, self.wm, self.inv, self.diag, self.u, self.v = refs
        self.half = 0.5 * factor
        self.circular = circular
        self.planes, self.rows, self.lanes = self.f.shape
        self.unroll = unroll

    def build(self):
        shape = (self.rows, self.lanes)
        sub = iota(shape, 0)
        half = self.half
        self.u[self.planes] = jnp.zeros(shape, F32)
        self.v[self.planes] = jnp.zeros(shape, F32)

        def step(m, carry):
            before, b = carry
            after = self.b[m + 1]
            wl = half * (b + roll(b, -1, 1))
            beside = roll(b, -1, 0)
            if not self.circular:
                beside = only(sub < self.rows - 1, beside)
            ws = half * (b + beside)
            wm = half * (b + after)
            below = roll(ws, 1, 0)
            if not self.circular:
                below = jnp.where(sub == 0, half * b, below)
            diag = self.a[m] + (wl + roll(wl, 1, 1) + ws + below + wm + before)
            inv = jnp.where(b > 0.0, 1.0 / diag, 0.0)
            self.ws[m] = ws if self.circular else only(sub < self.rows - 1, ws)
            self.wl[m] = wl
            self.wm[m] = wm
            self.diag[m] = diag
            self.inv[m] = inv
            return wm, after

        first = self.b[0]
        lax.fori_loop(0, self.planes, step, (half * first, first), unroll=self.unroll)

    def start(self, weight):
        def step(m, carry):
            self.u[m] = (weight * self.f[m]) * self.inv[m]
            return carry

        lax.fori_loop(0, self.planes, step, 0, unroll=self.unroll)

    def beside(self, m, u, after, flow):
        wl, ws, wm = self.wl[m], self.ws[m], self.wm[m]
        along = wl * roll(u, -1, 1) + roll(wl * u, 1, 1)
        across = ws * roll(u, -1, 0) + roll(ws * u, 1, 0)
        return self.f[m] + (along + across + (wm * after + flow)), wm * u

    def sweep(self, weight, src, dst):
        def step(m, carry):
            flow, u = carry
            after = src[m + 1]
            total, flow = self.beside(m, u, after, flow)
            dst[m] = (1.0 - weight) * u + (weight * self.inv[m]) * total
            return flow, after

        first = src[0]
        lax.fori_loop(0, self.planes, step, (jnp.zeros_like(first), first), unroll=self.unroll)

    def sweeps_down(self):
        self.start(WEIGHTS[0])
        self.sweep(WEIGHTS[1], self.u, self.v)
        self.sweep(WEIGHTS[2], self.v, self.u)

    def sweeps_up(self):
        self.sweep(WEIGHTS[0], self.u, self.v)
        self.sweep(WEIGHTS[1], self.v, self.u)
        self.sweep(WEIGHTS[2], self.u, self.v)

    def residual_pairs(self, src, dst, rows):
        def step(m, carry):
            flow, u = carry
            total = None
            for k in (2 * m, 2 * m + 1):
                after = src[k + 1]
                part, flow = self.beside(k, u, after, flow)
                part = (part - self.diag[k] * u)[:rows]
                total = part if total is None else total + part
                u = after
            dst[m] = total
            return flow, u

        first = src[0]
        lax.fori_loop(0, self.planes // 2, step, (jnp.zeros_like(first), first), unroll=max(self.unroll // 2, 1))

    def residual(self, src, dst, rows, lanes):
        def step(m, carry):
            flow, u = carry
            after = src[m + 1]
            part, flow = self.beside(m, u, after, flow)
            dst[m] = (part - self.diag[m] * u)[:rows, :lanes]
            return flow, after

        first = src[0]
        lax.fori_loop(0, self.planes, step, (jnp.zeros_like(first), first), unroll=self.unroll)


def sum_planes(src, dst, rows):
    def step(m, carry):
        dst[m] = src[2 * m][:rows] + src[2 * m + 1][:rows]
        return carry

    lax.fori_loop(0, dst.shape[0], step, 0, unroll=8)


def places():
    ix, iy = lax.axis_index("gx"), lax.axis_index("gy")
    nx, ny = lax.axis_size("gx"), lax.axis_size("gy")
    return ix, iy, ix % 2 == 0, iy % 2 == 0, ix < nx - 1, ix > 0, iy < ny - 1, iy > 0


def pack_x_kernel(f, a, b, xa, xb):
    ix, iy, even_x, even_y, *_ = places()
    sub = iota((8, 128), 0)

    def x_step(q, carry):
        extra_low = extra_high = jnp.zeros((8, 128), F32)
        for j in range(4):
            z = 4 * q + j
            fz, az, bz = f[z], a[z], b[z]
            low = jnp.where(sub < 3, fz, jnp.where(sub < 6, roll(az, 3, 0), roll(bz, 6, 0)))
            high = jnp.where(sub < 3, roll(fz, 3, 0), jnp.where(sub < 6, roll(az, 6, 0), roll(bz, 2, 0)))
            here = sub // 2 == j
            extra_low = jnp.where(here, roll(bz, 2 * j - 2, 0), extra_low)
            extra_high = jnp.where(here, roll(bz, 2 * j - 6, 0), extra_high)
            xa[z] = either(even_x, high, low)
            xb[z] = either(even_x, low, high)
        xa[64 + q] = either(even_x, extra_high, extra_low)
        xb[64 + q] = either(even_x, extra_low, extra_high)
        return carry

    lax.fori_loop(0, 16, x_step, 0, unroll=4)


def pack_y_kernel(f_in, a_in, b_in, f, a, b, ya, yb, sems):
    ix, iy, even_x, even_y, *_ = places()
    lane = iota((8, 128), 1)
    copies = [
        pltpu.make_async_copy(src, dst, sems.at[n]) for n, (src, dst) in enumerate(((f_in, f), (a_in, a), (b_in, b)))
    ]
    for copy in copies:
        copy.start()
    for copy in copies:
        copy.wait()

    def y_side(z, shift):
        return jnp.where(
            lane < YH,
            roll(f[z], shift, 1),
            jnp.where(lane < 2 * YH, roll(a[z], shift + YH, 1), roll(b[z], shift + 2 * YH, 1)),
        )

    def y_step(z, carry):
        low = jnp.where(lane < 64, y_side(z, 0), roll(y_side(z + 32, 0), 64, 1))
        high = jnp.where(lane < 64, y_side(z, YH), roll(y_side(z + 32, YH), 64, 1))
        ya[z] = either(even_y, high, low)
        yb[z] = either(even_y, low, high)
        return carry

    lax.fori_loop(0, 32, y_step, 0, unroll=8)


def corner_kernel(ya, yb, ca, cb):
    ix, iy, even_x, even_y, *_ = places()
    sub = iota((8, 128), 0)

    def step(z, carry):
        right, left = either(even_y, ya[z], yb[z]), either(even_y, yb[z], ya[z])
        low = jnp.where(sub < 4, left, roll(right, 4, 0))
        high = jnp.where(sub < 4, roll(left, 4, 0), right)
        ca[z] = either(even_x, high, low)
        cb[z] = either(even_x, low, high)
        return carry

    lax.fori_loop(0, 32, step, 0, unroll=4)


class Rows:
    def __init__(self, top, bottom):
        self.top, self.bottom = top, bottom
        self.shape = (top.shape[0], 16, top.shape[2])

    def __getitem__(self, m):
        return jnp.concatenate([self.top[m], self.bottom[m]], 0)


def spread_columns(lane, high, low, at):
    return jnp.where(lane < YH, roll(high, -at, 1), only(lane >= 128 - YH, roll(low, 128 - YH - at, 1)))


def coarse_fine(pairs, wide):
    half = indicator(iota((256, 128), 0) // 2 == iota((256, 128), 1))
    wide[...] = matmul(pairs[...].reshape(256, 256), half)
    return 0.125 * (wide[pl.ds(0, 128, stride=2), :] + wide[pl.ds(1, 128, stride=2), :])


def own_rows_kernel(f, a, b, ya, yb, fx, ax, bx, alpha, beta, pairs, wide):
    ix, iy, even_x, even_y, has_right, has_left, has_above, has_below = places()
    lane = iota((8, 128), 1)

    def unpack(z, carry):
        up = only(has_above, either(even_y, ya[z], yb[z]))
        down = only(has_below, either(even_y, yb[z], ya[z]))
        for n, (own, full) in enumerate(((f, fx), (a, ax), (b, bx))):
            for h in range(2):
                full[z + 32 * h, :, 0:128] = own[z + 32 * h]
                full[z + 32 * h, :, 128:256] = spread_columns(lane, up, down, 64 * h + YH * n)
        return carry

    lax.fori_loop(0, 32, unpack, 0, unroll=8)
    bx[64] = jnp.zeros((8, 256), F32)
    sum_planes(ax, pairs, 8)
    alpha[...] = coarse_fine(pairs, wide)
    sum_planes(bx, pairs, 8)
    beta[...] = coarse_fine(pairs, wide)


def fine_down_kernel(
    f, a, b, alpha_in, beta_in, xa, xb, ca, cb,
    pack, ra, rb, own_u, fx, ws, wl, wm, inv, diag,
    ax, bx, u, v, pairs, wide,
):
    ix, iy, even_x, even_y, has_right, has_left, has_above, has_below = places()
    lane, sub = iota((8, 128), 1), iota((8, 128), 0)

    def unpack(q, carry):
        for j in range(4):
            zz = 4 * q + j
            corner_r = only(has_right, either(even_x, ca[zz], cb[zz]))
            corner_l = only(has_left, either(even_x, cb[zz], ca[zz]))
            up = only(has_above, jnp.where(sub < 4, roll(corner_r, 4, 0), corner_l))
            down = only(has_below, jnp.where(sub < 4, corner_r, roll(corner_l, 4, 0)))
            for h in range(2):
                z, e = zz + 32 * h, 64 + q + 8 * h
                main_r = only(has_right, either(even_x, xa[z], xb[z]))
                main_l = only(has_left, either(even_x, xb[z], xa[z]))
                extra_r = only(has_right, either(even_x, xa[e], xb[e]))
                extra_l = only(has_left, either(even_x, xb[e], xa[e]))
                beside = (
                    jnp.where(sub < 3, main_r, only(sub >= 5, roll(main_l, 5, 0))),
                    jnp.where(sub < 3, roll(main_r, -3, 0), only(sub >= 5, roll(main_l, 2, 0))),
                    jnp.where(
                        sub < 2,
                        roll(main_r, 2, 0),
                        jnp.where(
                            sub < 4,
                            roll(extra_r, 2 - 2 * j, 0),
                            jnp.where(sub < 6, roll(main_l, 6, 0), roll(extra_l, 6 - 2 * j, 0)),
                        ),
                    ),
                )
                for n, full in enumerate((fx, ax, bx)):
                    full[z, :, 0:128] = beside[n]
                    full[z, :, 128:256] = spread_columns(lane, up, down, 64 * h + YH * n)
        return carry

    lax.fori_loop(0, 8, unpack, 0, unroll=2)
    bx[64] = jnp.zeros((8, 256), F32)
    level = Level((Rows(f, fx), Rows(a, ax), Rows(b, bx), ws, wl, wm, inv, diag, u, v), 1.0, True, 16)
    level.build()
    level.sweeps_down()
    level.residual_pairs(u, pairs, 8)
    source = coarse_fine(pairs, wide)
    alpha, beta = alpha_in[...], beta_in[...]

    at = iota((128, 128), 1)
    pack[0:16] = jnp.where(at < 64, source, roll(alpha, 64, 1)).reshape(16, 8, 128)
    second = jnp.zeros((128, 128), F32)
    for end, part in (
        (112, roll(beta, -16, 1)),
        (104, roll(beta, 32, 1)),
        (96, roll(alpha, -32, 1)),
        (88, roll(alpha, 16, 1)),
        (80, roll(source, -48, 1)),
        (72, source),
        (64, beta),
    ):
        second = jnp.where(at < end, part, second)
    pack[16:32] = second.reshape(16, 8, 128)

    for z in range(32):
        own_u[z] = u[z, 0:8, :]
        own_u[z + 32] = u[z + 32, 0:8, :]
        one, two = u[z, 0:8, 0:128], u[z + 32, 0:8, 0:128]
        low = jnp.where(sub < 4, one, roll(two, 4, 0))
        high = jnp.where(sub < 4, roll(one, 4, 0), two)
        ra[z] = either(even_x, high, low)
        rb[z] = either(even_x, low, high)
    for t in range(2):
        low = high = jnp.zeros((8, 128), F32)
        for g in range(2):
            for k in range(16):
                edge = u[16 * (2 * t + g) + k, 0:8, 128:256]
                edge = roll(jnp.where(lane < 4, edge, roll(edge, 8, 1)), 8 * k, 1)
                here = (lane // 8 == k) & (sub // 4 == g)
                turned = roll(edge, 4, 0)
                low = jnp.where(here, turned if g else edge, low)
                high = jnp.where(here, edge if g else turned, high)
        ra[32 + t] = either(even_x, high, low)
        rb[32 + t] = either(even_x, low, high)


def middle_down_kernel(
    pack, ga, gb,
    copies, f1, a1, b, u,
    ws, wl, wm, inv, diag, v, pairs, wide,
):
    ix, iy, even_x, even_y, has_right, has_left, has_above, has_below = places()
    lane, sub = iota((8, 128), 1), iota((8, 128), 0)

    def fields(one, two):
        def halo(right, left):
            return jnp.where(lane < 72, roll(two, right, 1), only(lane >= 120, roll(two, left, 1)))

        return (
            jnp.where(lane < 64, one, halo(0, 48)),
            jnp.where(lane < 64, roll(one, 64, 1), halo(-16, 32)),
            jnp.where(lane < 64, two, halo(-32, 16)),
        )

    def unpack(t, carry):
        own = fields(pack[t], pack[16 + t])
        right = fields(
            only(has_right, either(even_x, ga[t], gb[t])), only(has_right, either(even_x, ga[16 + t], gb[16 + t]))
        )
        left = fields(
            only(has_left, either(even_x, gb[t], ga[t])), only(has_left, either(even_x, gb[16 + t], ga[16 + t]))
        )
        for n, full in enumerate((f1, a1, b)):
            full[2 * t, 0:8] = jnp.where(sub < 4, own[n], roll(right[n], 4, 0))
            full[2 * t, 8:16] = only(sub >= 4, roll(left[n], 4, 0))
            full[2 * t + 1, 0:8] = jnp.where(sub < 4, roll(own[n], 4, 0), right[n])
            full[2 * t + 1, 8:16] = only(sub >= 4, left[n])
        return carry

    lax.fori_loop(0, 16, unpack, 0, unroll=4)
    b[32] = jnp.zeros((16, 128), F32)
    level = Level((f1, a1, b, ws, wl, wm, inv, diag, u, v), 0.25, True, 16)
    level.build()
    level.sweeps_down()

    lanes_in, lanes_out = iota((128, 128), 0), iota((128, 128), 1)
    half = indicator((lanes_in // 2 == lanes_out) & (lanes_out < 32))

    def coarse():
        wide[...] = matmul(pairs[...].reshape(128, 128), half)
        rows = [wide[pl.ds(k, 16, stride=8), :] for k in range(4)]
        return 0.125 * (rows[0] + rows[1]), 0.125 * (rows[2] + rows[3])

    sum_planes(a1, pairs, 8)
    alpha = coarse()
    sum_planes(b, pairs, 8)
    beta = coarse()
    level.residual_pairs(u, pairs, 8)
    source = coarse()
    for k in range(2):
        block = source[k] + roll(alpha[k], 32, 1) + roll(beta[k], 64, 1)
        for d in range(8):
            copies[2 * d + k] = block


def edges_kernel(_, ra, rb, b, u, sa, sb):
    ix, iy, even_x, even_y, *_ = places()
    sub = iota((8, 128), 0)

    def edges(z, carry):
        mine, far = u[z, 0:8], u[z, 8:16]
        turned = roll(mine, 4, 0)
        high = jnp.where(
            sub >= 4, turned, jnp.where(sub == 3, roll(far, 4, 0), roll(b[z, 8:16], 1, 0))
        )
        low = jnp.where(sub == 1, roll(b[z, 0:8], 5, 0), turned)
        sa[z] = either(even_x, high, low)
        sb[z] = either(even_x, low, high)
        return carry

    lax.fori_loop(0, 32, edges, 0, unroll=8)
    sa[32:66] = ra[...]
    sb[32:66] = rb[...]


def bottom_kernel(
    own, ya, yb,
    out,
    f2, a2, b2, ws2, wl2, wm2, inv2, diag2, u2, v2,
    f3, a3, b3, ws3, wl3, wm3, inv3, diag3, u3, v3,
    pairs, wide,
):
    ix, iy, even_x, even_y, has_right, has_left, has_above, has_below = places()
    lane, sub = iota((8, 128), 1), iota((8, 128), 0)

    at = iota((16, 128), 1)
    for x in range(16):
        mine = own[x]
        up = only(has_above, either(even_y, ya[x], yb[x]))
        down = only(has_below, either(even_y, yb[x], ya[x]))
        for n, full in enumerate((f2, a2, b2)):
            full[x] = jnp.where(
                at < 32,
                roll(mine, -32 * n, 1),
                jnp.where(at < 64, roll(up, 32 - 32 * n, 1), only(at >= 96, roll(down, 96 - 32 * n, 1))),
            )
    b2[16] = jnp.zeros((16, 128), F32)
    b3[8] = jnp.zeros((8, 128), F32)
    level2 = Level((f2, a2, b2, ws2, wl2, wm2, inv2, diag2, u2, v2), 0.0625, False, 16)
    level2.build()
    level2.sweeps_down()

    lanes_in, lanes_out = iota((128, 128), 0), iota((128, 128), 1)
    half = indicator(half_wrapped(lanes_in, 96, 64) == lanes_out)
    twice = indicator(lanes_in == half_wrapped(lanes_out, 96, 64))

    def coarse():
        wide[0:128, :] = matmul(pairs[...].reshape(128, 128), half)
        halves = wide[pl.ds(0, 64, stride=2), :] + wide[pl.ds(1, 64, stride=2), :]
        return (0.125 * halves).reshape(8, 8, 128)

    sum_planes(a2, pairs, 16)
    a3[...] = coarse()
    sum_planes(b2, pairs, 16)
    b3[0:8] = coarse()
    level2.residual_pairs(u2, pairs, 16)
    f3[...] = coarse()
    level3 = Level((f3, a3, b3, ws3, wl3, wm3, inv3, diag3, u3, v3), 0.015625, False, 8)
    level3.build()
    level3.start(BOTTOM_WEIGHT)

    def two_sweeps(_, carry):
        level3.sweep(BOTTOM_WEIGHT, u3, v3)
        level3.sweep(BOTTOM_WEIGHT, v3, u3)
        return carry

    lax.fori_loop(0, (BOTTOM - 2) // 2, two_sweeps, 0)
    level3.sweep(BOTTOM_WEIGHT, u3, v3)

    fine = matmul(v3[0:8].reshape(64, 128), twice)
    wide[pl.ds(0, 64, stride=2), :] = fine
    wide[pl.ds(1, 64, stride=2), :] = fine
    for x in range(16):
        u2[x] = u2[x] + only(inv2[x] > 0.0, wide[16 * (x // 2) : 16 * (x // 2) + 16, :])
    level2.sweeps_up()
    out[...] = v2[0:16]


def ready_kernel(xa, xb, own_u, u0):
    ix, iy, even_x, even_y, has_right, has_left, has_above, has_below = places()
    lane, sub = iota((8, 128), 1), iota((8, 128), 0)

    for z in range(64):
        t, e = z % 32, z // 32
        right = only(has_right, either(even_x, xa[32 + t], xb[32 + t]))
        left = only(has_left, either(even_x, xb[32 + t], xa[32 + t]))
        u0[z, 0:8, :] = own_u[z]
        u0[z, 8:16, 0:128] = jnp.where(
            sub < 4, roll(right, 4, 0) if e else right, left if e else roll(left, 4, 0)
        )
        g, k = z // 16, z % 16
        t, e = 32 + g // 2, g % 2
        right = only(has_right, either(even_x, xa[32 + t], xb[32 + t]))
        left = only(has_left, either(even_x, xb[32 + t], xa[32 + t]))
        edge = jnp.where(sub < 4, roll(right, 4, 0) if e else right, left if e else roll(left, 4, 0))
        u0[z, 8:16, 128:256] = jnp.where(
            lane < 4, roll(edge, -8 * k, 1), only(lane >= 124, roll(edge, 120 - 8 * k, 1))
        )
    u0[64] = jnp.zeros((16, 256), F32)


def up_kernel(
    v2, xa, xb, f1, a1, b1, u1, u0_in, f0, f0x, ws0, wl0, wm0, inv0, diag0,
    field_out, residual_out,
    u0, v0, bx1, ws1, wl1, wm1, inv1, diag1, ux1, v1, spread,
):
    ix, iy, even_x, even_y, has_right, has_left, has_above, has_below = places()
    sub = iota((8, 128), 0)
    lanes_in, lanes_out = iota((128, 128), 0), iota((128, 128), 1)

    def fill_1(z, carry):
        right = only(has_right, either(even_x, xa[z], xb[z]))
        left = only(has_left, either(even_x, xb[z], xa[z]))
        ux1[z, 0:8] = jnp.where(sub < 4, u1[z, 0:8], right)
        ux1[z, 8:16] = jnp.where(sub == 0, right, only(sub >= 3, left))
        bx1[z, 0:8] = b1[z, 0:8]
        bx1[z, 8:16] = jnp.where(
            sub == 0, roll(right, -1, 0), jnp.where(sub == 3, roll(left, 3, 0), b1[z, 8:16])
        )
        return carry

    lax.fori_loop(0, 32, fill_1, 0, unroll=8)
    bx1[32] = jnp.zeros((16, 128), F32)
    level1 = Level((f1, a1, bx1, ws1, wl1, wm1, inv1, diag1, ux1, v1), 0.25, True, 16)
    level1.build()
    double = indicator(lanes_in == jnp.where(lanes_out < 96, lanes_out // 2, 64 + lanes_out // 2))
    columns = [v2[jnp.clip(2 * ix + k, 0, 15)] for k in range(-3, 5)]
    fine = matmul(jnp.concatenate(columns, 0), double)
    for k in range(8):
        for e in range(2):
            for x in range(2):
                spread[pl.ds(e * 16 + (2 * (k - 3) + x) % 16, 16, stride=32), :] = fine[16 * k : 16 * k + 16]

    def correct_1(z, carry):
        rows = spread[pl.ds(pl.multiple_of(16 * z, 16), 16), :]
        ux1[z] = ux1[z] + only(inv1[z] > 0.0, rows)
        return carry

    lax.fori_loop(0, 32, correct_1, 0, unroll=8)
    level1.sweeps_up()

    for z in range(32):
        parts = v1[z, 0:8], v1[z, 8:16]
        rows = jnp.where(sub < 6, parts[0], parts[1])
        spread[pl.ds(16 * z, 8, stride=2), :] = rows
        spread[pl.ds(16 * z + 1, 8, stride=2), :] = rows
    lanes_in, lanes_out = iota((128, 256), 0), iota((128, 256), 1)
    double = indicator(lanes_in == lanes_out // 2)

    def correct_0(z, carry):
        fine = matmul(spread[pl.ds(pl.multiple_of(64 * z, 64), 64), :], double)
        for k in range(4):
            rows = fine[16 * k : 16 * k + 16]
            for e in range(2):
                m = 8 * z + 2 * k + e
                u0[m] = u0_in[m] + only(inv0[m] > 0.0, rows)
        return carry

    lax.fori_loop(0, 8, correct_0, 0, unroll=4)
    level0 = Level((Rows(f0, f0x), None, u0, ws0, wl0, wm0, inv0, diag0, u0, v0), 1.0, True, 16)
    u0[64] = jnp.zeros((16, 256), F32)
    v0[64] = jnp.zeros((16, 256), F32)
    level0.sweeps_up()
    level0.residual(v0, residual_out, 8, 128)

    def out(z, carry):
        field_out[z] = v0[z, 0:8, 0:128]
        return carry

    lax.fori_loop(0, 64, out, 0, unroll=4)


def call(kernel, outs, scratch, n_in, any_in=0, sems=0, cost=1):
    vmem = pl.BlockSpec(memory_space=pltpu.VMEM)
    anywhere = pl.BlockSpec(memory_space=pltpu.HBM)
    scratch_shapes = [pltpu.VMEM(shape, F32) for shape in scratch]
    if sems:
        scratch_shapes.append(pltpu.SemaphoreType.DMA((sems,)))
    need = sum(4 * p * r * n for p, r, n in ((1,) * (3 - len(shape)) + shape for shape in scratch))
    return pl.pallas_call(
        kernel,
        out_shape=[jax.ShapeDtypeStruct(shape, F32) for shape in outs],
        in_specs=[vmem] * (n_in - any_in) + [anywhere] * any_in,
        out_specs=[vmem] * len(outs),
        scratch_shapes=scratch_shapes,
        cost_estimate=pl.CostEstimate(flops=0, bytes_accessed=cost * 3_000_000, transcendentals=0),
        compiler_params=pltpu.CompilerParams(vmem_limit_bytes=need + 4 * 1024 * 1024),
    )


def swaps(axis):
    size = lax.axis_size(axis)
    first = [(i, i ^ 1) for i in range(size)]
    second = [(i, i + 1 if i % 2 else i - 1) for i in range(size)]
    if axis == "gx":
        second = [(i, j % size) for i, j in second]
    else:
        second = [(i, j) for i, j in second if 0 <= j < size]
    return first, second


def swap(a, b, axis):
    first, second = swaps(axis)
    return lax.ppermute(a, axis, first), lax.ppermute(b, axis, second)


def body(right_side, alpha, beta):
    def tiles(n):
        return (n, 8, 128)

    f, a, b, ya, yb = call(pack_y_kernel, [tiles(64)] * 3 + [tiles(32)] * 2, [], 3, any_in=3, sems=3)(
        right_side, alpha, beta
    )
    ya, yb = swap(ya, yb, "gy")
    xa, xb = call(pack_x_kernel, [tiles(80), tiles(80)], [], 3, cost=50)(f, a, b)
    xa, xb = swap(xa, xb, "gx")
    ca, cb = call(corner_kernel, [tiles(32), tiles(32)], [], 2)(ya, yb)
    ca, cb = swap(ca, cb, "gx")
    top, top_more = (64, 8, 256), (65, 8, 256)
    f, a, b, alpha, beta = call(
        own_rows_kernel, [top, top, top_more, (128, 128), (128, 128)], [(32, 8, 256), (256, 128)], 5, cost=50
    )(f, a, b, ya, yb)

    full, more = (64, 16, 256), (65, 16, 256)
    pack, ra, rb, own_u, *fine = call(
        fine_down_kernel,
        [tiles(32), tiles(34), tiles(34), top, top] + [full] * 5,
        [top, top_more, more, more, (32, 8, 256), (256, 128)],
        9,
    )(f, a, b, alpha, beta, xa, xb, ca, cb)
    ga, gb = swap(pack, pack, "gx")

    full, more = (32, 16, 128), (33, 16, 128)
    copies, f1, a1, b1, u1 = call(
        middle_down_kernel,
        [(16, 16, 128), full, full, more, more],
        [full, full, full, full, full, more, tiles(16), (128, 128)],
        3,
    )(pack, ga, gb)
    own = lax.all_to_all(copies, "gx", 0, 0, tiled=True)
    ya, yb = swap(own, own, "gy")
    sa, sb = call(edges_kernel, [tiles(66), tiles(66)], [], 5, cost=50)(own, ra, rb, b1, u1)
    sa, sb = swap(sa, sb, "gx")
    (u0,) = call(ready_kernel, [(65, 16, 256)], [], 3)(sa, sb, own_u)

    def level(planes, rows, lanes):
        one, two = (planes, rows, lanes), (planes + 1, rows, lanes)
        return [one, one, two, one, one, one, one, one, two, two]

    (u2,) = call(
        bottom_kernel,
        [(16, 16, 128)],
        level(16, 16, 128) + level(8, 8, 128) + [(8, 16, 128), (128, 128)],
        3,
        cost=50,
    )(own, ya, yb)
    return tuple(
        call(
            up_kernel,
            [tiles(64), tiles(64)],
            [(65, 16, 256)] * 2 + level(32, 16, 128)[2:] + [(512, 128)],
            15,
        )(u2, sa, sb, f1, a1, b1, u1, u0, f, *fine)
    )


def solution(mesh):
    return jax.shard_map(
        body,
        mesh=mesh,
        in_specs=(P(None, "gx", "gy"),) * 3,
        out_specs=(P(None, "gx", "gy"),) * 2,
        check_vma=False,
    )
```

```python
import functools

import jax
import jax.numpy as jnp
from jax import lax
from jax.experimental import pallas as pl
from jax.experimental.pallas import tpu as pltpu
from jax.sharding import PartitionSpec as P

F32 = jnp.float32
WEIGHTS = (0.6, 0.75, 0.9)
BOTTOM_WEIGHT = 0.8
BOTTOM = 12
YH = 20


def roll(x, shift, axis):
    shift %= x.shape[axis]
    return x if shift == 0 else pltpu.roll(x, shift, axis)


def iota(shape, axis):
    return lax.broadcasted_iota(jnp.int32, shape, axis)


def either(flag, a, b):
    return jnp.where(flag, a, b)


def only(flag, a):
    return jnp.where(flag, a, 0.0)


def matmul(a, chooser):
    total = None
    for _ in range(3):
        part = a.astype(jnp.bfloat16)
        product = jnp.dot(part, chooser, preferred_element_type=F32)
        total = product if total is None else total + product
        a = a - part.astype(F32)
    return total


def indicator(mask):
    return jnp.where(mask, 1.0, 0.0).astype(jnp.bfloat16)


def half_wrapped(i, low, high):
    return jnp.where(i < high, i // 2, jnp.where(i >= low, 64 + i // 2, -1))


class Level:
    def __init__(self, refs, factor, circular, unroll):
        self.f, self.a, self.b, self.ws, self.wl, self.wm, self.inv, self.diag, self.u, self.v = refs
        self.half = 0.5 * factor
        self.circular = circular
        self.planes, self.rows, self.lanes = self.f.shape
        self.unroll = unroll

    def build(self):
        shape = (self.rows, self.lanes)
        sub = iota(shape, 0)
        half = self.half
        self.u[self.planes] = jnp.zeros(shape, F32)
        self.v[self.planes] = jnp.zeros(shape, F32)

        def step(m, carry):
            before, b = carry
            after = self.b[m + 1]
            wl = half * (b + roll(b, -1, 1))
            beside = roll(b, -1, 0)
            if not self.circular:
                beside = only(sub < self.rows - 1, beside)
            ws = half * (b + beside)
            wm = half * (b + after)
            below = roll(ws, 1, 0)
            if not self.circular:
                below = jnp.where(sub == 0, half * b, below)
            diag = self.a[m] + (wl + roll(wl, 1, 1) + ws + below + wm + before)
            inv = jnp.where(b > 0.0, 1.0 / diag, 0.0)
            self.ws[m] = ws if self.circular else only(sub < self.rows - 1, ws)
            self.wl[m] = wl
            self.wm[m] = wm
            self.diag[m] = diag
            self.inv[m] = inv
            return wm, after

        first = self.b[0]
        lax.fori_loop(0, self.planes, step, (half * first, first), unroll=self.unroll)

    def start(self, weight):
        def step(m, carry):
            self.u[m] = (weight * self.f[m]) * self.inv[m]
            return carry

        lax.fori_loop(0, self.planes, step, 0, unroll=self.unroll)

    def beside(self, m, u, after, flow):
        wl, ws, wm = self.wl[m], self.ws[m], self.wm[m]
        along = wl * roll(u, -1, 1) + roll(wl * u, 1, 1)
        across = ws * roll(u, -1, 0) + roll(ws * u, 1, 0)
        return self.f[m] + (along + across + (wm * after + flow)), wm * u

    def sweep(self, weight, src, dst):
        def step(m, carry):
            flow, u = carry
            after = src[m + 1]
            total, flow = self.beside(m, u, after, flow)
            dst[m] = (1.0 - weight) * u + (weight * self.inv[m]) * total
            return flow, after

        first = src[0]
        lax.fori_loop(0, self.planes, step, (jnp.zeros_like(first), first), unroll=self.unroll)

    def sweeps_down(self):
        self.start(WEIGHTS[0])
        self.sweep(WEIGHTS[1], self.u, self.v)
        self.sweep(WEIGHTS[2], self.v, self.u)

    def sweeps_up(self):
        self.sweep(WEIGHTS[0], self.u, self.v)
        self.sweep(WEIGHTS[1], self.v, self.u)
        self.sweep(WEIGHTS[2], self.u, self.v)

    def residual_pairs(self, src, dst, rows):
        def step(m, carry):
            flow, u = carry
            total = None
            for k in (2 * m, 2 * m + 1):
                after = src[k + 1]
                part, flow = self.beside(k, u, after, flow)
                part = (part - self.diag[k] * u)[:rows]
                total = part if total is None else total + part
                u = after
            dst[m] = total
            return flow, u

        first = src[0]
        lax.fori_loop(0, self.planes // 2, step, (jnp.zeros_like(first), first), unroll=max(self.unroll // 2, 1))

    def residual(self, src, dst, rows, lanes):
        def step(m, carry):
            flow, u = carry
            after = src[m + 1]
            part, flow = self.beside(m, u, after, flow)
            dst[m] = (part - self.diag[m] * u)[:rows, :lanes]
            return flow, after

        first = src[0]
        lax.fori_loop(0, self.planes, step, (jnp.zeros_like(first), first), unroll=self.unroll)


def sum_planes(src, dst, rows):
    def step(m, carry):
        dst[m] = src[2 * m][:rows] + src[2 * m + 1][:rows]
        return carry

    lax.fori_loop(0, dst.shape[0], step, 0, unroll=8)


def places():
    ix, iy = lax.axis_index("gx"), lax.axis_index("gy")
    nx, ny = lax.axis_size("gx"), lax.axis_size("gy")
    return ix, iy, ix % 2 == 0, iy % 2 == 0, ix < nx - 1, ix > 0, iy < ny - 1, iy > 0


def pack_kernel(field, *refs):
    own, *refs = refs
    before, (xa, xb, ya, yb) = refs[:-4], refs[-4:]
    ix, iy, even_x, even_y, *_ = places()
    lane, sub = iota((8, 128), 1), iota((8, 128), 0)

    def y_step(z, carry):
        parts = []
        for shift in (0, YH):
            first = roll(own[z], shift + YH * field, 1)
            second = roll(own[z + 32], shift + YH * field + 64, 1)
            parts.append(jnp.where(lane < 64, first, second))
        low, high = parts
        here = (lane % 64 >= YH * field) & (lane % 64 < YH * (field + 1))
        for out, value, old in ((ya, either(even_y, high, low), 2), (yb, either(even_y, low, high), 3)):
            out[z] = jnp.where(here, value, before[old][z]) if before else only(here, value)
        return carry

    lax.fori_loop(0, 32, y_step, 0, unroll=8)

    def x_step(q, carry):
        extra_low = extra_high = jnp.zeros((8, 128), F32)
        for j in range(4):
            z = 4 * q + j
            value = own[z]
            low, high = roll(value, 3 * field, 0), roll(value, (3, 6, 2)[field], 0)
            for out, chosen, old in ((xa, either(even_x, high, low), 0), (xb, either(even_x, low, high), 1)):
                out[z] = jnp.where(sub < 3 * field, before[old][z], chosen) if before else chosen
            if field == 2:
                here = sub // 2 == j
                extra_low = jnp.where(here, roll(value, 2 * j - 2, 0), extra_low)
                extra_high = jnp.where(here, roll(value, 2 * j - 6, 0), extra_high)
        if field == 2:
            xa[64 + q] = either(even_x, extra_high, extra_low)
            xb[64 + q] = either(even_x, extra_low, extra_high)
        return carry

    lax.fori_loop(0, 16, x_step, 0, unroll=4)


def corner_kernel(ya, yb, ca, cb):
    ix, iy, even_x, even_y, *_ = places()
    sub = iota((8, 128), 0)

    def step(z, carry):
        right, left = either(even_y, ya[z], yb[z]), either(even_y, yb[z], ya[z])
        low = jnp.where(sub < 4, left, roll(right, 4, 0))
        high = jnp.where(sub < 4, roll(left, 4, 0), right)
        ca[z] = either(even_x, high, low)
        cb[z] = either(even_x, low, high)
        return carry

    lax.fori_loop(0, 32, step, 0, unroll=4)


class Rows:
    def __init__(self, top, bottom):
        self.top, self.bottom = top, bottom
        self.shape = (top.shape[0], 16, top.shape[2])

    def __getitem__(self, m):
        return jnp.concatenate([self.top[m], self.bottom[m]], 0)


def spread_columns(lane, high, low, at):
    return jnp.where(lane < YH, roll(high, -at, 1), only(lane >= 128 - YH, roll(low, 128 - YH - at, 1)))


def coarse_fine(pairs, wide):
    half = indicator(iota((256, 128), 0) // 2 == iota((256, 128), 1))
    wide[...] = matmul(pairs[...].reshape(256, 256), half)
    return 0.125 * (wide[pl.ds(0, 128, stride=2), :] + wide[pl.ds(1, 128, stride=2), :])


def own_rows_kernel(f, a, b, ya, yb, fx, ax, bx, ab, pairs, wide):
    ix, iy, even_x, even_y, has_right, has_left, has_above, has_below = places()
    lane = iota((8, 128), 1)

    def unpack(z, carry):
        up = only(has_above, either(even_y, ya[z], yb[z]))
        down = only(has_below, either(even_y, yb[z], ya[z]))
        for n, (own, full) in enumerate(((f, fx), (a, ax), (b, bx))):
            for h in range(2):
                full[z + 32 * h, :, 0:128] = own[z + 32 * h]
                full[z + 32 * h, :, 128:256] = spread_columns(lane, up, down, 64 * h + YH * n)
        return carry

    lax.fori_loop(0, 32, unpack, 0, unroll=8)
    bx[64] = jnp.zeros((8, 256), F32)
    sum_planes(ax, pairs, 8)
    ab[0:16] = coarse_fine(pairs, wide).reshape(16, 8, 128)
    sum_planes(bx, pairs, 8)
    ab[16:32] = coarse_fine(pairs, wide).reshape(16, 8, 128)


def fine_down_kernel(
    f, a, b, xa, xb, ca, cb,
    source, u, fx, ws, wl, wm, inv, diag,
    ax, bx, v, pairs, wide,
):
    ix, iy, even_x, even_y, has_right, has_left, has_above, has_below = places()
    lane, sub = iota((8, 128), 1), iota((8, 128), 0)

    def unpack(q, carry):
        for j in range(4):
            zz = 4 * q + j
            corner_r = only(has_right, either(even_x, ca[zz], cb[zz]))
            corner_l = only(has_left, either(even_x, cb[zz], ca[zz]))
            up = only(has_above, jnp.where(sub < 4, roll(corner_r, 4, 0), corner_l))
            down = only(has_below, jnp.where(sub < 4, corner_r, roll(corner_l, 4, 0)))
            for h in range(2):
                z, e = zz + 32 * h, 64 + q + 8 * h
                main_r = only(has_right, either(even_x, xa[z], xb[z]))
                main_l = only(has_left, either(even_x, xb[z], xa[z]))
                extra_r = only(has_right, either(even_x, xa[e], xb[e]))
                extra_l = only(has_left, either(even_x, xb[e], xa[e]))
                beside = (
                    jnp.where(sub < 3, main_r, only(sub >= 5, roll(main_l, 5, 0))),
                    jnp.where(sub < 3, roll(main_r, -3, 0), only(sub >= 5, roll(main_l, 2, 0))),
                    jnp.where(
                        sub < 2,
                        roll(main_r, 2, 0),
                        jnp.where(
                            sub < 4,
                            roll(extra_r, 2 - 2 * j, 0),
                            jnp.where(sub < 6, roll(main_l, 6, 0), roll(extra_l, 6 - 2 * j, 0)),
                        ),
                    ),
                )
                for n, full in enumerate((fx, ax, bx)):
                    full[z, :, 0:128] = beside[n]
                    full[z, :, 128:256] = spread_columns(lane, up, down, 64 * h + YH * n)
        return carry

    lax.fori_loop(0, 8, unpack, 0, unroll=2)
    bx[64] = jnp.zeros((8, 256), F32)
    level = Level((Rows(f, fx), Rows(a, ax), Rows(b, bx), ws, wl, wm, inv, diag, u, v), 1.0, True, 16)
    level.build()
    level.sweeps_down()
    level.residual_pairs(u, pairs, 8)
    source[...] = coarse_fine(pairs, wide).reshape(16, 8, 128)


def u_edges_kernel(u, ra, rb):
    ix, iy, even_x, even_y, *_ = places()
    lane, sub = iota((8, 128), 1), iota((8, 128), 0)

    def main(z, carry):
        one, two = u[z, 0:8, 0:128], u[z + 32, 0:8, 0:128]
        low = jnp.where(sub < 4, one, roll(two, 4, 0))
        high = jnp.where(sub < 4, roll(one, 4, 0), two)
        ra[z] = either(even_x, high, low)
        rb[z] = either(even_x, low, high)
        return carry

    lax.fori_loop(0, 32, main, 0, unroll=8)
    for t in range(2):
        low = high = jnp.zeros((8, 128), F32)
        for g in range(2):
            for k in range(16):
                edge = u[16 * (2 * t + g) + k, 0:8, 128:256]
                edge = roll(jnp.where(lane < 4, edge, roll(edge, 8, 1)), 8 * k, 1)
                here = (lane // 8 == k) & (sub // 4 == g)
                turned = roll(edge, 4, 0)
                low = jnp.where(here, turned if g else edge, low)
                high = jnp.where(here, edge if g else turned, high)
        ra[32 + t] = either(even_x, high, low)
        rb[32 + t] = either(even_x, low, high)


def middle_down_kernel(
    source_in, ga, gb, ab, aba, abb,
    copies, f1, a1, b, u,
    ws, wl, wm, inv, diag, v, pairs, wide,
):
    ix, iy, even_x, even_y, has_right, has_left, has_above, has_below = places()
    sub = iota((8, 128), 0)

    def unpack(t, carry):
        for own, one, two, at, full in (
            (source_in, ga, gb, 0, f1),
            (ab, aba, abb, 0, a1),
            (ab, aba, abb, 16, b),
        ):
            mine = own[at + t]
            right = only(has_right, either(even_x, one[at + t], two[at + t]))
            left = only(has_left, either(even_x, two[at + t], one[at + t]))
            full[2 * t, 0:8] = jnp.where(sub < 4, mine, roll(right, 4, 0))
            full[2 * t, 8:16] = only(sub >= 4, roll(left, 4, 0))
            full[2 * t + 1, 0:8] = jnp.where(sub < 4, roll(mine, 4, 0), right)
            full[2 * t + 1, 8:16] = only(sub >= 4, left)
        return carry

    lax.fori_loop(0, 16, unpack, 0, unroll=4)
    b[32] = jnp.zeros((16, 128), F32)
    level = Level((f1, a1, b, ws, wl, wm, inv, diag, u, v), 0.25, True, 16)
    level.build()
    level.sweeps_down()

    lanes_in, lanes_out = iota((128, 128), 0), iota((128, 128), 1)
    half = indicator((lanes_in // 2 == lanes_out) & (lanes_out < 32))

    def coarse():
        wide[...] = matmul(pairs[...].reshape(128, 128), half)
        rows = [wide[pl.ds(k, 16, stride=8), :] for k in range(4)]
        return 0.125 * (rows[0] + rows[1]), 0.125 * (rows[2] + rows[3])

    sum_planes(a1, pairs, 8)
    alpha = coarse()
    sum_planes(b, pairs, 8)
    beta = coarse()
    level.residual_pairs(u, pairs, 8)
    source = coarse()
    for k in range(2):
        block = source[k] + roll(alpha[k], 32, 1) + roll(beta[k], 64, 1)
        for d in range(8):
            copies[2 * d + k] = block


def edges_kernel(_, b, u, sa, sb):
    ix, iy, even_x, even_y, *_ = places()
    sub = iota((8, 128), 0)

    def edges(z, carry):
        mine, far = u[z, 0:8], u[z, 8:16]
        turned = roll(mine, 4, 0)
        high = jnp.where(
            sub >= 4, turned, jnp.where(sub == 3, roll(far, 4, 0), roll(b[z, 8:16], 1, 0))
        )
        low = jnp.where(sub == 1, roll(b[z, 0:8], 5, 0), turned)
        sa[z] = either(even_x, high, low)
        sb[z] = either(even_x, low, high)
        return carry

    lax.fori_loop(0, 32, edges, 0, unroll=8)


def bottom_kernel(
    own, ya, yb,
    out,
    f2, a2, b2, ws2, wl2, wm2, inv2, diag2, u2, v2,
    f3, a3, b3, ws3, wl3, wm3, inv3, diag3, u3, v3,
    pairs, wide,
):
    ix, iy, even_x, even_y, has_right, has_left, has_above, has_below = places()
    lane, sub = iota((8, 128), 1), iota((8, 128), 0)

    at = iota((16, 128), 1)
    for x in range(16):
        mine = own[x]
        up = only(has_above, either(even_y, ya[x], yb[x]))
        down = only(has_below, either(even_y, yb[x], ya[x]))
        for n, full in enumerate((f2, a2, b2)):
            full[x] = jnp.where(
                at < 32,
                roll(mine, -32 * n, 1),
                jnp.where(at < 64, roll(up, 32 - 32 * n, 1), only(at >= 96, roll(down, 96 - 32 * n, 1))),
            )
    b2[16] = jnp.zeros((16, 128), F32)
    b3[8] = jnp.zeros((8, 128), F32)
    level2 = Level((f2, a2, b2, ws2, wl2, wm2, inv2, diag2, u2, v2), 0.0625, False, 16)
    level2.build()
    level2.sweeps_down()

    lanes_in, lanes_out = iota((128, 128), 0), iota((128, 128), 1)
    half = indicator(half_wrapped(lanes_in, 96, 64) == lanes_out)
    twice = indicator(lanes_in == half_wrapped(lanes_out, 96, 64))

    def coarse():
        wide[0:128, :] = matmul(pairs[...].reshape(128, 128), half)
        halves = wide[pl.ds(0, 64, stride=2), :] + wide[pl.ds(1, 64, stride=2), :]
        return (0.125 * halves).reshape(8, 8, 128)

    sum_planes(a2, pairs, 16)
    a3[...] = coarse()
    sum_planes(b2, pairs, 16)
    b3[0:8] = coarse()
    level2.residual_pairs(u2, pairs, 16)
    f3[...] = coarse()
    level3 = Level((f3, a3, b3, ws3, wl3, wm3, inv3, diag3, u3, v3), 0.015625, False, 8)
    level3.build()
    level3.start(BOTTOM_WEIGHT)

    def two_sweeps(_, carry):
        level3.sweep(BOTTOM_WEIGHT, u3, v3)
        level3.sweep(BOTTOM_WEIGHT, v3, u3)
        return carry

    lax.fori_loop(0, (BOTTOM - 2) // 2, two_sweeps, 0)
    level3.sweep(BOTTOM_WEIGHT, u3, v3)

    fine = matmul(v3[0:8].reshape(64, 128), twice)
    wide[pl.ds(0, 64, stride=2), :] = fine
    wide[pl.ds(1, 64, stride=2), :] = fine
    for x in range(16):
        u2[x] = u2[x] + only(inv2[x] > 0.0, wide[16 * (x // 2) : 16 * (x // 2) + 16, :])
    level2.sweeps_up()
    out[...] = v2[0:16]


def ready_kernel(copies_in, xa, xb, own_u, copies, u0):
    ix, iy, even_x, even_y, has_right, has_left, has_above, has_below = places()
    lane, sub = iota((8, 128), 1), iota((8, 128), 0)

    for z in range(64):
        t, e = z % 32, z // 32
        right = only(has_right, either(even_x, xa[t], xb[t]))
        left = only(has_left, either(even_x, xb[t], xa[t]))
        u0[z, 0:8, :] = own_u[z, 0:8, :]
        u0[z, 8:16, 0:128] = jnp.where(
            sub < 4, roll(right, 4, 0) if e else right, left if e else roll(left, 4, 0)
        )
        g, k = z // 16, z % 16
        t, e = 32 + g // 2, g % 2
        right = only(has_right, either(even_x, xa[t], xb[t]))
        left = only(has_left, either(even_x, xb[t], xa[t]))
        edge = jnp.where(sub < 4, roll(right, 4, 0) if e else right, left if e else roll(left, 4, 0))
        u0[z, 8:16, 128:256] = jnp.where(
            lane < 4, roll(edge, -8 * k, 1), only(lane >= 124, roll(edge, 120 - 8 * k, 1))
        )
    u0[64] = jnp.zeros((16, 256), F32)
    copies[...] = copies_in[...]


def up_kernel(
    v2, xa, xb, f1, a1, b1, u1, u0_in, f0, f0x, ws0, wl0, wm0, inv0, diag0,
    field_out, residual_out,
    u0, v0, bx1, ws1, wl1, wm1, inv1, diag1, ux1, v1, spread,
):
    ix, iy, even_x, even_y, has_right, has_left, has_above, has_below = places()
    sub = iota((8, 128), 0)
    lanes_in, lanes_out = iota((128, 128), 0), iota((128, 128), 1)

    def fill_1(z, carry):
        right = only(has_right, either(even_x, xa[z], xb[z]))
        left = only(has_left, either(even_x, xb[z], xa[z]))
        ux1[z, 0:8] = jnp.where(sub < 4, u1[z, 0:8], right)
        ux1[z, 8:16] = jnp.where(sub == 0, right, only(sub >= 3, left))
        bx1[z, 0:8] = b1[z, 0:8]
        bx1[z, 8:16] = jnp.where(
            sub == 0, roll(right, -1, 0), jnp.where(sub == 3, roll(left, 3, 0), b1[z, 8:16])
        )
        return carry

    lax.fori_loop(0, 32, fill_1, 0, unroll=8)
    bx1[32] = jnp.zeros((16, 128), F32)
    level1 = Level((f1, a1, bx1, ws1, wl1, wm1, inv1, diag1, ux1, v1), 0.25, True, 16)
    level1.build()
    double = indicator(lanes_in == jnp.where(lanes_out < 96, lanes_out // 2, 64 + lanes_out // 2))
    columns = [v2[jnp.clip(2 * ix + k, 0, 15)] for k in range(-3, 5)]
    fine = matmul(jnp.concatenate(columns, 0), double)
    for k in range(8):
        for e in range(2):
            for x in range(2):
                spread[pl.ds(e * 16 + (2 * (k - 3) + x) % 16, 16, stride=32), :] = fine[16 * k : 16 * k + 16]

    def correct_1(z, carry):
        rows = spread[pl.ds(pl.multiple_of(16 * z, 16), 16), :]
        ux1[z] = ux1[z] + only(inv1[z] > 0.0, rows)
        return carry

    lax.fori_loop(0, 32, correct_1, 0, unroll=8)
    level1.sweeps_up()

    for z in range(32):
        parts = v1[z, 0:8], v1[z, 8:16]
        rows = jnp.where(sub < 6, parts[0], parts[1])
        spread[pl.ds(16 * z, 8, stride=2), :] = rows
        spread[pl.ds(16 * z + 1, 8, stride=2), :] = rows
    lanes_in, lanes_out = iota((128, 256), 0), iota((128, 256), 1)
    double = indicator(lanes_in == lanes_out // 2)

    def correct_0(z, carry):
        fine = matmul(spread[pl.ds(pl.multiple_of(64 * z, 64), 64), :], double)
        for k in range(4):
            rows = fine[16 * k : 16 * k + 16]
            for e in range(2):
                m = 8 * z + 2 * k + e
                u0[m] = u0_in[m] + only(inv0[m] > 0.0, rows)
        return carry

    lax.fori_loop(0, 8, correct_0, 0, unroll=4)
    level0 = Level((Rows(f0, f0x), None, u0, ws0, wl0, wm0, inv0, diag0, u0, v0), 1.0, True, 16)
    u0[64] = jnp.zeros((16, 256), F32)
    v0[64] = jnp.zeros((16, 256), F32)
    level0.sweeps_up()
    level0.residual(v0, residual_out, 8, 128)

    def out(z, carry):
        field_out[z] = v0[z, 0:8, 0:128]
        return carry

    lax.fori_loop(0, 64, out, 0, unroll=4)


def call(kernel, outs, scratch, n_in, cost=1):
    vmem = pl.BlockSpec(memory_space=pltpu.VMEM)
    need = sum(4 * p * r * n for p, r, n in ((1,) * (3 - len(shape)) + shape for shape in scratch))
    return pl.pallas_call(
        kernel,
        out_shape=[jax.ShapeDtypeStruct(shape, F32) for shape in outs],
        in_specs=[vmem] * n_in,
        out_specs=[vmem] * len(outs),
        scratch_shapes=[pltpu.VMEM(shape, F32) for shape in scratch],
        cost_estimate=pl.CostEstimate(
            flops=cost * 1_000_000_000, bytes_accessed=cost * 3_000_000, transcendentals=0
        ),
        compiler_params=pltpu.CompilerParams(vmem_limit_bytes=need + 4 * 1024 * 1024),
    )


def swaps(axis):
    size = lax.axis_size(axis)
    first = [(i, i ^ 1) for i in range(size)]
    second = [(i, i + 1 if i % 2 else i - 1) for i in range(size)]
    second = [(i, j % size) for i, j in second]
    return first, second


def swap(a, b, axis):
    first, second = swaps(axis)
    return lax.ppermute(a, axis, first), lax.ppermute(b, axis, second)


def body(right_side, alpha, beta):
    def tiles(n):
        return (n, 8, 128)

    f, a, b = right_side, alpha, beta
    sizes = [tiles(64), tiles(64), tiles(32), tiles(32)]
    packs = call(functools.partial(pack_kernel, 0), sizes, [], 1)(f)
    packs = call(functools.partial(pack_kernel, 1), sizes, [], 5)(a, *packs)
    sizes = [tiles(80), tiles(80), tiles(32), tiles(32)]
    xa, xb, ya, yb = call(functools.partial(pack_kernel, 2), sizes, [], 5)(b, *packs)
    xa, xb = swap(xa, xb, "gx")
    ya, yb = swap(ya, yb, "gy")
    ca, cb = call(corner_kernel, [tiles(32), tiles(32)], [], 2)(ya, yb)
    ca, cb = swap(ca, cb, "gx")
    top, top_more = (64, 8, 256), (65, 8, 256)
    f, a, b, ab = call(
        own_rows_kernel, [top, top, top_more, tiles(32)], [(32, 8, 256), (256, 128)], 5, cost=3
    )(f, a, b, ya, yb)
    aba, abb = swap(ab, ab, "gx")

    full, more = (64, 16, 256), (65, 16, 256)
    source, u, *fine = call(
        fine_down_kernel,
        [tiles(16), more, top] + [full] * 5,
        [top, top_more, more, (32, 8, 256), (256, 128)],
        7,
        cost=50,
    )(f, a, b, xa, xb, ca, cb)
    ga, gb = swap(source, source, "gx")
    ra, rb = call(u_edges_kernel, [tiles(34), tiles(34)], [], 1, cost=50)(u)
    ra, rb = swap(ra, rb, "gx")

    full, more = (32, 16, 128), (33, 16, 128)
    copies, f1, a1, b1, u1 = call(
        middle_down_kernel,
        [(16, 16, 128), full, full, more, more],
        [full, full, full, full, full, more, tiles(16), (128, 128)],
        6,
        cost=50,
    )(source, ga, gb, ab, aba, abb)
    copies, u0 = call(ready_kernel, [(16, 16, 128), (65, 16, 256)], [], 4)(copies, ra, rb, u)
    own = lax.all_to_all(copies, "gx", 0, 0, tiled=True)
    ya, yb = swap(own, own, "gy")
    sa, sb = call(edges_kernel, [tiles(32), tiles(32)], [], 3, cost=50)(own, b1, u1)
    sa, sb = swap(sa, sb, "gx")

    def level(planes, rows, lanes):
        one, two = (planes, rows, lanes), (planes + 1, rows, lanes)
        return [one, one, two, one, one, one, one, one, two, two]

    (u2,) = call(
        bottom_kernel,
        [(16, 16, 128)],
        level(16, 16, 128) + level(8, 8, 128) + [(8, 16, 128), (128, 128)],
        3,
        cost=50,
    )(own, ya, yb)
    return tuple(
        call(
            up_kernel,
            [tiles(64), tiles(64)],
            [(65, 16, 256)] * 2 + level(32, 16, 128)[2:] + [(512, 128)],
            15,
        )(u2, sa, sb, f1, a1, b1, u1, u0, f, *fine)
    )


def solution(mesh):
    return jax.shard_map(
        body,
        mesh=mesh,
        in_specs=(P(None, "gx", "gy"),) * 3,
        out_specs=(P(None, "gx", "gy"),) * 2,
        check_vma=False,
    )
```

```python
import functools

import jax
import jax.numpy as jnp
from jax import lax
from jax.experimental import pallas as pl
from jax.experimental.pallas import tpu as pltpu
from jax.sharding import PartitionSpec as P

F32 = jnp.float32
WEIGHTS = (0.6, 0.75, 0.9)
BOTTOM_WEIGHT = 0.8
BOTTOM = 12
YH = 20


def roll(x, shift, axis):
    shift %= x.shape[axis]
    return x if shift == 0 else pltpu.roll(x, shift, axis)


def iota(shape, axis):
    return lax.broadcasted_iota(jnp.int32, shape, axis)


def either(flag, a, b):
    return jnp.where(flag, a, b)


def only(flag, a):
    return jnp.where(flag, a, 0.0)


def matmul(a, chooser):
    total = None
    for _ in range(3):
        part = a.astype(jnp.bfloat16)
        product = jnp.dot(part, chooser, preferred_element_type=F32)
        total = product if total is None else total + product
        a = a - part.astype(F32)
    return total


def indicator(mask):
    return jnp.where(mask, 1.0, 0.0).astype(jnp.bfloat16)


def half_wrapped(i, low, high):
    return jnp.where(i < high, i // 2, jnp.where(i >= low, 64 + i // 2, -1))


class Level:
    def __init__(self, refs, factor, circular, unroll):
        self.f, self.a, self.b, self.ws, self.wl, self.wm, self.inv, self.diag, self.u, self.v = refs
        self.half = 0.5 * factor
        self.circular = circular
        self.planes, self.rows, self.lanes = self.f.shape
        self.unroll = unroll

    def build(self, weight=None):
        shape = (self.rows, self.lanes)
        sub = iota(shape, 0)
        half = self.half
        self.u[self.planes] = jnp.zeros(shape, F32)
        self.v[self.planes] = jnp.zeros(shape, F32)

        def step(m, carry):
            before, b = carry
            after = self.b[m + 1]
            wl = half * (b + roll(b, -1, 1))
            beside = roll(b, -1, 0)
            if not self.circular:
                beside = only(sub < self.rows - 1, beside)
            ws = half * (b + beside)
            wm = half * (b + after)
            below = roll(ws, 1, 0)
            if not self.circular:
                below = jnp.where(sub == 0, half * b, below)
            diag = self.a[m] + (wl + roll(wl, 1, 1) + ws + below + wm + before)
            inv = jnp.where(b > 0.0, 1.0 / diag, 0.0)
            self.ws[m] = ws if self.circular else only(sub < self.rows - 1, ws)
            self.wl[m] = wl
            self.wm[m] = wm
            self.diag[m] = diag
            self.inv[m] = inv
            if weight is not None:
                self.u[m] = (weight * self.f[m]) * inv
            return wm, after

        first = self.b[0]
        lax.fori_loop(0, self.planes, step, (half * first, first), unroll=self.unroll)

    def beside(self, m, u, after, flow):
        wl, ws, wm = self.wl[m], self.ws[m], self.wm[m]
        along = wl * roll(u, -1, 1) + roll(wl * u, 1, 1)
        across = ws * roll(u, -1, 0) + roll(ws * u, 1, 0)
        return self.f[m] + (along + across + (wm * after + flow)), wm * u

    def sweep(self, weight, src, dst):
        def step(m, carry):
            flow, u = carry
            after = src[m + 1]
            total, flow = self.beside(m, u, after, flow)
            dst[m] = (1.0 - weight) * u + (weight * self.inv[m]) * total
            return flow, after

        first = src[0]
        lax.fori_loop(0, self.planes, step, (jnp.zeros_like(first), first), unroll=self.unroll)

    def sweeps_down(self):
        self.sweep(WEIGHTS[1], self.u, self.v)
        self.sweep(WEIGHTS[2], self.v, self.u)

    def sweeps_up(self):
        self.sweep(WEIGHTS[0], self.u, self.v)
        self.sweep(WEIGHTS[1], self.v, self.u)
        self.sweep(WEIGHTS[2], self.u, self.v)

    def residual_pairs(self, src, dst, rows):
        def step(m, carry):
            flow, u = carry
            total = None
            for k in (2 * m, 2 * m + 1):
                after = src[k + 1]
                part, flow = self.beside(k, u, after, flow)
                part = (part - self.diag[k] * u)[:rows]
                total = part if total is None else total + part
                u = after
            dst[m] = total
            return flow, u

        first = src[0]
        lax.fori_loop(0, self.planes // 2, step, (jnp.zeros_like(first), first), unroll=max(self.unroll // 2, 1))

    def residual(self, src, dst, rows, lanes):
        def step(m, carry):
            flow, u = carry
            after = src[m + 1]
            part, flow = self.beside(m, u, after, flow)
            dst[m] = (part - self.diag[m] * u)[:rows, :lanes]
            return flow, after

        first = src[0]
        lax.fori_loop(0, self.planes, step, (jnp.zeros_like(first), first), unroll=self.unroll)


def sum_planes(src, dst, rows):
    def step(m, carry):
        dst[m] = src[2 * m][:rows] + src[2 * m + 1][:rows]
        return carry

    lax.fori_loop(0, dst.shape[0], step, 0, unroll=8)


def places():
    ix, iy = lax.axis_index("gx"), lax.axis_index("gy")
    nx, ny = lax.axis_size("gx"), lax.axis_size("gy")
    return ix, iy, ix % 2 == 0, iy % 2 == 0, ix < nx - 1, ix > 0, iy < ny - 1, iy > 0


def pieces(plane):
    for tile in range(3):
        first = 3 * plane - 8 * tile
        if -3 < first < 8:
            yield tile, first, (max(first, 0) - first, min(first + 3, 8) - first)


def pack_three(read, low_row, high_row, write):
    sub = iota((8, 128), 0)
    low = [jnp.zeros((8, 128), F32)] * 3
    high = [jnp.zeros((8, 128), F32)] * 3
    for plane in range(8):
        rows = read(plane)
        for tile, first, _ in pieces(plane):
            here = (sub >= first) & (sub < first + 3)
            low[tile] = jnp.where(here, roll(rows, first - low_row, 0), low[tile])
            high[tile] = jnp.where(here, roll(rows, first - high_row, 0), high[tile])
    for tile in range(3):
        write(tile, low[tile], high[tile])


def unpack_three(plane, into, tile_of, row):
    sub = iota((8, 128), 0)
    for tile, first, (low, high) in pieces(plane):
        here = (sub >= row + low) & (sub < row + high)
        into = jnp.where(here, roll(tile_of(tile), row - first, 0), into)
    return into


def pack_kernel(field, *refs):
    own, *refs = refs
    before, (xa, xb, ya, yb) = refs[:-4], refs[-4:]
    ix, iy, even_x, even_y, *_ = places()
    lane, sub = iota((8, 128), 1), iota((8, 128), 0)

    def y_step(z, carry):
        parts = []
        for shift in (0, YH):
            first = roll(own[z], shift + YH * field, 1)
            second = roll(own[z + 32], shift + YH * field + 64, 1)
            parts.append(jnp.where(lane < 64, first, second))
        low, high = parts
        here = (lane % 64 >= YH * field) & (lane % 64 < YH * (field + 1))
        for out, value, old in ((ya, either(even_y, high, low), 2), (yb, either(even_y, low, high), 3)):
            out[z] = jnp.where(here, value, before[old][z]) if before else only(here, value)
        return carry

    lax.fori_loop(0, 32, y_step, 0, unroll=8)

    def x_step(q, carry):
        extra_low = extra_high = jnp.zeros((8, 128), F32)
        for j in range(4):
            z = 4 * q + j
            value = own[z]
            low, high = roll(value, 3 * field, 0), roll(value, (3, 6, 2)[field], 0)
            for out, chosen, old in ((xa, either(even_x, high, low), 0), (xb, either(even_x, low, high), 1)):
                out[z] = jnp.where(sub < 3 * field, before[old][z], chosen) if before else chosen
            if field == 2:
                here = sub // 2 == j
                extra_low = jnp.where(here, roll(value, 2 * j - 2, 0), extra_low)
                extra_high = jnp.where(here, roll(value, 2 * j - 6, 0), extra_high)
        if field == 2:
            xa[64 + q] = either(even_x, extra_high, extra_low)
            xb[64 + q] = either(even_x, extra_low, extra_high)
        return carry

    lax.fori_loop(0, 16, x_step, 0, unroll=4)


def corner_kernel(ya, yb, ca, cb):
    ix, iy, even_x, even_y, *_ = places()
    sub = iota((8, 128), 0)

    def step(z, carry):
        right, left = either(even_y, ya[z], yb[z]), either(even_y, yb[z], ya[z])
        low = jnp.where(sub < 4, left, roll(right, 4, 0))
        high = jnp.where(sub < 4, roll(left, 4, 0), right)
        ca[z] = either(even_x, high, low)
        cb[z] = either(even_x, low, high)
        return carry

    lax.fori_loop(0, 32, step, 0, unroll=4)


class Rows:
    def __init__(self, top, bottom):
        self.top, self.bottom = top, bottom
        self.shape = (top.shape[0], 16, top.shape[2])

    def __getitem__(self, m):
        return jnp.concatenate([self.top[m], self.bottom[m]], 0)


def spread_columns(lane, high, low, at):
    return jnp.where(lane < YH, roll(high, -at, 1), only(lane >= 128 - YH, roll(low, 128 - YH - at, 1)))


def coarse_fine(pairs, wide):
    half = indicator(iota((256, 128), 0) // 2 == iota((256, 128), 1))
    wide[...] = matmul(pairs[...].reshape(256, 256), half)
    return 0.125 * (wide[pl.ds(0, 128, stride=2), :] + wide[pl.ds(1, 128, stride=2), :])


def own_rows_kernel(f, a, b, ya, yb, fx, ax, bx, ab, packed, pairs, wide):
    ix, iy, even_x, even_y, has_right, has_left, has_above, has_below = places()
    lane = iota((8, 128), 1)

    def unpack(z, carry):
        up = only(has_above, either(even_y, ya[z], yb[z]))
        down = only(has_below, either(even_y, yb[z], ya[z]))
        for n, (own, full) in enumerate(((f, fx), (a, ax), (b, bx))):
            for h in range(2):
                full[z + 32 * h, :, 0:128] = own[z + 32 * h]
                full[z + 32 * h, :, 128:256] = spread_columns(lane, up, down, 64 * h + YH * n)
        return carry

    lax.fori_loop(0, 32, unpack, 0, unroll=8)
    bx[64] = jnp.zeros((8, 256), F32)
    sum_planes(ax, pairs, 8)
    ab[0:16] = coarse_fine(pairs, wide).reshape(16, 8, 128)
    sum_planes(bx, pairs, 8)
    ab[16:32] = coarse_fine(pairs, wide).reshape(16, 8, 128)
    for t in range(16):
        packed[t] = jnp.where(lane < 64, ab[t], roll(ab[16 + t], 64, 1))
    for t in range(4):
        packed[16 + t] = halo_lanes([ab[t + 4 * q + 16 * n] for q in range(4) for n in range(2)])


def halo_lanes(parts):
    lane = iota((8, 128), 1)
    packed = jnp.zeros((8, 128), F32)
    for n, part in enumerate(parts):
        pair = jnp.where(lane < 16 * n + 8, roll(part, 16 * n - 64, 1), roll(part, 16 * n + 8 - 120, 1))
        packed = jnp.where(lane // 16 == n, pair, packed)
    return packed


def with_halo_lanes(own, packed, n):
    lane = iota((8, 128), 1)
    right, left = roll(packed, 64 - 16 * n, 1), roll(packed, 112 - 16 * n, 1)
    return jnp.where(lane < 64, own, jnp.where(lane < 72, right, only(lane >= 120, left)))


def fine_down_kernel(
    f, a, b, xa, xb, ca, cb,
    source, packed, u, fx, ws, wl, wm, inv, diag,
    ax, bx, v, pairs, wide,
):
    ix, iy, even_x, even_y, has_right, has_left, has_above, has_below = places()
    lane, sub = iota((8, 128), 1), iota((8, 128), 0)

    def unpack(q, carry):
        for j in range(4):
            zz = 4 * q + j
            corner_r = only(has_right, either(even_x, ca[zz], cb[zz]))
            corner_l = only(has_left, either(even_x, cb[zz], ca[zz]))
            up = only(has_above, jnp.where(sub < 4, roll(corner_r, 4, 0), corner_l))
            down = only(has_below, jnp.where(sub < 4, corner_r, roll(corner_l, 4, 0)))
            for h in range(2):
                z, e = zz + 32 * h, 64 + q + 8 * h
                main_r = only(has_right, either(even_x, xa[z], xb[z]))
                main_l = only(has_left, either(even_x, xb[z], xa[z]))
                extra_r = only(has_right, either(even_x, xa[e], xb[e]))
                extra_l = only(has_left, either(even_x, xb[e], xa[e]))
                beside = (
                    jnp.where(sub < 3, main_r, only(sub >= 5, roll(main_l, 5, 0))),
                    jnp.where(sub < 3, roll(main_r, -3, 0), only(sub >= 5, roll(main_l, 2, 0))),
                    jnp.where(
                        sub < 2,
                        roll(main_r, 2, 0),
                        jnp.where(
                            sub < 4,
                            roll(extra_r, 2 - 2 * j, 0),
                            jnp.where(sub < 6, roll(main_l, 6, 0), roll(extra_l, 6 - 2 * j, 0)),
                        ),
                    ),
                )
                for n, full in enumerate((fx, ax, bx)):
                    full[z, :, 0:128] = beside[n]
                    full[z, :, 128:256] = spread_columns(lane, up, down, 64 * h + YH * n)
        return carry

    lax.fori_loop(0, 8, unpack, 0, unroll=2)
    bx[64] = jnp.zeros((8, 256), F32)
    level = Level((Rows(f, fx), Rows(a, ax), Rows(b, bx), ws, wl, wm, inv, diag, u, v), 1.0, True, 16)
    level.build(WEIGHTS[0])
    level.sweeps_down()
    level.residual_pairs(u, pairs, 8)
    source[...] = coarse_fine(pairs, wide).reshape(16, 8, 128)
    for t in range(8):
        packed[t] = jnp.where(lane < 64, source[t], roll(source[t + 8], 64, 1))
    for t in range(2):
        packed[8 + t] = halo_lanes([source[t + 2 * q] for q in range(8)])


def u_edges_kernel(u, ra, rb):
    ix, iy, even_x, even_y, *_ = places()
    lane, sub = iota((8, 128), 1), iota((8, 128), 0)

    def put(at, low, high):
        ra[at] = either(even_x, high, low)
        rb[at] = either(even_x, low, high)

    def main(g, carry):
        pack_three(
            lambda z: u[8 * g + z, 0:8, 0:128], 1, 4, lambda tile, low, high: put(3 * g + tile, low, high)
        )
        return carry

    lax.fori_loop(0, 8, main, 0, unroll=2)
    for t in range(2):
        low = high = jnp.zeros((8, 128), F32)
        for g in range(2):
            for k in range(16):
                edge = u[16 * (2 * t + g) + k, 0:8, 128:256]
                edge = roll(jnp.where(lane < 4, edge, roll(edge, 8, 1)), 8 * k, 1)
                here = (lane // 8 == k) & (sub // 4 == g)
                turned = roll(edge, 4, 0)
                low = jnp.where(here, turned if g else edge, low)
                high = jnp.where(here, edge if g else turned, high)
        put(24 + t, low, high)


def middle_down_kernel(
    source_in, ga, gb, ab, aba, abb, _a, _b,
    copies, f1, a1, b, u,
    ws, wl, wm, inv, diag, v, pairs, wide,
):
    ix, iy, even_x, even_y, has_right, has_left, has_above, has_below = places()
    sub = iota((8, 128), 0)

    def right(one, two, at):
        return only(has_right, either(even_x, one[at], two[at]))

    def left(one, two, at):
        return only(has_left, either(even_x, two[at], one[at]))

    for t in range(16):
        sides = []
        for side in (right, left):
            f = side(ga, gb, t % 8)
            f = with_halo_lanes(roll(f, 64, 1) if t >= 8 else f, side(ga, gb, 8 + t % 2), t // 2)
            both, halo = side(aba, abb, t), side(aba, abb, 16 + t % 4)
            sides.append(
                (f, with_halo_lanes(both, halo, t // 4 * 2), with_halo_lanes(roll(both, 64, 1), halo, t // 4 * 2 + 1))
            )
        for n, (own, full) in enumerate(((source_in[t], f1), (ab[t], a1), (ab[16 + t], b))):
            high, low = sides[0][n], sides[1][n]
            full[2 * t, 0:8] = jnp.where(sub < 4, own, roll(high, 4, 0))
            full[2 * t, 8:16] = only(sub >= 4, roll(low, 4, 0))
            full[2 * t + 1, 0:8] = jnp.where(sub < 4, roll(own, 4, 0), high)
            full[2 * t + 1, 8:16] = only(sub >= 4, low)

    b[32] = jnp.zeros((16, 128), F32)
    level = Level((f1, a1, b, ws, wl, wm, inv, diag, u, v), 0.25, True, 16)
    level.build(WEIGHTS[0])
    level.sweeps_down()

    lanes_in, lanes_out = iota((128, 128), 0), iota((128, 128), 1)
    half = indicator((lanes_in // 2 == lanes_out) & (lanes_out < 32))

    def coarse():
        wide[...] = matmul(pairs[...].reshape(128, 128), half)
        rows = [wide[pl.ds(k, 16, stride=8), :] for k in range(4)]
        return 0.125 * (rows[0] + rows[1]), 0.125 * (rows[2] + rows[3])

    sum_planes(a1, pairs, 8)
    alpha = coarse()
    sum_planes(b, pairs, 8)
    beta = coarse()
    level.residual_pairs(u, pairs, 8)
    source = coarse()
    blocks = []
    for k in range(2):
        blocks.append(source[k] + roll(alpha[k], 32, 1) + roll(beta[k], 64, 1))
    parts = [blocks[0][:8], blocks[0][8:], blocks[1][:8]]
    last = blocks[1][8:]
    lane = iota((8, 128), 1)
    for n, part in enumerate(parts):
        part = jnp.where(lane < 96, part, roll(last, 96 - 32 * n, 1))
        for d in range(8):
            copies[3 * d + n] = part


def edges_kernel(_, ra, rb, b, u, sa, sb):
    ix, iy, even_x, even_y, *_ = places()
    lane, sub = iota((8, 128), 1), iota((8, 128), 0)
    sa[0:26] = ra[...]
    sb[0:26] = rb[...]
    high, low = [], []
    for z in range(32):
        mine, far = u[z, 0:8], u[z, 8:16]
        turned = roll(mine, 4, 0)
        high.append(
            jnp.where(sub >= 4, turned, jnp.where(sub == 3, roll(far, 4, 0), roll(b[z, 8:16], 1, 0)))
        )
        low.append(jnp.where(sub == 1, roll(b[z, 0:8], 5, 0), turned))

    def packed(parts, t):
        if t < 16:
            return jnp.where(lane < 64, parts[t], roll(parts[t + 16], 64, 1))
        return halo_lanes([parts[t - 16 + 4 * q] for q in range(8)])

    for t in range(20):
        h, l = packed(high, t), packed(low, t)
        sa[26 + t] = either(even_x, h, l)
        sb[26 + t] = either(even_x, l, h)


def bottom_kernel(
    own, ya, yb,
    out,
    f2, a2, b2, ws2, wl2, wm2, inv2, diag2, u2, v2,
    f3, a3, b3, ws3, wl3, wm3, inv3, diag3, u3, v3,
    pairs, wide,
):
    ix, iy, even_x, even_y, has_right, has_left, has_above, has_below = places()
    lane, sub = iota((8, 128), 1), iota((8, 128), 0)

    def put(n, x, rows, own_part, up, down):
        up, down = only(has_above, up), only(has_below, down)
        (f2, a2, b2)[n][x, rows : rows + 8] = jnp.where(
            lane < 32, own_part, jnp.where(lane < 64, roll(up, 32, 1), only(lane >= 96, roll(down, 96, 1)))
        )

    for d in range(8):
        tiles = [
            (own[3 * d + t], either(even_y, ya[3 * d + t], yb[3 * d + t]), either(even_y, yb[3 * d + t], ya[3 * d + t]))
            for t in range(3)
        ]
        for n in range(3):
            for t in range(3):
                put(n, 2 * d + t // 2, 8 * (t % 2), *(roll(tile, -32 * n, 1) for tile in tiles[t]))
            put(n, 2 * d + 1, 8, *(roll(tile, -96, 1) for tile in tiles[n]))
    b2[16] = jnp.zeros((16, 128), F32)
    b3[8] = jnp.zeros((8, 128), F32)
    level2 = Level((f2, a2, b2, ws2, wl2, wm2, inv2, diag2, u2, v2), 0.0625, False, 16)
    level2.build(WEIGHTS[0])
    level2.sweeps_down()

    lanes_in, lanes_out = iota((128, 128), 0), iota((128, 128), 1)
    half = indicator(half_wrapped(lanes_in, 96, 64) == lanes_out)
    twice = indicator(lanes_in == half_wrapped(lanes_out, 96, 64))

    def coarse():
        wide[0:128, :] = matmul(pairs[...].reshape(128, 128), half)
        halves = wide[pl.ds(0, 64, stride=2), :] + wide[pl.ds(1, 64, stride=2), :]
        return (0.125 * halves).reshape(8, 8, 128)

    sum_planes(a2, pairs, 16)
    a3[...] = coarse()
    sum_planes(b2, pairs, 16)
    b3[0:8] = coarse()
    level2.residual_pairs(u2, pairs, 16)
    f3[...] = coarse()
    level3 = Level((f3, a3, b3, ws3, wl3, wm3, inv3, diag3, u3, v3), 0.015625, False, 8)
    level3.build(BOTTOM_WEIGHT)

    def two_sweeps(_, carry):
        level3.sweep(BOTTOM_WEIGHT, u3, v3)
        level3.sweep(BOTTOM_WEIGHT, v3, u3)
        return carry

    lax.fori_loop(0, (BOTTOM - 2) // 2, two_sweeps, 0)
    level3.sweep(BOTTOM_WEIGHT, u3, v3)

    fine = matmul(v3[0:8].reshape(64, 128), twice)
    wide[pl.ds(0, 64, stride=2), :] = fine
    wide[pl.ds(1, 64, stride=2), :] = fine
    for x in range(16):
        u2[x] = u2[x] + only(inv2[x] > 0.0, wide[16 * (x // 2) : 16 * (x // 2) + 16, :])
    level2.sweeps_up()
    out[...] = v2[0:16]


def ready_kernel(xa, xb, own_u, u0):
    ix, iy, even_x, even_y, has_right, has_left, has_above, has_below = places()
    lane, sub = iota((8, 128), 1), iota((8, 128), 0)

    for z in range(64):
        u0[z, 0:8, :] = own_u[z, 0:8, :]
        far, at = own_u[z, 8:16, 0:128], 3 * (z // 8)
        far = unpack_three(z % 8, far, lambda t: only(has_right, either(even_x, xa[at + t], xb[at + t])), 1)
        far = unpack_three(z % 8, far, lambda t: only(has_left, either(even_x, xb[at + t], xa[at + t])), 4)
        u0[z, 8:16, 0:128] = far
        g, k = z // 16, z % 16
        t, e = 24 + g // 2, g % 2
        right = only(has_right, either(even_x, xa[t], xb[t]))
        left = only(has_left, either(even_x, xb[t], xa[t]))
        edge = jnp.where(sub < 4, roll(right, 4, 0) if e else right, left if e else roll(left, 4, 0))
        u0[z, 8:16, 128:256] = jnp.where(
            lane < 4, roll(edge, -8 * k, 1), only(lane >= 124, roll(edge, 120 - 8 * k, 1))
        )
    u0[64] = jnp.zeros((16, 256), F32)


def up_kernel(
    v2, xa, xb, f1, a1, b1, u1, u0_in, f0, f0x, ws0, wl0, wm0, inv0, diag0,
    field_out, residual_out,
    u0, v0, bx1, ws1, wl1, wm1, inv1, diag1, ux1, v1, spread,
):
    ix, iy, even_x, even_y, has_right, has_left, has_above, has_below = places()
    sub = iota((8, 128), 0)
    lanes_in, lanes_out = iota((128, 128), 0), iota((128, 128), 1)

    def received(one, two, z):
        main = either(even_x, one[26 + z % 16], two[26 + z % 16])
        halo = either(even_x, one[42 + z % 4], two[42 + z % 4])
        return with_halo_lanes(roll(main, 64, 1) if z >= 16 else main, halo, z // 4)

    for z in range(32):
        right = only(has_right, received(xa, xb, z))
        left = only(has_left, received(xb, xa, z))
        ux1[z, 0:8] = jnp.where(sub < 4, u1[z, 0:8], right)
        ux1[z, 8:16] = jnp.where(sub == 0, right, only(sub >= 3, left))
        bx1[z, 0:8] = b1[z, 0:8]
        bx1[z, 8:16] = jnp.where(
            sub == 0, roll(right, -1, 0), jnp.where(sub == 3, roll(left, 3, 0), b1[z, 8:16])
        )
    bx1[32] = jnp.zeros((16, 128), F32)
    level1 = Level((f1, a1, bx1, ws1, wl1, wm1, inv1, diag1, ux1, v1), 0.25, True, 16)
    level1.build()
    double = indicator(lanes_in == jnp.where(lanes_out < 96, lanes_out // 2, 64 + lanes_out // 2))
    columns = [v2[jnp.clip(2 * ix + k, 0, 15)] for k in range(-3, 5)]
    fine = matmul(jnp.concatenate(columns, 0), double)
    for k in range(8):
        for e in range(2):
            for x in range(2):
                spread[pl.ds(e * 16 + (2 * (k - 3) + x) % 16, 16, stride=32), :] = fine[16 * k : 16 * k + 16]

    def correct_1(z, carry):
        rows = spread[pl.ds(pl.multiple_of(16 * z, 16), 16), :]
        ux1[z] = ux1[z] + only(inv1[z] > 0.0, rows)
        return carry

    lax.fori_loop(0, 32, correct_1, 0, unroll=8)
    level1.sweeps_up()

    for z in range(32):
        parts = v1[z, 0:8], v1[z, 8:16]
        rows = jnp.where(sub < 6, parts[0], parts[1])
        spread[pl.ds(16 * z, 8, stride=2), :] = rows
        spread[pl.ds(16 * z + 1, 8, stride=2), :] = rows
    lanes_in, lanes_out = iota((128, 256), 0), iota((128, 256), 1)
    double = indicator(lanes_in == lanes_out // 2)

    def correct_0(z, carry):
        fine = matmul(spread[pl.ds(pl.multiple_of(64 * z, 64), 64), :], double)
        for k in range(4):
            rows = fine[16 * k : 16 * k + 16]
            for e in range(2):
                m = 8 * z + 2 * k + e
                u0[m] = u0_in[m] + only(inv0[m] > 0.0, rows)
        return carry

    lax.fori_loop(0, 8, correct_0, 0, unroll=4)
    level0 = Level((Rows(f0, f0x), None, u0, ws0, wl0, wm0, inv0, diag0, u0, v0), 1.0, True, 16)
    u0[64] = jnp.zeros((16, 256), F32)
    v0[64] = jnp.zeros((16, 256), F32)
    level0.sweeps_up()
    level0.residual(v0, residual_out, 8, 128)

    def out(z, carry):
        field_out[z] = v0[z, 0:8, 0:128]
        return carry

    lax.fori_loop(0, 64, out, 0, unroll=4)


def call(kernel, outs, scratch, n_in, cost=1):
    vmem = pl.BlockSpec(memory_space=pltpu.VMEM)
    need = sum(4 * p * r * n for p, r, n in ((1,) * (3 - len(shape)) + shape for shape in scratch))
    return pl.pallas_call(
        kernel,
        out_shape=[jax.ShapeDtypeStruct(shape, F32) for shape in outs],
        in_specs=[vmem] * n_in,
        out_specs=[vmem] * len(outs),
        scratch_shapes=[pltpu.VMEM(shape, F32) for shape in scratch],
        cost_estimate=pl.CostEstimate(
            flops=cost * 1_000_000_000, bytes_accessed=cost * 3_000_000, transcendentals=0
        ),
        compiler_params=pltpu.CompilerParams(vmem_limit_bytes=need + 4 * 1024 * 1024),
    )


def swaps(axis):
    size = lax.axis_size(axis)
    first = [(i, i ^ 1) for i in range(size)]
    second = [(i, i + 1 if i % 2 else i - 1) for i in range(size)]
    second = [(i, j % size) for i, j in second]
    return first, second


def swap(a, b, axis):
    first, second = swaps(axis)
    return lax.ppermute(a, axis, first), lax.ppermute(b, axis, second)


def body(right_side, alpha, beta):
    def tiles(n):
        return (n, 8, 128)

    f, a, b = right_side, alpha, beta
    sizes = [tiles(64), tiles(64), tiles(32), tiles(32)]
    packs = call(functools.partial(pack_kernel, 0), sizes, [], 1)(f)
    packs = call(functools.partial(pack_kernel, 1), sizes, [], 5)(a, *packs)
    sizes = [tiles(80), tiles(80), tiles(32), tiles(32)]
    xa, xb, ya, yb = call(functools.partial(pack_kernel, 2), sizes, [], 5)(b, *packs)
    xa, xb = swap(xa, xb, "gx")
    ya, yb = swap(ya, yb, "gy")
    ca, cb = call(corner_kernel, [tiles(32), tiles(32)], [], 2)(ya, yb)
    ca, cb = swap(ca, cb, "gx")
    top, top_more = (64, 8, 256), (65, 8, 256)
    f, a, b, ab, packed = call(
        own_rows_kernel, [top, top, top_more, tiles(32), tiles(20)], [(32, 8, 256), (256, 128)], 5, cost=3
    )(f, a, b, ya, yb)
    aba, abb = swap(packed, packed, "gx")

    full, more = (64, 16, 256), (65, 16, 256)
    source, packed, u, *fine = call(
        fine_down_kernel,
        [tiles(16), tiles(10), more, top] + [full] * 5,
        [top, top_more, more, (32, 8, 256), (256, 128)],
        7,
        cost=50,
    )(f, a, b, xa, xb, ca, cb)
    ga, gb = swap(packed, packed, "gx")
    ra, rb = call(u_edges_kernel, [tiles(26), tiles(26)], [], 1, cost=50)(u)

    full, more = (32, 16, 128), (33, 16, 128)
    copies, f1, a1, b1, u1 = call(
        middle_down_kernel,
        [tiles(24), full, full, more, more],
        [full, full, full, full, full, more, tiles(16), (128, 128)],
        8,
        cost=50,
    )(source, ga, gb, ab, aba, abb, ra, rb)
    own = lax.all_to_all(copies, "gx", 0, 0, tiled=True)
    ya, yb = swap(own, own, "gy")
    sa, sb = call(edges_kernel, [tiles(46), tiles(46)], [], 5, cost=50)(own, ra, rb, b1, u1)
    sa, sb = swap(sa, sb, "gx")
    (u0,) = call(ready_kernel, [(65, 16, 256)], [], 3)(sa, sb, u)

    def level(planes, rows, lanes):
        one, two = (planes, rows, lanes), (planes + 1, rows, lanes)
        return [one, one, two, one, one, one, one, one, two, two]

    (u2,) = call(
        bottom_kernel,
        [(16, 16, 128)],
        level(16, 16, 128) + level(8, 8, 128) + [(8, 16, 128), (128, 128)],
        3,
        cost=50,
    )(own, ya, yb)
    return tuple(
        call(
            up_kernel,
            [tiles(64), tiles(64)],
            [(65, 16, 256)] * 2 + level(32, 16, 128)[2:] + [(512, 128)],
            15,
        )(u2, sa, sb, f1, a1, b1, u1, u0, f, *fine)
    )


def solution(mesh):
    return jax.shard_map(
        body,
        mesh=mesh,
        in_specs=(P(None, "gx", "gy"),) * 3,
        out_specs=(P(None, "gx", "gy"),) * 2,
        check_vma=False,
    )
```

```python
import functools

import jax
import jax.numpy as jnp
from jax import lax
from jax.experimental import pallas as pl
from jax.experimental.pallas import tpu as pltpu
from jax.sharding import PartitionSpec as P

F32 = jnp.float32
WEIGHTS = (0.6, 0.75, 0.9)
BOTTOM_WEIGHT = 0.8
BOTTOM = 12
YH = 20


def roll(x, shift, axis):
    shift %= x.shape[axis]
    return x if shift == 0 else pltpu.roll(x, shift, axis)


def iota(shape, axis):
    return lax.broadcasted_iota(jnp.int32, shape, axis)


def either(flag, a, b):
    return jnp.where(flag, a, b)


def only(flag, a):
    return jnp.where(flag, a, 0.0)


def matmul(a, chooser):
    total = None
    for _ in range(3):
        part = a.astype(jnp.bfloat16)
        product = jnp.dot(part, chooser, preferred_element_type=F32)
        total = product if total is None else total + product
        a = a - part.astype(F32)
    return total


def indicator(mask):
    return jnp.where(mask, 1.0, 0.0).astype(jnp.bfloat16)


def half_wrapped(i, low, high):
    return jnp.where(i < high, i // 2, jnp.where(i >= low, 64 + i // 2, -1))


class Level:
    def __init__(self, refs, factor, circular, unroll):
        self.f, self.a, self.b, self.ws, self.wl, self.wm, self.inv, self.diag, self.u, self.v = refs
        self.half = 0.5 * factor
        self.circular = circular
        self.planes, self.rows, self.lanes = self.f.shape
        self.unroll = unroll

    def build(self, weight=None):
        shape = (self.rows, self.lanes)
        sub = iota(shape, 0)
        half = self.half
        self.u[self.planes] = jnp.zeros(shape, F32)
        self.v[self.planes] = jnp.zeros(shape, F32)

        def step(m, carry):
            before, b = carry
            after = self.b[m + 1]
            wl = half * (b + roll(b, -1, 1))
            beside = roll(b, -1, 0)
            if not self.circular:
                beside = only(sub < self.rows - 1, beside)
            ws = half * (b + beside)
            wm = half * (b + after)
            below = roll(ws, 1, 0)
            if not self.circular:
                below = jnp.where(sub == 0, half * b, below)
            diag = self.a[m] + (wl + roll(wl, 1, 1) + ws + below + wm + before)
            inv = jnp.where(b > 0.0, 1.0 / diag, 0.0)
            self.ws[m] = ws if self.circular else only(sub < self.rows - 1, ws)
            self.wl[m] = wl
            self.wm[m] = wm
            self.diag[m] = diag
            self.inv[m] = inv
            if weight is not None:
                self.u[m] = (weight * self.f[m]) * inv
            return wm, after

        first = self.b[0]
        lax.fori_loop(0, self.planes, step, (half * first, first), unroll=self.unroll)

    def beside(self, m, u, after, flow):
        wl, ws, wm = self.wl[m], self.ws[m], self.wm[m]
        along = wl * roll(u, -1, 1) + roll(wl * u, 1, 1)
        across = ws * roll(u, -1, 0) + roll(ws * u, 1, 0)
        return self.f[m] + (along + across + (wm * after + flow)), wm * u

    def sweep(self, weight, src, dst):
        def step(m, carry):
            flow, u = carry
            after = src[m + 1]
            total, flow = self.beside(m, u, after, flow)
            dst[m] = (1.0 - weight) * u + (weight * self.inv[m]) * total
            return flow, after

        first = src[0]
        lax.fori_loop(0, self.planes, step, (jnp.zeros_like(first), first), unroll=self.unroll)

    def sweeps_down(self):
        self.sweep(WEIGHTS[1], self.u, self.v)
        self.sweep(WEIGHTS[2], self.v, self.u)

    def sweeps_up(self):
        self.sweep(WEIGHTS[0], self.u, self.v)
        self.sweep(WEIGHTS[1], self.v, self.u)
        self.sweep(WEIGHTS[2], self.u, self.v)

    def residual_pairs(self, src, dst, rows):
        def step(m, carry):
            flow, u = carry
            total = None
            for k in (2 * m, 2 * m + 1):
                after = src[k + 1]
                part, flow = self.beside(k, u, after, flow)
                part = (part - self.diag[k] * u)[:rows]
                total = part if total is None else total + part
                u = after
            dst[m] = total
            return flow, u

        first = src[0]
        lax.fori_loop(0, self.planes // 2, step, (jnp.zeros_like(first), first), unroll=max(self.unroll // 2, 1))

    def residual(self, src, dst, rows, lanes):
        def step(m, carry):
            flow, u = carry
            after = src[m + 1]
            part, flow = self.beside(m, u, after, flow)
            dst[m] = (part - self.diag[m] * u)[:rows, :lanes]
            return flow, after

        first = src[0]
        lax.fori_loop(0, self.planes, step, (jnp.zeros_like(first), first), unroll=self.unroll)


def sum_planes(src, dst, rows):
    def step(m, carry):
        dst[m] = src[2 * m][:rows] + src[2 * m + 1][:rows]
        return carry

    lax.fori_loop(0, dst.shape[0], step, 0, unroll=8)


def places():
    ix, iy = lax.axis_index("gx"), lax.axis_index("gy")
    nx, ny = lax.axis_size("gx"), lax.axis_size("gy")
    return ix, iy, ix % 2 == 0, iy % 2 == 0, ix < nx - 1, ix > 0, iy < ny - 1, iy > 0


def pieces(plane):
    for tile in range(3):
        first = 3 * plane - 8 * tile
        if -3 < first < 8:
            yield tile, first, (max(first, 0) - first, min(first + 3, 8) - first)


def pack_three(read, low_row, high_row, write):
    sub = iota((8, 128), 0)
    low = [jnp.zeros((8, 128), F32)] * 3
    high = [jnp.zeros((8, 128), F32)] * 3
    for plane in range(8):
        rows = read(plane)
        for tile, first, _ in pieces(plane):
            here = (sub >= first) & (sub < first + 3)
            low[tile] = jnp.where(here, roll(rows, first - low_row, 0), low[tile])
            high[tile] = jnp.where(here, roll(rows, first - high_row, 0), high[tile])
    for tile in range(3):
        write(tile, low[tile], high[tile])


def unpack_three(plane, into, tile_of, row):
    sub = iota((8, 128), 0)
    for tile, first, (low, high) in pieces(plane):
        here = (sub >= row + low) & (sub < row + high)
        into = jnp.where(here, roll(tile_of(tile), row - first, 0), into)
    return into


def pack_kernel(field, *refs):
    own, *refs = refs
    before, (xa, xb, ya, yb) = refs[:-4], refs[-4:]
    ix, iy, even_x, even_y, *_ = places()
    lane, sub = iota((8, 128), 1), iota((8, 128), 0)

    def y_step(z, carry):
        parts = []
        for shift in (0, YH):
            first = roll(own[z], shift + YH * field, 1)
            second = roll(own[z + 32], shift + YH * field + 64, 1)
            parts.append(jnp.where(lane < 64, first, second))
        low, high = parts
        here = (lane % 64 >= YH * field) & (lane % 64 < YH * (field + 1))
        for out, value, old in ((ya, either(even_y, high, low), 2), (yb, either(even_y, low, high), 3)):
            out[z] = jnp.where(here, value, before[old][z]) if before else only(here, value)
        return carry

    lax.fori_loop(0, 32, y_step, 0, unroll=8)

    def x_step(q, carry):
        extra_low = extra_high = jnp.zeros((8, 128), F32)
        for j in range(4):
            z = 4 * q + j
            value = own[z]
            low, high = roll(value, 3 * field, 0), roll(value, (3, 6, 2)[field], 0)
            for out, chosen, old in ((xa, either(even_x, high, low), 0), (xb, either(even_x, low, high), 1)):
                out[z] = jnp.where(sub < 3 * field, before[old][z], chosen) if before else chosen
            if field == 2:
                here = sub // 2 == j
                extra_low = jnp.where(here, roll(value, 2 * j - 2, 0), extra_low)
                extra_high = jnp.where(here, roll(value, 2 * j - 6, 0), extra_high)
        if field == 2:
            xa[64 + q] = either(even_x, extra_high, extra_low)
            xb[64 + q] = either(even_x, extra_low, extra_high)
        return carry

    lax.fori_loop(0, 16, x_step, 0, unroll=4)


def corner_kernel(ya, yb, ca, cb):
    ix, iy, even_x, even_y, *_ = places()
    sub = iota((8, 128), 0)

    def step(z, carry):
        right, left = either(even_y, ya[z], yb[z]), either(even_y, yb[z], ya[z])
        low = jnp.where(sub < 4, left, roll(right, 4, 0))
        high = jnp.where(sub < 4, roll(left, 4, 0), right)
        ca[z] = either(even_x, high, low)
        cb[z] = either(even_x, low, high)
        return carry

    lax.fori_loop(0, 32, step, 0, unroll=4)


class Rows:
    def __init__(self, top, bottom):
        self.top, self.bottom = top, bottom
        self.shape = (top.shape[0], 16, top.shape[2])

    def __getitem__(self, m):
        return jnp.concatenate([self.top[m], self.bottom[m]], 0)


def spread_columns(lane, high, low, at):
    return jnp.where(lane < YH, roll(high, -at, 1), only(lane >= 128 - YH, roll(low, 128 - YH - at, 1)))


def coarse_fine(pairs, wide):
    half = indicator(iota((256, 128), 0) // 2 == iota((256, 128), 1))
    wide[...] = matmul(pairs[...].reshape(256, 256), half)
    return 0.125 * (wide[pl.ds(0, 128, stride=2), :] + wide[pl.ds(1, 128, stride=2), :])


def own_rows_kernel(f, a, b, ya, yb, fx, ax, bx, ab, packed, pairs, wide):
    ix, iy, even_x, even_y, has_right, has_left, has_above, has_below = places()
    lane = iota((8, 128), 1)

    def unpack(z, carry):
        up = only(has_above, either(even_y, ya[z], yb[z]))
        down = only(has_below, either(even_y, yb[z], ya[z]))
        for n, (own, full) in enumerate(((f, fx), (a, ax), (b, bx))):
            for h in range(2):
                full[z + 32 * h, :, 0:128] = own[z + 32 * h]
                full[z + 32 * h, :, 128:256] = spread_columns(lane, up, down, 64 * h + YH * n)
        return carry

    lax.fori_loop(0, 32, unpack, 0, unroll=8)
    bx[64] = jnp.zeros((8, 256), F32)
    sum_planes(ax, pairs, 8)
    ab[0:16] = coarse_fine(pairs, wide).reshape(16, 8, 128)
    sum_planes(bx, pairs, 8)
    ab[16:32] = coarse_fine(pairs, wide).reshape(16, 8, 128)
    for t in range(16):
        packed[t] = jnp.where(lane < 64, ab[t], roll(ab[16 + t], 64, 1))
    for t in range(4):
        packed[16 + t] = halo_lanes([ab[t + 4 * q + 16 * n] for q in range(4) for n in range(2)])


def halo_lanes(parts):
    lane = iota((8, 128), 1)
    packed = jnp.zeros((8, 128), F32)
    for n, part in enumerate(parts):
        pair = jnp.where(lane < 16 * n + 8, roll(part, 16 * n - 64, 1), roll(part, 16 * n + 8 - 120, 1))
        packed = jnp.where(lane // 16 == n, pair, packed)
    return packed


def with_halo_lanes(own, packed, n):
    lane = iota((8, 128), 1)
    right, left = roll(packed, 64 - 16 * n, 1), roll(packed, 112 - 16 * n, 1)
    return jnp.where(lane < 64, own, jnp.where(lane < 72, right, only(lane >= 120, left)))


def fine_down_kernel(
    f, a, b, xa, xb, ca, cb,
    source, packed, u, fx, ws, wl, wm, inv, diag,
    ax, bx, v, pairs, wide,
):
    ix, iy, even_x, even_y, has_right, has_left, has_above, has_below = places()
    lane, sub = iota((8, 128), 1), iota((8, 128), 0)

    def unpack(q, carry):
        for j in range(4):
            zz = 4 * q + j
            corner_r = only(has_right, either(even_x, ca[zz], cb[zz]))
            corner_l = only(has_left, either(even_x, cb[zz], ca[zz]))
            up = only(has_above, jnp.where(sub < 4, roll(corner_r, 4, 0), corner_l))
            down = only(has_below, jnp.where(sub < 4, corner_r, roll(corner_l, 4, 0)))
            for h in range(2):
                z, e = zz + 32 * h, 64 + q + 8 * h
                main_r = only(has_right, either(even_x, xa[z], xb[z]))
                main_l = only(has_left, either(even_x, xb[z], xa[z]))
                extra_r = only(has_right, either(even_x, xa[e], xb[e]))
                extra_l = only(has_left, either(even_x, xb[e], xa[e]))
                beside = (
                    jnp.where(sub < 3, main_r, only(sub >= 5, roll(main_l, 5, 0))),
                    jnp.where(sub < 3, roll(main_r, -3, 0), only(sub >= 5, roll(main_l, 2, 0))),
                    jnp.where(
                        sub < 2,
                        roll(main_r, 2, 0),
                        jnp.where(
                            sub < 4,
                            roll(extra_r, 2 - 2 * j, 0),
                            jnp.where(sub < 6, roll(main_l, 6, 0), roll(extra_l, 6 - 2 * j, 0)),
                        ),
                    ),
                )
                for n, full in enumerate((fx, ax, bx)):
                    full[z, :, 0:128] = beside[n]
                    full[z, :, 128:256] = spread_columns(lane, up, down, 64 * h + YH * n)
        return carry

    lax.fori_loop(0, 8, unpack, 0, unroll=2)
    bx[64] = jnp.zeros((8, 256), F32)
    level = Level((Rows(f, fx), Rows(a, ax), Rows(b, bx), ws, wl, wm, inv, diag, u, v), 1.0, True, 16)
    level.build(WEIGHTS[0])
    level.sweeps_down()
    level.residual_pairs(u, pairs, 8)
    source[...] = coarse_fine(pairs, wide).reshape(16, 8, 128)
    for t in range(8):
        packed[t] = jnp.where(lane < 64, source[t], roll(source[t + 8], 64, 1))
    for t in range(2):
        packed[8 + t] = halo_lanes([source[t + 2 * q] for q in range(8)])


def u_edges_kernel(u, ra, rb):
    ix, iy, even_x, even_y, *_ = places()
    lane, sub = iota((8, 128), 1), iota((8, 128), 0)

    def put(at, low, high):
        ra[at] = either(even_x, high, low)
        rb[at] = either(even_x, low, high)

    def main(g, carry):
        pack_three(
            lambda z: u[8 * g + z, 0:8, 0:128], 1, 4, lambda tile, low, high: put(3 * g + tile, low, high)
        )
        return carry

    lax.fori_loop(0, 8, main, 0, unroll=2)
    for t in range(2):
        low = high = jnp.zeros((8, 128), F32)
        for g in range(2):
            for k in range(16):
                edge = u[16 * (2 * t + g) + k, 0:8, 128:256]
                edge = roll(jnp.where(lane < 4, edge, roll(edge, 8, 1)), 8 * k, 1)
                here = (lane // 8 == k) & (sub // 4 == g)
                turned = roll(edge, 4, 0)
                low = jnp.where(here, turned if g else edge, low)
                high = jnp.where(here, edge if g else turned, high)
        put(24 + t, low, high)


def middle_down_kernel(
    source_in, ga, gb, ab, aba, abb, _a, _b,
    copies, f1, a1, b, u,
    ws, wl, wm, inv, diag, v, pairs, wide,
):
    ix, iy, even_x, even_y, has_right, has_left, has_above, has_below = places()
    sub = iota((8, 128), 0)

    def right(one, two, at):
        return only(has_right, either(even_x, one[at], two[at]))

    def left(one, two, at):
        return only(has_left, either(even_x, two[at], one[at]))

    for t in range(16):
        sides = []
        for side in (right, left):
            f = side(ga, gb, t % 8)
            f = with_halo_lanes(roll(f, 64, 1) if t >= 8 else f, side(ga, gb, 8 + t % 2), t // 2)
            both, halo = side(aba, abb, t), side(aba, abb, 16 + t % 4)
            sides.append(
                (f, with_halo_lanes(both, halo, t // 4 * 2), with_halo_lanes(roll(both, 64, 1), halo, t // 4 * 2 + 1))
            )
        for n, (own, full) in enumerate(((source_in[t], f1), (ab[t], a1), (ab[16 + t], b))):
            high, low = sides[0][n], sides[1][n]
            full[2 * t, 0:8] = jnp.where(sub < 4, own, roll(high, 4, 0))
            full[2 * t, 8:16] = only(sub >= 4, roll(low, 4, 0))
            full[2 * t + 1, 0:8] = jnp.where(sub < 4, roll(own, 4, 0), high)
            full[2 * t + 1, 8:16] = only(sub >= 4, low)

    b[32] = jnp.zeros((16, 128), F32)
    level = Level((f1, a1, b, ws, wl, wm, inv, diag, u, v), 0.25, True, 16)
    level.build(WEIGHTS[0])
    level.sweeps_down()

    lanes_in, lanes_out = iota((128, 128), 0), iota((128, 128), 1)
    half = indicator((lanes_in // 2 == lanes_out) & (lanes_out < 32))

    def coarse():
        wide[...] = matmul(pairs[...].reshape(128, 128), half)
        rows = [wide[pl.ds(k, 16, stride=8), :] for k in range(4)]
        return 0.125 * (rows[0] + rows[1]), 0.125 * (rows[2] + rows[3])

    sum_planes(a1, pairs, 8)
    alpha = coarse()
    sum_planes(b, pairs, 8)
    beta = coarse()
    level.residual_pairs(u, pairs, 8)
    source = coarse()
    blocks = []
    for k in range(2):
        blocks.append(source[k] + roll(alpha[k], 32, 1) + roll(beta[k], 64, 1))
    parts = [blocks[0][:8], blocks[0][8:], blocks[1][:8]]
    last = blocks[1][8:]
    lane = iota((8, 128), 1)
    for n, part in enumerate(parts):
        part = jnp.where(lane < 96, part, roll(last, 96 - 32 * n, 1))
        for d in range(8):
            copies[3 * d + n] = part


def edges_kernel(_, ra, rb, b, u, sa, sb):
    ix, iy, even_x, even_y, *_ = places()
    lane, sub = iota((8, 128), 1), iota((8, 128), 0)
    sa[0:26] = ra[...]
    sb[0:26] = rb[...]
    high, low = [], []
    for z in range(32):
        mine, far = u[z, 0:8], u[z, 8:16]
        turned = roll(mine, 4, 0)
        high.append(
            jnp.where(sub >= 4, turned, jnp.where(sub == 3, roll(far, 4, 0), roll(b[z, 8:16], 1, 0)))
        )
        low.append(jnp.where(sub == 1, roll(b[z, 0:8], 5, 0), turned))

    def packed(parts, t):
        if t < 16:
            return jnp.where(lane < 64, parts[t], roll(parts[t + 16], 64, 1))
        return halo_lanes([parts[t - 16 + 4 * q] for q in range(8)])

    for t in range(20):
        h, l = packed(high, t), packed(low, t)
        sa[26 + t] = either(even_x, h, l)
        sb[26 + t] = either(even_x, l, h)


def bottom_kernel(
    own, ya, yb,
    out,
    f2, a2, b2, ws2, wl2, wm2, inv2, diag2, u2, v2,
    f3, a3, b3, ws3, wl3, wm3, inv3, diag3, u3, v3,
    pairs, wide,
):
    ix, iy, even_x, even_y, has_right, has_left, has_above, has_below = places()
    lane, sub = iota((8, 128), 1), iota((8, 128), 0)

    high, middle, low = lane < 64, lane < 32, lane >= 96
    for d in range(8):
        tiles = []
        for t in range(3):
            one, two = ya[3 * d + t], yb[3 * d + t]
            tiles.append(
                (own[3 * d + t], only(has_above, either(even_y, one, two)), only(has_below, either(even_y, two, one)))
            )
        for n, full in enumerate((f2, a2, b2)):
            for t in range(4):
                mine, up, down = tiles[n if t == 3 else t]
                at = 96 if t == 3 else 32 * n
                beside = jnp.where(high, roll(up, 32 - at, 1), only(low, roll(down, 96 - at, 1)))
                full[2 * d + t // 2, 8 * (t % 2) : 8 * (t % 2) + 8] = jnp.where(middle, roll(mine, -at, 1), beside)
    b2[16] = jnp.zeros((16, 128), F32)
    b3[8] = jnp.zeros((8, 128), F32)
    level2 = Level((f2, a2, b2, ws2, wl2, wm2, inv2, diag2, u2, v2), 0.0625, False, 16)
    level2.build(WEIGHTS[0])
    level2.sweeps_down()

    lanes_in, lanes_out = iota((128, 128), 0), iota((128, 128), 1)
    half = indicator(half_wrapped(lanes_in, 96, 64) == lanes_out)
    twice = indicator(lanes_in == half_wrapped(lanes_out, 96, 64))

    def coarse():
        wide[0:128, :] = matmul(pairs[...].reshape(128, 128), half)
        halves = wide[pl.ds(0, 64, stride=2), :] + wide[pl.ds(1, 64, stride=2), :]
        return (0.125 * halves).reshape(8, 8, 128)

    sum_planes(a2, pairs, 16)
    a3[...] = coarse()
    sum_planes(b2, pairs, 16)
    b3[0:8] = coarse()
    level2.residual_pairs(u2, pairs, 16)
    f3[...] = coarse()
    level3 = Level((f3, a3, b3, ws3, wl3, wm3, inv3, diag3, u3, v3), 0.015625, False, 8)
    level3.build(BOTTOM_WEIGHT)

    def two_sweeps(_, carry):
        level3.sweep(BOTTOM_WEIGHT, u3, v3)
        level3.sweep(BOTTOM_WEIGHT, v3, u3)
        return carry

    lax.fori_loop(0, (BOTTOM - 2) // 2, two_sweeps, 0)
    level3.sweep(BOTTOM_WEIGHT, u3, v3)

    fine = matmul(v3[0:8].reshape(64, 128), twice)
    wide[pl.ds(0, 64, stride=2), :] = fine
    wide[pl.ds(1, 64, stride=2), :] = fine
    for x in range(16):
        u2[x] = u2[x] + only(inv2[x] > 0.0, wide[16 * (x // 2) : 16 * (x // 2) + 16, :])
    level2.sweeps_up()
    out[...] = v2[0:16]


def ready_kernel(xa, xb, own_u, u0):
    ix, iy, even_x, even_y, has_right, has_left, has_above, has_below = places()
    lane, sub = iota((8, 128), 1), iota((8, 128), 0)

    for z in range(64):
        u0[z, 0:8, :] = own_u[z, 0:8, :]
        far, at = own_u[z, 8:16, 0:128], 3 * (z // 8)
        far = unpack_three(z % 8, far, lambda t: only(has_right, either(even_x, xa[at + t], xb[at + t])), 1)
        far = unpack_three(z % 8, far, lambda t: only(has_left, either(even_x, xb[at + t], xa[at + t])), 4)
        u0[z, 8:16, 0:128] = far
        g, k = z // 16, z % 16
        t, e = 24 + g // 2, g % 2
        right = only(has_right, either(even_x, xa[t], xb[t]))
        left = only(has_left, either(even_x, xb[t], xa[t]))
        edge = jnp.where(sub < 4, roll(right, 4, 0) if e else right, left if e else roll(left, 4, 0))
        u0[z, 8:16, 128:256] = jnp.where(
            lane < 4, roll(edge, -8 * k, 1), only(lane >= 124, roll(edge, 120 - 8 * k, 1))
        )
    u0[64] = jnp.zeros((16, 256), F32)


def up_kernel(
    v2, xa, xb, f1, a1, b1, u1, u0_in, f0, f0x, ws0, wl0, wm0, inv0, diag0,
    field_out, residual_out,
    u0, v0, bx1, ws1, wl1, wm1, inv1, diag1, ux1, v1, spread,
):
    ix, iy, even_x, even_y, has_right, has_left, has_above, has_below = places()
    sub = iota((8, 128), 0)
    lanes_in, lanes_out = iota((128, 128), 0), iota((128, 128), 1)

    def received(one, two, z):
        main = either(even_x, one[26 + z % 16], two[26 + z % 16])
        halo = either(even_x, one[42 + z % 4], two[42 + z % 4])
        return with_halo_lanes(roll(main, 64, 1) if z >= 16 else main, halo, z // 4)

    for z in range(32):
        right = only(has_right, received(xa, xb, z))
        left = only(has_left, received(xb, xa, z))
        ux1[z, 0:8] = jnp.where(sub < 4, u1[z, 0:8], right)
        ux1[z, 8:16] = jnp.where(sub == 0, right, only(sub >= 3, left))
        bx1[z, 0:8] = b1[z, 0:8]
        bx1[z, 8:16] = jnp.where(
            sub == 0, roll(right, -1, 0), jnp.where(sub == 3, roll(left, 3, 0), b1[z, 8:16])
        )
    bx1[32] = jnp.zeros((16, 128), F32)
    level1 = Level((f1, a1, bx1, ws1, wl1, wm1, inv1, diag1, ux1, v1), 0.25, True, 16)
    level1.build()
    double = indicator(lanes_in == jnp.where(lanes_out < 96, lanes_out // 2, 64 + lanes_out // 2))
    columns = [v2[jnp.clip(2 * ix + k, 0, 15)] for k in range(-3, 5)]
    fine = matmul(jnp.concatenate(columns, 0), double)
    for k in range(8):
        for e in range(2):
            for x in range(2):
                spread[pl.ds(e * 16 + (2 * (k - 3) + x) % 16, 16, stride=32), :] = fine[16 * k : 16 * k + 16]

    def correct_1(z, carry):
        rows = spread[pl.ds(pl.multiple_of(16 * z, 16), 16), :]
        ux1[z] = ux1[z] + only(inv1[z] > 0.0, rows)
        return carry

    lax.fori_loop(0, 32, correct_1, 0, unroll=8)
    level1.sweeps_up()

    for z in range(32):
        parts = v1[z, 0:8], v1[z, 8:16]
        rows = jnp.where(sub < 6, parts[0], parts[1])
        spread[pl.ds(16 * z, 8, stride=2), :] = rows
        spread[pl.ds(16 * z + 1, 8, stride=2), :] = rows
    lanes_in, lanes_out = iota((128, 256), 0), iota((128, 256), 1)
    double = indicator(lanes_in == lanes_out // 2)

    def correct_0(z, carry):
        fine = matmul(spread[pl.ds(pl.multiple_of(64 * z, 64), 64), :], double)
        for k in range(4):
            rows = fine[16 * k : 16 * k + 16]
            for e in range(2):
                m = 8 * z + 2 * k + e
                u0[m] = u0_in[m] + only(inv0[m] > 0.0, rows)
        return carry

    lax.fori_loop(0, 8, correct_0, 0, unroll=4)
    level0 = Level((Rows(f0, f0x), None, u0, ws0, wl0, wm0, inv0, diag0, u0, v0), 1.0, True, 16)
    u0[64] = jnp.zeros((16, 256), F32)
    v0[64] = jnp.zeros((16, 256), F32)
    level0.sweeps_up()
    level0.residual(v0, residual_out, 8, 128)

    def out(z, carry):
        field_out[z] = v0[z, 0:8, 0:128]
        return carry

    lax.fori_loop(0, 64, out, 0, unroll=4)


def call(kernel, outs, scratch, n_in, cost=1):
    vmem = pl.BlockSpec(memory_space=pltpu.VMEM)
    need = sum(4 * p * r * n for p, r, n in ((1,) * (3 - len(shape)) + shape for shape in scratch))
    return pl.pallas_call(
        kernel,
        out_shape=[jax.ShapeDtypeStruct(shape, F32) for shape in outs],
        in_specs=[vmem] * n_in,
        out_specs=[vmem] * len(outs),
        scratch_shapes=[pltpu.VMEM(shape, F32) for shape in scratch],
        cost_estimate=pl.CostEstimate(
            flops=cost * 1_000_000_000, bytes_accessed=cost * 3_000_000, transcendentals=0
        ),
        compiler_params=pltpu.CompilerParams(vmem_limit_bytes=need + 4 * 1024 * 1024),
    )


def swaps(axis):
    size = lax.axis_size(axis)
    first = [(i, i ^ 1) for i in range(size)]
    second = [(i, i + 1 if i % 2 else i - 1) for i in range(size)]
    second = [(i, j % size) for i, j in second]
    return first, second


def swap(a, b, axis):
    first, second = swaps(axis)
    return lax.ppermute(a, axis, first), lax.ppermute(b, axis, second)


def body(right_side, alpha, beta):
    def tiles(n):
        return (n, 8, 128)

    f, a, b = right_side, alpha, beta
    sizes = [tiles(64), tiles(64), tiles(32), tiles(32)]
    packs = call(functools.partial(pack_kernel, 0), sizes, [], 1)(f)
    packs = call(functools.partial(pack_kernel, 1), sizes, [], 5)(a, *packs)
    sizes = [tiles(80), tiles(80), tiles(32), tiles(32)]
    xa, xb, ya, yb = call(functools.partial(pack_kernel, 2), sizes, [], 5)(b, *packs)
    xa, xb = swap(xa, xb, "gx")
    ya, yb = swap(ya, yb, "gy")
    ca, cb = call(corner_kernel, [tiles(32), tiles(32)], [], 2)(ya, yb)
    ca, cb = swap(ca, cb, "gx")
    top, top_more = (64, 8, 256), (65, 8, 256)
    f, a, b, ab, packed = call(
        own_rows_kernel, [top, top, top_more, tiles(32), tiles(20)], [(32, 8, 256), (256, 128)], 5, cost=3
    )(f, a, b, ya, yb)
    aba, abb = swap(packed, packed, "gx")

    full, more = (64, 16, 256), (65, 16, 256)
    source, packed, u, *fine = call(
        fine_down_kernel,
        [tiles(16), tiles(10), more, top] + [full] * 5,
        [top, top_more, more, (32, 8, 256), (256, 128)],
        7,
        cost=50,
    )(f, a, b, xa, xb, ca, cb)
    ga, gb = swap(packed, packed, "gx")
    ra, rb = call(u_edges_kernel, [tiles(26), tiles(26)], [], 1, cost=50)(u)

    full, more = (32, 16, 128), (33, 16, 128)
    copies, f1, a1, b1, u1 = call(
        middle_down_kernel,
        [tiles(24), full, full, more, more],
        [full, full, full, full, full, more, tiles(16), (128, 128)],
        8,
        cost=50,
    )(source, ga, gb, ab, aba, abb, ra, rb)
    own = lax.all_to_all(copies, "gx", 0, 0, tiled=True)
    ya, yb = swap(own, own, "gy")
    sa, sb = call(edges_kernel, [tiles(46), tiles(46)], [], 5, cost=50)(own, ra, rb, b1, u1)
    sa, sb = swap(sa, sb, "gx")
    (u0,) = call(ready_kernel, [(65, 16, 256)], [], 3)(sa, sb, u)

    def level(planes, rows, lanes):
        one, two = (planes, rows, lanes), (planes + 1, rows, lanes)
        return [one, one, two, one, one, one, one, one, two, two]

    (u2,) = call(
        bottom_kernel,
        [(16, 16, 128)],
        level(16, 16, 128) + level(8, 8, 128) + [(8, 16, 128), (128, 128)],
        3,
        cost=50,
    )(own, ya, yb)
    return tuple(
        call(
            up_kernel,
            [tiles(64), tiles(64)],
            [(65, 16, 256)] * 2 + level(32, 16, 128)[2:] + [(512, 128)],
            15,
        )(u2, sa, sb, f1, a1, b1, u1, u0, f, *fine)
    )


def solution(mesh):
    return jax.shard_map(
        body,
        mesh=mesh,
        in_specs=(P(None, "gx", "gy"),) * 3,
        out_specs=(P(None, "gx", "gy"),) * 2,
        check_vma=False,
    )
```

```python
import functools

import jax
import jax.numpy as jnp
from jax import lax
from jax.experimental import pallas as pl
from jax.experimental.pallas import tpu as pltpu
from jax.sharding import PartitionSpec as P

F32 = jnp.float32
WEIGHTS = (0.6, 0.75, 0.9)
BOTTOM_WEIGHT = 0.8
BOTTOM = 12
YH = 20


def roll(x, shift, axis):
    shift %= x.shape[axis]
    return x if shift == 0 else pltpu.roll(x, shift, axis)


def iota(shape, axis):
    return lax.broadcasted_iota(jnp.int32, shape, axis)


def either(flag, a, b):
    return jnp.where(flag, a, b)


def only(flag, a):
    return jnp.where(flag, a, 0.0)


def matmul(a, chooser):
    total = None
    for _ in range(3):
        part = a.astype(jnp.bfloat16)
        product = jnp.dot(part, chooser, preferred_element_type=F32)
        total = product if total is None else total + product
        a = a - part.astype(F32)
    return total


def indicator(mask):
    return jnp.where(mask, 1.0, 0.0).astype(jnp.bfloat16)


def half_wrapped(i, low, high):
    return jnp.where(i < high, i // 2, jnp.where(i >= low, 64 + i // 2, -1))


class Level:
    def __init__(self, refs, factor, circular, unroll):
        self.f, self.a, self.b, self.ws, self.wl, self.wm, self.inv, self.diag, self.u, self.v = refs
        self.half = 0.5 * factor
        self.circular = circular
        self.planes, self.rows, self.lanes = self.f.shape
        self.unroll = unroll

    def build(self, weight=None):
        shape = (self.rows, self.lanes)
        sub = iota(shape, 0)
        half = self.half
        self.u[self.planes] = jnp.zeros(shape, F32)
        self.v[self.planes] = jnp.zeros(shape, F32)

        def step(m, carry):
            before, b = carry
            after = self.b[m + 1]
            wl = half * (b + roll(b, -1, 1))
            beside = roll(b, -1, 0)
            if not self.circular:
                beside = only(sub < self.rows - 1, beside)
            ws = half * (b + beside)
            wm = half * (b + after)
            below = roll(ws, 1, 0)
            if not self.circular:
                below = jnp.where(sub == 0, half * b, below)
            diag = self.a[m] + (wl + roll(wl, 1, 1) + ws + below + wm + before)
            inv = jnp.where(b > 0.0, 1.0 / diag, 0.0)
            self.ws[m] = ws if self.circular else only(sub < self.rows - 1, ws)
            self.wl[m] = wl
            self.wm[m] = wm
            self.diag[m] = diag
            self.inv[m] = inv
            if weight is not None:
                self.u[m] = (weight * self.f[m]) * inv
            return wm, after

        first = self.b[0]
        lax.fori_loop(0, self.planes, step, (half * first, first), unroll=self.unroll)

    def beside(self, m, u, after, flow):
        wl, ws, wm = self.wl[m], self.ws[m], self.wm[m]
        along = wl * roll(u, -1, 1) + roll(wl * u, 1, 1)
        across = ws * roll(u, -1, 0) + roll(ws * u, 1, 0)
        return self.f[m] + (along + across + (wm * after + flow)), wm * u

    def sweep(self, weight, src, dst):
        def step(m, carry):
            flow, u = carry
            after = src[m + 1]
            total, flow = self.beside(m, u, after, flow)
            dst[m] = (1.0 - weight) * u + (weight * self.inv[m]) * total
            return flow, after

        first = src[0]
        lax.fori_loop(0, self.planes, step, (jnp.zeros_like(first), first), unroll=self.unroll)

    def sweeps_down(self):
        self.sweep(WEIGHTS[1], self.u, self.v)
        self.sweep(WEIGHTS[2], self.v, self.u)

    def sweeps_up(self):
        self.sweep(WEIGHTS[0], self.u, self.v)
        self.sweep(WEIGHTS[1], self.v, self.u)
        self.sweep(WEIGHTS[2], self.u, self.v)

    def residual_pairs(self, src, dst, rows):
        def step(m, carry):
            flow, u = carry
            total = None
            for k in (2 * m, 2 * m + 1):
                after = src[k + 1]
                part, flow = self.beside(k, u, after, flow)
                part = (part - self.diag[k] * u)[:rows]
                total = part if total is None else total + part
                u = after
            dst[m] = total
            return flow, u

        first = src[0]
        lax.fori_loop(0, self.planes // 2, step, (jnp.zeros_like(first), first), unroll=max(self.unroll // 2, 1))

    def residual(self, src, dst, rows, lanes):
        def step(m, carry):
            flow, u = carry
            after = src[m + 1]
            part, flow = self.beside(m, u, after, flow)
            dst[m] = (part - self.diag[m] * u)[:rows, :lanes]
            return flow, after

        first = src[0]
        lax.fori_loop(0, self.planes, step, (jnp.zeros_like(first), first), unroll=self.unroll)


def sum_planes(src, dst, rows):
    def step(m, carry):
        dst[m] = src[2 * m][:rows] + src[2 * m + 1][:rows]
        return carry

    lax.fori_loop(0, dst.shape[0], step, 0, unroll=8)


def places():
    ix, iy = lax.axis_index("gx"), lax.axis_index("gy")
    nx, ny = lax.axis_size("gx"), lax.axis_size("gy")
    return ix, iy, ix % 2 == 0, iy % 2 == 0, ix < nx - 1, ix > 0, iy < ny - 1, iy > 0


def pieces(plane):
    for tile in range(3):
        first = 3 * plane - 8 * tile
        if -3 < first < 8:
            yield tile, first, (max(first, 0) - first, min(first + 3, 8) - first)


def pack_three(read, low_row, high_row, write):
    sub = iota((8, 128), 0)
    low = [jnp.zeros((8, 128), F32)] * 3
    high = [jnp.zeros((8, 128), F32)] * 3
    for plane in range(8):
        rows = read(plane)
        for tile, first, _ in pieces(plane):
            here = (sub >= first) & (sub < first + 3)
            low[tile] = jnp.where(here, roll(rows, first - low_row, 0), low[tile])
            high[tile] = jnp.where(here, roll(rows, first - high_row, 0), high[tile])
    for tile in range(3):
        write(tile, low[tile], high[tile])


def unpack_three(plane, into, tile_of, row):
    sub = iota((8, 128), 0)
    for tile, first, (low, high) in pieces(plane):
        here = (sub >= row + low) & (sub < row + high)
        into = jnp.where(here, roll(tile_of(tile), row - first, 0), into)
    return into


def pack_kernel(field, *refs):
    own, *refs = refs
    before, (xa, xb, ya, yb) = refs[:-4], refs[-4:]
    ix, iy, even_x, even_y, *_ = places()
    lane, sub = iota((8, 128), 1), iota((8, 128), 0)

    def y_step(z, carry):
        parts = []
        for shift in (0, YH):
            first = roll(own[z], shift + YH * field, 1)
            second = roll(own[z + 32], shift + YH * field + 64, 1)
            parts.append(jnp.where(lane < 64, first, second))
        low, high = parts
        here = (lane % 64 >= YH * field) & (lane % 64 < YH * (field + 1))
        for out, value, old in ((ya, either(even_y, high, low), 2), (yb, either(even_y, low, high), 3)):
            out[z] = jnp.where(here, value, before[old][z]) if before else only(here, value)
        return carry

    lax.fori_loop(0, 32, y_step, 0, unroll=8)

    def x_step(q, carry):
        extra_low = extra_high = jnp.zeros((8, 128), F32)
        for j in range(4):
            z = 4 * q + j
            value = own[z]
            low, high = roll(value, 3 * field, 0), roll(value, (3, 6, 2)[field], 0)
            for out, chosen, old in ((xa, either(even_x, high, low), 0), (xb, either(even_x, low, high), 1)):
                out[z] = jnp.where(sub < 3 * field, before[old][z], chosen) if before else chosen
            if field == 2:
                here = sub // 2 == j
                extra_low = jnp.where(here, roll(value, 2 * j - 2, 0), extra_low)
                extra_high = jnp.where(here, roll(value, 2 * j - 6, 0), extra_high)
        if field == 2:
            xa[64 + q] = either(even_x, extra_high, extra_low)
            xb[64 + q] = either(even_x, extra_low, extra_high)
        return carry

    lax.fori_loop(0, 16, x_step, 0, unroll=4)


def corner_kernel(ya, yb, ca, cb):
    ix, iy, even_x, even_y, *_ = places()
    sub = iota((8, 128), 0)

    def step(z, carry):
        right, left = either(even_y, ya[z], yb[z]), either(even_y, yb[z], ya[z])
        low = jnp.where(sub < 4, left, roll(right, 4, 0))
        high = jnp.where(sub < 4, roll(left, 4, 0), right)
        ca[z] = either(even_x, high, low)
        cb[z] = either(even_x, low, high)
        return carry

    lax.fori_loop(0, 32, step, 0, unroll=4)


class Rows:
    def __init__(self, top, bottom):
        self.top, self.bottom = top, bottom
        self.shape = (top.shape[0], 16, top.shape[2])

    def __getitem__(self, m):
        return jnp.concatenate([self.top[m], self.bottom[m]], 0)


def spread_columns(lane, high, low, at):
    return jnp.where(lane < YH, roll(high, -at, 1), only(lane >= 128 - YH, roll(low, 128 - YH - at, 1)))


def coarse_fine(pairs, wide):
    half = indicator(iota((256, 128), 0) // 2 == iota((256, 128), 1))
    wide[...] = matmul(pairs[...].reshape(256, 256), half)
    return 0.125 * (wide[pl.ds(0, 128, stride=2), :] + wide[pl.ds(1, 128, stride=2), :])


def own_rows_kernel(f, a, b, ya, yb, fx, ax, bx, ab, packed, pairs, wide):
    ix, iy, even_x, even_y, has_right, has_left, has_above, has_below = places()
    lane = iota((8, 128), 1)

    def unpack(z, carry):
        up = only(has_above, either(even_y, ya[z], yb[z]))
        down = only(has_below, either(even_y, yb[z], ya[z]))
        for n, (own, full) in enumerate(((f, fx), (a, ax), (b, bx))):
            for h in range(2):
                full[z + 32 * h, :, 0:128] = own[z + 32 * h]
                full[z + 32 * h, :, 128:256] = spread_columns(lane, up, down, 64 * h + YH * n)
        return carry

    lax.fori_loop(0, 32, unpack, 0, unroll=8)
    bx[64] = jnp.zeros((8, 256), F32)
    sum_planes(ax, pairs, 8)
    ab[0:16] = coarse_fine(pairs, wide).reshape(16, 8, 128)
    sum_planes(bx, pairs, 8)
    ab[16:32] = coarse_fine(pairs, wide).reshape(16, 8, 128)
    for t in range(16):
        packed[t] = jnp.where(lane < 64, ab[t], roll(ab[16 + t], 64, 1))
    for t in range(4):
        packed[16 + t] = halo_lanes([ab[t + 4 * q + 16 * n] for q in range(4) for n in range(2)])


def halo_lanes(parts):
    lane = iota((8, 128), 1)
    packed = jnp.zeros((8, 128), F32)
    for n, part in enumerate(parts):
        pair = jnp.where(lane < 16 * n + 8, roll(part, 16 * n - 64, 1), roll(part, 16 * n + 8 - 120, 1))
        packed = jnp.where(lane // 16 == n, pair, packed)
    return packed


def with_halo_lanes(own, packed, n):
    lane = iota((8, 128), 1)
    right, left = roll(packed, 64 - 16 * n, 1), roll(packed, 112 - 16 * n, 1)
    return jnp.where(lane < 64, own, jnp.where(lane < 72, right, only(lane >= 120, left)))


def fine_down_kernel(
    f, a, b, xa, xb, ca, cb,
    source, packed, u, fx, ws, wl, wm, inv, diag,
    ax, bx, v, pairs, wide,
):
    ix, iy, even_x, even_y, has_right, has_left, has_above, has_below = places()
    lane, sub = iota((8, 128), 1), iota((8, 128), 0)

    def unpack(q, carry):
        for j in range(4):
            zz = 4 * q + j
            corner_r = only(has_right, either(even_x, ca[zz], cb[zz]))
            corner_l = only(has_left, either(even_x, cb[zz], ca[zz]))
            up = only(has_above, jnp.where(sub < 4, roll(corner_r, 4, 0), corner_l))
            down = only(has_below, jnp.where(sub < 4, corner_r, roll(corner_l, 4, 0)))
            for h in range(2):
                z, e = zz + 32 * h, 64 + q + 8 * h
                main_r = only(has_right, either(even_x, xa[z], xb[z]))
                main_l = only(has_left, either(even_x, xb[z], xa[z]))
                extra_r = only(has_right, either(even_x, xa[e], xb[e]))
                extra_l = only(has_left, either(even_x, xb[e], xa[e]))
                beside = (
                    jnp.where(sub < 3, main_r, only(sub >= 5, roll(main_l, 5, 0))),
                    jnp.where(sub < 3, roll(main_r, -3, 0), only(sub >= 5, roll(main_l, 2, 0))),
                    jnp.where(
                        sub < 2,
                        roll(main_r, 2, 0),
                        jnp.where(
                            sub < 4,
                            roll(extra_r, 2 - 2 * j, 0),
                            jnp.where(sub < 6, roll(main_l, 6, 0), roll(extra_l, 6 - 2 * j, 0)),
                        ),
                    ),
                )
                for n, full in enumerate((fx, ax, bx)):
                    full[z, :, 0:128] = beside[n]
                    full[z, :, 128:256] = spread_columns(lane, up, down, 64 * h + YH * n)
        return carry

    lax.fori_loop(0, 8, unpack, 0, unroll=4)
    bx[64] = jnp.zeros((8, 256), F32)
    level = Level((Rows(f, fx), Rows(a, ax), Rows(b, bx), ws, wl, wm, inv, diag, u, v), 1.0, True, 16)
    level.build(WEIGHTS[0])
    level.sweeps_down()
    level.residual_pairs(u, pairs, 8)
    source[...] = coarse_fine(pairs, wide).reshape(16, 8, 128)
    for t in range(8):
        packed[t] = jnp.where(lane < 64, source[t], roll(source[t + 8], 64, 1))
    for t in range(2):
        packed[8 + t] = halo_lanes([source[t + 2 * q] for q in range(8)])


def u_edges_kernel(u, ra, rb):
    ix, iy, even_x, even_y, *_ = places()
    lane, sub = iota((8, 128), 1), iota((8, 128), 0)

    def put(at, low, high):
        ra[at] = either(even_x, high, low)
        rb[at] = either(even_x, low, high)

    def main(g, carry):
        pack_three(
            lambda z: u[8 * g + z, 0:8, 0:128], 1, 4, lambda tile, low, high: put(3 * g + tile, low, high)
        )
        return carry

    lax.fori_loop(0, 8, main, 0, unroll=2)
    for t in range(2):
        low = high = jnp.zeros((8, 128), F32)
        for g in range(2):
            for k in range(16):
                edge = u[16 * (2 * t + g) + k, 0:8, 128:256]
                edge = roll(jnp.where(lane < 4, edge, roll(edge, 8, 1)), 8 * k, 1)
                here = (lane // 8 == k) & (sub // 4 == g)
                turned = roll(edge, 4, 0)
                low = jnp.where(here, turned if g else edge, low)
                high = jnp.where(here, edge if g else turned, high)
        put(24 + t, low, high)


def middle_down_kernel(
    source_in, ga, gb, ab, aba, abb, _a, _b,
    copies, f1, a1, b, u,
    ws, wl, wm, inv, diag, v, pairs, wide,
):
    ix, iy, even_x, even_y, has_right, has_left, has_above, has_below = places()
    sub = iota((8, 128), 0)

    def right(one, two, at):
        return only(has_right, either(even_x, one[at], two[at]))

    def left(one, two, at):
        return only(has_left, either(even_x, two[at], one[at]))

    for t in range(16):
        sides = []
        for side in (right, left):
            f = side(ga, gb, t % 8)
            f = with_halo_lanes(roll(f, 64, 1) if t >= 8 else f, side(ga, gb, 8 + t % 2), t // 2)
            both, halo = side(aba, abb, t), side(aba, abb, 16 + t % 4)
            sides.append(
                (f, with_halo_lanes(both, halo, t // 4 * 2), with_halo_lanes(roll(both, 64, 1), halo, t // 4 * 2 + 1))
            )
        for n, (own, full) in enumerate(((source_in[t], f1), (ab[t], a1), (ab[16 + t], b))):
            high, low = sides[0][n], sides[1][n]
            full[2 * t, 0:8] = jnp.where(sub < 4, own, roll(high, 4, 0))
            full[2 * t, 8:16] = only(sub >= 4, roll(low, 4, 0))
            full[2 * t + 1, 0:8] = jnp.where(sub < 4, roll(own, 4, 0), high)
            full[2 * t + 1, 8:16] = only(sub >= 4, low)

    b[32] = jnp.zeros((16, 128), F32)
    level = Level((f1, a1, b, ws, wl, wm, inv, diag, u, v), 0.25, True, 16)
    level.build(WEIGHTS[0])
    level.sweeps_down()

    lanes_in, lanes_out = iota((128, 128), 0), iota((128, 128), 1)
    half = indicator((lanes_in // 2 == lanes_out) & (lanes_out < 32))

    def coarse():
        wide[...] = matmul(pairs[...].reshape(128, 128), half)
        rows = [wide[pl.ds(k, 16, stride=8), :] for k in range(4)]
        return 0.125 * (rows[0] + rows[1]), 0.125 * (rows[2] + rows[3])

    sum_planes(a1, pairs, 8)
    alpha = coarse()
    sum_planes(b, pairs, 8)
    beta = coarse()
    level.residual_pairs(u, pairs, 8)
    source = coarse()
    blocks = []
    for k in range(2):
        blocks.append(source[k] + roll(alpha[k], 32, 1) + roll(beta[k], 64, 1))
    parts = [blocks[0][:8], blocks[0][8:], blocks[1][:8]]
    last = blocks[1][8:]
    lane = iota((8, 128), 1)
    for n, part in enumerate(parts):
        part = jnp.where(lane < 96, part, roll(last, 96 - 32 * n, 1))
        for d in range(8):
            copies[3 * d + n] = part


def edges_kernel(_, ra, rb, b, u, sa, sb):
    ix, iy, even_x, even_y, *_ = places()
    lane, sub = iota((8, 128), 1), iota((8, 128), 0)
    sa[0:26] = ra[...]
    sb[0:26] = rb[...]
    high, low = [], []
    for z in range(32):
        mine, far = u[z, 0:8], u[z, 8:16]
        turned = roll(mine, 4, 0)
        high.append(
            jnp.where(sub >= 4, turned, jnp.where(sub == 3, roll(far, 4, 0), roll(b[z, 8:16], 1, 0)))
        )
        low.append(jnp.where(sub == 1, roll(b[z, 0:8], 5, 0), turned))

    def packed(parts, t):
        if t < 16:
            return jnp.where(lane < 64, parts[t], roll(parts[t + 16], 64, 1))
        return halo_lanes([parts[t - 16 + 4 * q] for q in range(8)])

    for t in range(20):
        h, l = packed(high, t), packed(low, t)
        sa[26 + t] = either(even_x, h, l)
        sb[26 + t] = either(even_x, l, h)


def bottom_kernel(
    own, ya, yb,
    out,
    f2, a2, b2, ws2, wl2, wm2, inv2, diag2, u2, v2,
    f3, a3, b3, ws3, wl3, wm3, inv3, diag3, u3, v3,
    pairs, wide,
):
    ix, iy, even_x, even_y, has_right, has_left, has_above, has_below = places()
    lane, sub = iota((8, 128), 1), iota((8, 128), 0)

    high, middle, low = lane < 64, lane < 32, lane >= 96
    for d in range(8):
        tiles = []
        for t in range(3):
            one, two = ya[3 * d + t], yb[3 * d + t]
            tiles.append(
                (own[3 * d + t], only(has_above, either(even_y, one, two)), only(has_below, either(even_y, two, one)))
            )
        for n, full in enumerate((f2, a2, b2)):
            for t in range(4):
                mine, up, down = tiles[n if t == 3 else t]
                at = 96 if t == 3 else 32 * n
                beside = jnp.where(high, roll(up, 32 - at, 1), only(low, roll(down, 96 - at, 1)))
                full[2 * d + t // 2, 8 * (t % 2) : 8 * (t % 2) + 8] = jnp.where(middle, roll(mine, -at, 1), beside)
    b2[16] = jnp.zeros((16, 128), F32)
    b3[8] = jnp.zeros((8, 128), F32)
    level2 = Level((f2, a2, b2, ws2, wl2, wm2, inv2, diag2, u2, v2), 0.0625, False, 16)
    level2.build(WEIGHTS[0])
    level2.sweeps_down()

    lanes_in, lanes_out = iota((128, 128), 0), iota((128, 128), 1)
    half = indicator(half_wrapped(lanes_in, 96, 64) == lanes_out)
    twice = indicator(lanes_in == half_wrapped(lanes_out, 96, 64))

    def coarse():
        wide[0:128, :] = matmul(pairs[...].reshape(128, 128), half)
        halves = wide[pl.ds(0, 64, stride=2), :] + wide[pl.ds(1, 64, stride=2), :]
        return (0.125 * halves).reshape(8, 8, 128)

    sum_planes(a2, pairs, 16)
    a3[...] = coarse()
    sum_planes(b2, pairs, 16)
    b3[0:8] = coarse()
    level2.residual_pairs(u2, pairs, 16)
    f3[...] = coarse()
    level3 = Level((f3, a3, b3, ws3, wl3, wm3, inv3, diag3, u3, v3), 0.015625, False, 8)
    level3.build(BOTTOM_WEIGHT)

    def two_sweeps(_, carry):
        level3.sweep(BOTTOM_WEIGHT, u3, v3)
        level3.sweep(BOTTOM_WEIGHT, v3, u3)
        return carry

    lax.fori_loop(0, (BOTTOM - 2) // 2, two_sweeps, 0)
    level3.sweep(BOTTOM_WEIGHT, u3, v3)

    fine = matmul(v3[0:8].reshape(64, 128), twice)
    wide[pl.ds(0, 64, stride=2), :] = fine
    wide[pl.ds(1, 64, stride=2), :] = fine
    for x in range(16):
        u2[x] = u2[x] + only(inv2[x] > 0.0, wide[16 * (x // 2) : 16 * (x // 2) + 16, :])
    level2.sweeps_up()
    out[...] = v2[0:16]


def ready_kernel(xa, xb, own_u, u0):
    ix, iy, even_x, even_y, has_right, has_left, has_above, has_below = places()
    lane, sub = iota((8, 128), 1), iota((8, 128), 0)

    for z in range(64):
        u0[z, 0:8, :] = own_u[z, 0:8, :]
        far, at = own_u[z, 8:16, 0:128], 3 * (z // 8)
        far = unpack_three(z % 8, far, lambda t: only(has_right, either(even_x, xa[at + t], xb[at + t])), 1)
        far = unpack_three(z % 8, far, lambda t: only(has_left, either(even_x, xb[at + t], xa[at + t])), 4)
        u0[z, 8:16, 0:128] = far
        g, k = z // 16, z % 16
        t, e = 24 + g // 2, g % 2
        right = only(has_right, either(even_x, xa[t], xb[t]))
        left = only(has_left, either(even_x, xb[t], xa[t]))
        edge = jnp.where(sub < 4, roll(right, 4, 0) if e else right, left if e else roll(left, 4, 0))
        u0[z, 8:16, 128:256] = jnp.where(
            lane < 4, roll(edge, -8 * k, 1), only(lane >= 124, roll(edge, 120 - 8 * k, 1))
        )
    u0[64] = jnp.zeros((16, 256), F32)


def up_kernel(
    v2, xa, xb, f1, a1, b1, u1, u0_in, f0, f0x, ws0, wl0, wm0, inv0, diag0,
    field_out, residual_out,
    u0, v0, bx1, ws1, wl1, wm1, inv1, diag1, ux1, v1, spread,
):
    ix, iy, even_x, even_y, has_right, has_left, has_above, has_below = places()
    sub = iota((8, 128), 0)
    lanes_in, lanes_out = iota((128, 128), 0), iota((128, 128), 1)

    def received(one, two, z):
        main = either(even_x, one[26 + z % 16], two[26 + z % 16])
        halo = either(even_x, one[42 + z % 4], two[42 + z % 4])
        return with_halo_lanes(roll(main, 64, 1) if z >= 16 else main, halo, z // 4)

    for z in range(32):
        right = only(has_right, received(xa, xb, z))
        left = only(has_left, received(xb, xa, z))
        ux1[z, 0:8] = jnp.where(sub < 4, u1[z, 0:8], right)
        ux1[z, 8:16] = jnp.where(sub == 0, right, only(sub >= 3, left))
        bx1[z, 0:8] = b1[z, 0:8]
        bx1[z, 8:16] = jnp.where(
            sub == 0, roll(right, -1, 0), jnp.where(sub == 3, roll(left, 3, 0), b1[z, 8:16])
        )
    bx1[32] = jnp.zeros((16, 128), F32)
    level1 = Level((f1, a1, bx1, ws1, wl1, wm1, inv1, diag1, ux1, v1), 0.25, True, 16)
    level1.build()
    double = indicator(lanes_in == jnp.where(lanes_out < 96, lanes_out // 2, 64 + lanes_out // 2))
    columns = [v2[jnp.clip(2 * ix + k, 0, 15)] for k in range(-3, 5)]
    fine = matmul(jnp.concatenate(columns, 0), double)
    for k in range(8):
        for e in range(2):
            for x in range(2):
                spread[pl.ds(e * 16 + (2 * (k - 3) + x) % 16, 16, stride=32), :] = fine[16 * k : 16 * k + 16]

    def correct_1(z, carry):
        rows = spread[pl.ds(pl.multiple_of(16 * z, 16), 16), :]
        ux1[z] = ux1[z] + only(inv1[z] > 0.0, rows)
        return carry

    lax.fori_loop(0, 32, correct_1, 0, unroll=8)
    level1.sweeps_up()

    for z in range(32):
        parts = v1[z, 0:8], v1[z, 8:16]
        rows = jnp.where(sub < 6, parts[0], parts[1])
        spread[pl.ds(16 * z, 8, stride=2), :] = rows
        spread[pl.ds(16 * z + 1, 8, stride=2), :] = rows
    lanes_in, lanes_out = iota((128, 256), 0), iota((128, 256), 1)
    double = indicator(lanes_in == lanes_out // 2)

    def correct_0(z, carry):
        fine = matmul(spread[pl.ds(pl.multiple_of(64 * z, 64), 64), :], double)
        for k in range(4):
            rows = fine[16 * k : 16 * k + 16]
            for e in range(2):
                m = 8 * z + 2 * k + e
                u0[m] = u0_in[m] + only(inv0[m] > 0.0, rows)
        return carry

    lax.fori_loop(0, 8, correct_0, 0, unroll=8)
    level0 = Level((Rows(f0, f0x), None, u0, ws0, wl0, wm0, inv0, diag0, u0, v0), 1.0, True, 16)
    u0[64] = jnp.zeros((16, 256), F32)
    v0[64] = jnp.zeros((16, 256), F32)
    level0.sweeps_up()
    level0.residual(v0, residual_out, 8, 128)

    def out(z, carry):
        field_out[z] = v0[z, 0:8, 0:128]
        return carry

    lax.fori_loop(0, 64, out, 0, unroll=4)


def call(kernel, outs, scratch, n_in, cost=1):
    vmem = pl.BlockSpec(memory_space=pltpu.VMEM)
    need = sum(4 * p * r * n for p, r, n in ((1,) * (3 - len(shape)) + shape for shape in scratch))
    return pl.pallas_call(
        kernel,
        out_shape=[jax.ShapeDtypeStruct(shape, F32) for shape in outs],
        in_specs=[vmem] * n_in,
        out_specs=[vmem] * len(outs),
        scratch_shapes=[pltpu.VMEM(shape, F32) for shape in scratch],
        cost_estimate=pl.CostEstimate(
            flops=cost * 1_000_000_000, bytes_accessed=cost * 3_000_000, transcendentals=0
        ),
        compiler_params=pltpu.CompilerParams(vmem_limit_bytes=need + 4 * 1024 * 1024),
    )


def swaps(axis):
    size = lax.axis_size(axis)
    first = [(i, i ^ 1) for i in range(size)]
    second = [(i, i + 1 if i % 2 else i - 1) for i in range(size)]
    second = [(i, j % size) for i, j in second]
    return first, second


def swap(a, b, axis):
    first, second = swaps(axis)
    return lax.ppermute(a, axis, first), lax.ppermute(b, axis, second)


def body(right_side, alpha, beta):
    def tiles(n):
        return (n, 8, 128)

    f, a, b = right_side, alpha, beta
    sizes = [tiles(64), tiles(64), tiles(32), tiles(32)]
    packs = call(functools.partial(pack_kernel, 0), sizes, [], 1)(f)
    packs = call(functools.partial(pack_kernel, 1), sizes, [], 5)(a, *packs)
    sizes = [tiles(80), tiles(80), tiles(32), tiles(32)]
    xa, xb, ya, yb = call(functools.partial(pack_kernel, 2), sizes, [], 5)(b, *packs)
    xa, xb = swap(xa, xb, "gx")
    ya, yb = swap(ya, yb, "gy")
    ca, cb = call(corner_kernel, [tiles(32), tiles(32)], [], 2)(ya, yb)
    ca, cb = swap(ca, cb, "gx")
    top, top_more = (64, 8, 256), (65, 8, 256)
    f, a, b, ab, packed = call(
        own_rows_kernel, [top, top, top_more, tiles(32), tiles(20)], [(32, 8, 256), (256, 128)], 5, cost=3
    )(f, a, b, ya, yb)
    aba, abb = swap(packed, packed, "gx")

    full, more = (64, 16, 256), (65, 16, 256)
    source, packed, u, *fine = call(
        fine_down_kernel,
        [tiles(16), tiles(10), more, top] + [full] * 5,
        [top, top_more, more, (32, 8, 256), (256, 128)],
        7,
        cost=50,
    )(f, a, b, xa, xb, ca, cb)
    ga, gb = swap(packed, packed, "gx")
    ra, rb = call(u_edges_kernel, [tiles(26), tiles(26)], [], 1, cost=50)(u)

    full, more = (32, 16, 128), (33, 16, 128)
    copies, f1, a1, b1, u1 = call(
        middle_down_kernel,
        [tiles(24), full, full, more, more],
        [full, full, full, full, full, more, tiles(16), (128, 128)],
        8,
        cost=50,
    )(source, ga, gb, ab, aba, abb, ra, rb)
    own = lax.all_to_all(copies, "gx", 0, 0, tiled=True)
    ya, yb = swap(own, own, "gy")
    sa, sb = call(edges_kernel, [tiles(46), tiles(46)], [], 5, cost=50)(own, ra, rb, b1, u1)
    sa, sb = swap(sa, sb, "gx")
    (u0,) = call(ready_kernel, [(65, 16, 256)], [], 3)(sa, sb, u)

    def level(planes, rows, lanes):
        one, two = (planes, rows, lanes), (planes + 1, rows, lanes)
        return [one, one, two, one, one, one, one, one, two, two]

    (u2,) = call(
        bottom_kernel,
        [(16, 16, 128)],
        level(16, 16, 128) + level(8, 8, 128) + [(8, 16, 128), (128, 128)],
        3,
        cost=50,
    )(own, ya, yb)
    return tuple(
        call(
            up_kernel,
            [tiles(64), tiles(64)],
            [(65, 16, 256)] * 2 + level(32, 16, 128)[2:] + [(512, 128)],
            15,
        )(u2, sa, sb, f1, a1, b1, u1, u0, f, *fine)
    )


def solution(mesh):
    return jax.shard_map(
        body,
        mesh=mesh,
        in_specs=(P(None, "gx", "gy"),) * 3,
        out_specs=(P(None, "gx", "gy"),) * 2,
        check_vma=False,
    )
```

```python
import functools

import jax
import jax.numpy as jnp
from jax import lax
from jax.experimental import pallas as pl
from jax.experimental.pallas import tpu as pltpu
from jax.sharding import PartitionSpec as P

F32 = jnp.float32
WEIGHTS = (0.6, 0.75, 0.9)
BOTTOM_WEIGHT = 0.8
BOTTOM = 12
YH = 20


def roll(x, shift, axis):
    shift %= x.shape[axis]
    return x if shift == 0 else pltpu.roll(x, shift, axis)


def iota(shape, axis):
    return lax.broadcasted_iota(jnp.int32, shape, axis)


def either(flag, a, b):
    return jnp.where(flag, a, b)


def only(flag, a):
    return jnp.where(flag, a, 0.0)


def matmul(a, chooser):
    total = None
    for _ in range(3):
        part = a.astype(jnp.bfloat16)
        product = jnp.dot(part, chooser, preferred_element_type=F32)
        total = product if total is None else total + product
        a = a - part.astype(F32)
    return total


def indicator(mask):
    return jnp.where(mask, 1.0, 0.0).astype(jnp.bfloat16)


def half_wrapped(i, low, high):
    return jnp.where(i < high, i // 2, jnp.where(i >= low, 64 + i // 2, -1))


class Level:
    def __init__(self, refs, factor, circular, unroll):
        self.f, self.a, self.b, self.ws, self.wl, self.wm, self.inv, self.diag, self.u, self.v = refs
        self.half = 0.5 * factor
        self.circular = circular
        self.planes, self.rows, self.lanes = self.f.shape
        self.unroll = unroll

    def build(self, weight=None):
        shape = (self.rows, self.lanes)
        sub = iota(shape, 0)
        half = self.half
        self.u[self.planes] = jnp.zeros(shape, F32)
        self.v[self.planes] = jnp.zeros(shape, F32)

        def step(m, carry):
            before, b = carry
            after = self.b[m + 1]
            wl = half * (b + roll(b, -1, 1))
            beside = roll(b, -1, 0)
            if not self.circular:
                beside = only(sub < self.rows - 1, beside)
            ws = half * (b + beside)
            wm = half * (b + after)
            below = roll(ws, 1, 0)
            if not self.circular:
                below = jnp.where(sub == 0, half * b, below)
            diag = self.a[m] + (wl + roll(wl, 1, 1) + ws + below + wm + before)
            inv = jnp.where(b > 0.0, 1.0 / diag, 0.0)
            self.ws[m] = ws if self.circular else only(sub < self.rows - 1, ws)
            self.wl[m] = wl
            self.wm[m] = wm
            self.diag[m] = diag
            self.inv[m] = inv
            if weight is not None:
                self.u[m] = (weight * self.f[m]) * inv
            return wm, after

        first = self.b[0]
        lax.fori_loop(0, self.planes, step, (half * first, first), unroll=self.unroll)

    def beside(self, m, u, after, flow):
        wl, ws, wm = self.wl[m], self.ws[m], self.wm[m]
        along = wl * roll(u, -1, 1) + roll(wl * u, 1, 1)
        across = ws * roll(u, -1, 0) + roll(ws * u, 1, 0)
        return self.f[m] + (along + across + (wm * after + flow)), wm * u

    def sweep(self, weight, src, dst):
        def step(m, carry):
            flow, u = carry
            after = src[m + 1]
            total, flow = self.beside(m, u, after, flow)
            dst[m] = (1.0 - weight) * u + (weight * self.inv[m]) * total
            return flow, after

        first = src[0]
        lax.fori_loop(0, self.planes, step, (jnp.zeros_like(first), first), unroll=self.unroll)

    def sweeps_down(self):
        self.sweep(WEIGHTS[1], self.u, self.v)
        self.sweep(WEIGHTS[2], self.v, self.u)

    def sweeps_up(self):
        self.sweep(WEIGHTS[0], self.u, self.v)
        self.sweep(WEIGHTS[1], self.v, self.u)
        self.sweep(WEIGHTS[2], self.u, self.v)

    def residual_pairs(self, src, dst, rows):
        def step(m, carry):
            flow, u = carry
            total = None
            for k in (2 * m, 2 * m + 1):
                after = src[k + 1]
                part, flow = self.beside(k, u, after, flow)
                part = (part - self.diag[k] * u)[:rows]
                total = part if total is None else total + part
                u = after
            dst[m] = total
            return flow, u

        first = src[0]
        lax.fori_loop(0, self.planes // 2, step, (jnp.zeros_like(first), first), unroll=max(self.unroll // 2, 1))

    def residual(self, src, dst, rows, lanes):
        def step(m, carry):
            flow, u = carry
            after = src[m + 1]
            part, flow = self.beside(m, u, after, flow)
            dst[m] = (part - self.diag[m] * u)[:rows, :lanes]
            return flow, after

        first = src[0]
        lax.fori_loop(0, self.planes, step, (jnp.zeros_like(first), first), unroll=self.unroll)


def sum_planes(src, dst, rows):
    def step(m, carry):
        dst[m] = src[2 * m][:rows] + src[2 * m + 1][:rows]
        return carry

    lax.fori_loop(0, dst.shape[0], step, 0, unroll=8)


def places():
    ix, iy = lax.axis_index("gx"), lax.axis_index("gy")
    nx, ny = lax.axis_size("gx"), lax.axis_size("gy")
    return ix, iy, ix % 2 == 0, iy % 2 == 0, ix < nx - 1, ix > 0, iy < ny - 1, iy > 0


def pieces(plane):
    for tile in range(3):
        first = 3 * plane - 8 * tile
        if -3 < first < 8:
            yield tile, first, (max(first, 0) - first, min(first + 3, 8) - first)


def pack_three(read, low_row, high_row, write):
    sub = iota((8, 128), 0)
    low = [jnp.zeros((8, 128), F32)] * 3
    high = [jnp.zeros((8, 128), F32)] * 3
    for plane in range(8):
        rows = read(plane)
        for tile, first, _ in pieces(plane):
            here = (sub >= first) & (sub < first + 3)
            low[tile] = jnp.where(here, roll(rows, first - low_row, 0), low[tile])
            high[tile] = jnp.where(here, roll(rows, first - high_row, 0), high[tile])
    for tile in range(3):
        write(tile, low[tile], high[tile])


def unpack_three(plane, into, tile_of, row):
    sub = iota((8, 128), 0)
    for tile, first, (low, high) in pieces(plane):
        here = (sub >= row + low) & (sub < row + high)
        into = jnp.where(here, roll(tile_of(tile), row - first, 0), into)
    return into


def pack_kernel(field, *refs):
    own, *refs = refs
    before, (xa, xb, ya, yb) = refs[:-4], refs[-4:]
    ix, iy, even_x, even_y, *_ = places()
    lane, sub = iota((8, 128), 1), iota((8, 128), 0)

    def y_step(z, carry):
        parts = []
        for shift in (0, YH):
            first = roll(own[z], shift + YH * field, 1)
            second = roll(own[z + 32], shift + YH * field + 64, 1)
            parts.append(jnp.where(lane < 64, first, second))
        low, high = parts
        here = (lane % 64 >= YH * field) & (lane % 64 < YH * (field + 1))
        for out, value, old in ((ya, either(even_y, high, low), 2), (yb, either(even_y, low, high), 3)):
            out[z] = jnp.where(here, value, before[old][z]) if before else only(here, value)
        return carry

    lax.fori_loop(0, 32, y_step, 0, unroll=16)

    def x_step(q, carry):
        extra_low = extra_high = jnp.zeros((8, 128), F32)
        for j in range(4):
            z = 4 * q + j
            value = own[z]
            low, high = roll(value, 3 * field, 0), roll(value, (3, 6, 2)[field], 0)
            for out, chosen, old in ((xa, either(even_x, high, low), 0), (xb, either(even_x, low, high), 1)):
                out[z] = jnp.where(sub < 3 * field, before[old][z], chosen) if before else chosen
            if field == 2:
                here = sub // 2 == j
                extra_low = jnp.where(here, roll(value, 2 * j - 2, 0), extra_low)
                extra_high = jnp.where(here, roll(value, 2 * j - 6, 0), extra_high)
        if field == 2:
            xa[64 + q] = either(even_x, extra_high, extra_low)
            xb[64 + q] = either(even_x, extra_low, extra_high)
        return carry

    lax.fori_loop(0, 16, x_step, 0, unroll=8)


def corner_kernel(ya, yb, ca, cb):
    ix, iy, even_x, even_y, *_ = places()
    sub = iota((8, 128), 0)

    def step(z, carry):
        right, left = either(even_y, ya[z], yb[z]), either(even_y, yb[z], ya[z])
        low = jnp.where(sub < 4, left, roll(right, 4, 0))
        high = jnp.where(sub < 4, roll(left, 4, 0), right)
        ca[z] = either(even_x, high, low)
        cb[z] = either(even_x, low, high)
        return carry

    lax.fori_loop(0, 32, step, 0, unroll=4)


class Rows:
    def __init__(self, top, bottom):
        self.top, self.bottom = top, bottom
        self.shape = (top.shape[0], 16, top.shape[2])

    def __getitem__(self, m):
        return jnp.concatenate([self.top[m], self.bottom[m]], 0)


def spread_columns(lane, high, low, at):
    return jnp.where(lane < YH, roll(high, -at, 1), only(lane >= 128 - YH, roll(low, 128 - YH - at, 1)))


def coarse_fine(pairs, wide):
    half = indicator(iota((256, 128), 0) // 2 == iota((256, 128), 1))
    wide[...] = matmul(pairs[...].reshape(256, 256), half)
    return 0.125 * (wide[pl.ds(0, 128, stride=2), :] + wide[pl.ds(1, 128, stride=2), :])


def own_rows_kernel(f, a, b, ya, yb, fx, ax, bx, ab, packed, pairs, wide):
    ix, iy, even_x, even_y, has_right, has_left, has_above, has_below = places()
    lane = iota((8, 128), 1)

    def unpack(z, carry):
        up = only(has_above, either(even_y, ya[z], yb[z]))
        down = only(has_below, either(even_y, yb[z], ya[z]))
        for n, (own, full) in enumerate(((f, fx), (a, ax), (b, bx))):
            for h in range(2):
                full[z + 32 * h, :, 0:128] = own[z + 32 * h]
                full[z + 32 * h, :, 128:256] = spread_columns(lane, up, down, 64 * h + YH * n)
        return carry

    lax.fori_loop(0, 32, unpack, 0, unroll=8)
    bx[64] = jnp.zeros((8, 256), F32)
    sum_planes(ax, pairs, 8)
    ab[0:16] = coarse_fine(pairs, wide).reshape(16, 8, 128)
    sum_planes(bx, pairs, 8)
    ab[16:32] = coarse_fine(pairs, wide).reshape(16, 8, 128)
    for t in range(16):
        packed[t] = jnp.where(lane < 64, ab[t], roll(ab[16 + t], 64, 1))
    for t in range(4):
        packed[16 + t] = halo_lanes([ab[t + 4 * q + 16 * n] for q in range(4) for n in range(2)])


def halo_lanes(parts):
    lane = iota((8, 128), 1)
    packed = jnp.zeros((8, 128), F32)
    for n, part in enumerate(parts):
        pair = jnp.where(lane < 16 * n + 8, roll(part, 16 * n - 64, 1), roll(part, 16 * n + 8 - 120, 1))
        packed = jnp.where(lane // 16 == n, pair, packed)
    return packed


def with_halo_lanes(own, packed, n):
    lane = iota((8, 128), 1)
    right, left = roll(packed, 64 - 16 * n, 1), roll(packed, 112 - 16 * n, 1)
    return jnp.where(lane < 64, own, jnp.where(lane < 72, right, only(lane >= 120, left)))


def fine_down_kernel(
    f, a, b, xa, xb, ca, cb,
    source, packed, u, fx, ws, wl, wm, inv, diag,
    ax, bx, v, pairs, wide,
):
    ix, iy, even_x, even_y, has_right, has_left, has_above, has_below = places()
    lane, sub = iota((8, 128), 1), iota((8, 128), 0)

    def unpack(q, carry):
        for j in range(4):
            zz = 4 * q + j
            corner_r = only(has_right, either(even_x, ca[zz], cb[zz]))
            corner_l = only(has_left, either(even_x, cb[zz], ca[zz]))
            up = only(has_above, jnp.where(sub < 4, roll(corner_r, 4, 0), corner_l))
            down = only(has_below, jnp.where(sub < 4, corner_r, roll(corner_l, 4, 0)))
            for h in range(2):
                z, e = zz + 32 * h, 64 + q + 8 * h
                main_r = only(has_right, either(even_x, xa[z], xb[z]))
                main_l = only(has_left, either(even_x, xb[z], xa[z]))
                extra_r = only(has_right, either(even_x, xa[e], xb[e]))
                extra_l = only(has_left, either(even_x, xb[e], xa[e]))
                beside = (
                    jnp.where(sub < 3, main_r, only(sub >= 5, roll(main_l, 5, 0))),
                    jnp.where(sub < 3, roll(main_r, -3, 0), only(sub >= 5, roll(main_l, 2, 0))),
                    jnp.where(
                        sub < 2,
                        roll(main_r, 2, 0),
                        jnp.where(
                            sub < 4,
                            roll(extra_r, 2 - 2 * j, 0),
                            jnp.where(sub < 6, roll(main_l, 6, 0), roll(extra_l, 6 - 2 * j, 0)),
                        ),
                    ),
                )
                for n, full in enumerate((fx, ax, bx)):
                    full[z, :, 0:128] = beside[n]
                    full[z, :, 128:256] = spread_columns(lane, up, down, 64 * h + YH * n)
        return carry

    lax.fori_loop(0, 8, unpack, 0, unroll=4)
    bx[64] = jnp.zeros((8, 256), F32)
    level = Level((Rows(f, fx), Rows(a, ax), Rows(b, bx), ws, wl, wm, inv, diag, u, v), 1.0, True, 16)
    level.build(WEIGHTS[0])
    level.sweeps_down()
    level.residual_pairs(u, pairs, 8)
    source[...] = coarse_fine(pairs, wide).reshape(16, 8, 128)
    for t in range(8):
        packed[t] = jnp.where(lane < 64, source[t], roll(source[t + 8], 64, 1))
    for t in range(2):
        packed[8 + t] = halo_lanes([source[t + 2 * q] for q in range(8)])


def u_edges_kernel(u, ra, rb):
    ix, iy, even_x, even_y, *_ = places()
    lane, sub = iota((8, 128), 1), iota((8, 128), 0)

    def put(at, low, high):
        ra[at] = either(even_x, high, low)
        rb[at] = either(even_x, low, high)

    def main(g, carry):
        pack_three(
            lambda z: u[8 * g + z, 0:8, 0:128], 1, 4, lambda tile, low, high: put(3 * g + tile, low, high)
        )
        return carry

    lax.fori_loop(0, 8, main, 0, unroll=2)
    for t in range(2):
        low = high = jnp.zeros((8, 128), F32)
        for g in range(2):
            for k in range(16):
                edge = u[16 * (2 * t + g) + k, 0:8, 128:256]
                edge = roll(jnp.where(lane < 4, edge, roll(edge, 8, 1)), 8 * k, 1)
                here = (lane // 8 == k) & (sub // 4 == g)
                turned = roll(edge, 4, 0)
                low = jnp.where(here, turned if g else edge, low)
                high = jnp.where(here, edge if g else turned, high)
        put(24 + t, low, high)


def middle_down_kernel(
    source_in, ga, gb, ab, aba, abb, _a, _b,
    copies, f1, a1, b, u,
    ws, wl, wm, inv, diag, v, pairs, wide,
):
    ix, iy, even_x, even_y, has_right, has_left, has_above, has_below = places()
    sub = iota((8, 128), 0)

    def right(one, two, at):
        return only(has_right, either(even_x, one[at], two[at]))

    def left(one, two, at):
        return only(has_left, either(even_x, two[at], one[at]))

    for t in range(16):
        sides = []
        for side in (right, left):
            f = side(ga, gb, t % 8)
            f = with_halo_lanes(roll(f, 64, 1) if t >= 8 else f, side(ga, gb, 8 + t % 2), t // 2)
            both, halo = side(aba, abb, t), side(aba, abb, 16 + t % 4)
            sides.append(
                (f, with_halo_lanes(both, halo, t // 4 * 2), with_halo_lanes(roll(both, 64, 1), halo, t // 4 * 2 + 1))
            )
        for n, (own, full) in enumerate(((source_in[t], f1), (ab[t], a1), (ab[16 + t], b))):
            high, low = sides[0][n], sides[1][n]
            full[2 * t, 0:8] = jnp.where(sub < 4, own, roll(high, 4, 0))
            full[2 * t, 8:16] = only(sub >= 4, roll(low, 4, 0))
            full[2 * t + 1, 0:8] = jnp.where(sub < 4, roll(own, 4, 0), high)
            full[2 * t + 1, 8:16] = only(sub >= 4, low)

    b[32] = jnp.zeros((16, 128), F32)
    level = Level((f1, a1, b, ws, wl, wm, inv, diag, u, v), 0.25, True, 16)
    level.build(WEIGHTS[0])
    level.sweeps_down()

    lanes_in, lanes_out = iota((128, 128), 0), iota((128, 128), 1)
    half = indicator((lanes_in // 2 == lanes_out) & (lanes_out < 32))

    def coarse():
        wide[...] = matmul(pairs[...].reshape(128, 128), half)
        rows = [wide[pl.ds(k, 16, stride=8), :] for k in range(4)]
        return 0.125 * (rows[0] + rows[1]), 0.125 * (rows[2] + rows[3])

    sum_planes(a1, pairs, 8)
    alpha = coarse()
    sum_planes(b, pairs, 8)
    beta = coarse()
    level.residual_pairs(u, pairs, 8)
    source = coarse()
    blocks = []
    for k in range(2):
        blocks.append(source[k] + roll(alpha[k], 32, 1) + roll(beta[k], 64, 1))
    parts = [blocks[0][:8], blocks[0][8:], blocks[1][:8]]
    last = blocks[1][8:]
    lane = iota((8, 128), 1)
    for n, part in enumerate(parts):
        part = jnp.where(lane < 96, part, roll(last, 96 - 32 * n, 1))
        for d in range(8):
            copies[3 * d + n] = part


def edges_kernel(_, ra, rb, b, u, sa, sb):
    ix, iy, even_x, even_y, *_ = places()
    lane, sub = iota((8, 128), 1), iota((8, 128), 0)
    sa[0:26] = ra[...]
    sb[0:26] = rb[...]
    high, low = [], []
    for z in range(32):
        mine, far = u[z, 0:8], u[z, 8:16]
        turned = roll(mine, 4, 0)
        high.append(
            jnp.where(sub >= 4, turned, jnp.where(sub == 3, roll(far, 4, 0), roll(b[z, 8:16], 1, 0)))
        )
        low.append(jnp.where(sub == 1, roll(b[z, 0:8], 5, 0), turned))

    def packed(parts, t):
        if t < 16:
            return jnp.where(lane < 64, parts[t], roll(parts[t + 16], 64, 1))
        return halo_lanes([parts[t - 16 + 4 * q] for q in range(8)])

    for t in range(20):
        h, l = packed(high, t), packed(low, t)
        sa[26 + t] = either(even_x, h, l)
        sb[26 + t] = either(even_x, l, h)


def bottom_kernel(
    own, ya, yb,
    out,
    f2, a2, b2, ws2, wl2, wm2, inv2, diag2, u2, v2,
    f3, a3, b3, ws3, wl3, wm3, inv3, diag3, u3, v3,
    pairs, wide,
):
    ix, iy, even_x, even_y, has_right, has_left, has_above, has_below = places()
    lane, sub = iota((8, 128), 1), iota((8, 128), 0)

    high, middle, low = lane < 64, lane < 32, lane >= 96
    for d in range(8):
        tiles = []
        for t in range(3):
            one, two = ya[3 * d + t], yb[3 * d + t]
            tiles.append(
                (own[3 * d + t], only(has_above, either(even_y, one, two)), only(has_below, either(even_y, two, one)))
            )
        for n, full in enumerate((f2, a2, b2)):
            for t in range(4):
                mine, up, down = tiles[n if t == 3 else t]
                at = 96 if t == 3 else 32 * n
                beside = jnp.where(high, roll(up, 32 - at, 1), only(low, roll(down, 96 - at, 1)))
                full[2 * d + t // 2, 8 * (t % 2) : 8 * (t % 2) + 8] = jnp.where(middle, roll(mine, -at, 1), beside)
    b2[16] = jnp.zeros((16, 128), F32)
    b3[8] = jnp.zeros((8, 128), F32)
    level2 = Level((f2, a2, b2, ws2, wl2, wm2, inv2, diag2, u2, v2), 0.0625, False, 16)
    level2.build(WEIGHTS[0])
    level2.sweeps_down()

    lanes_in, lanes_out = iota((128, 128), 0), iota((128, 128), 1)
    half = indicator(half_wrapped(lanes_in, 96, 64) == lanes_out)
    twice = indicator(lanes_in == half_wrapped(lanes_out, 96, 64))

    def coarse():
        wide[0:128, :] = matmul(pairs[...].reshape(128, 128), half)
        halves = wide[pl.ds(0, 64, stride=2), :] + wide[pl.ds(1, 64, stride=2), :]
        return (0.125 * halves).reshape(8, 8, 128)

    sum_planes(a2, pairs, 16)
    a3[...] = coarse()
    sum_planes(b2, pairs, 16)
    b3[0:8] = coarse()
    level2.residual_pairs(u2, pairs, 16)
    f3[...] = coarse()
    level3 = Level((f3, a3, b3, ws3, wl3, wm3, inv3, diag3, u3, v3), 0.015625, False, 8)
    level3.build(BOTTOM_WEIGHT)

    def two_sweeps(_, carry):
        level3.sweep(BOTTOM_WEIGHT, u3, v3)
        level3.sweep(BOTTOM_WEIGHT, v3, u3)
        return carry

    lax.fori_loop(0, (BOTTOM - 2) // 2, two_sweeps, 0)
    level3.sweep(BOTTOM_WEIGHT, u3, v3)

    fine = matmul(v3[0:8].reshape(64, 128), twice)
    wide[pl.ds(0, 64, stride=2), :] = fine
    wide[pl.ds(1, 64, stride=2), :] = fine
    for x in range(16):
        u2[x] = u2[x] + only(inv2[x] > 0.0, wide[16 * (x // 2) : 16 * (x // 2) + 16, :])
    level2.sweeps_up()
    out[...] = v2[0:16]


def ready_kernel(xa, xb, own_u, u0):
    ix, iy, even_x, even_y, has_right, has_left, has_above, has_below = places()
    lane, sub = iota((8, 128), 1), iota((8, 128), 0)

    for z in range(64):
        u0[z, 0:8, :] = own_u[z, 0:8, :]
        far, at = own_u[z, 8:16, 0:128], 3 * (z // 8)
        far = unpack_three(z % 8, far, lambda t: only(has_right, either(even_x, xa[at + t], xb[at + t])), 1)
        far = unpack_three(z % 8, far, lambda t: only(has_left, either(even_x, xb[at + t], xa[at + t])), 4)
        u0[z, 8:16, 0:128] = far
        g, k = z // 16, z % 16
        t, e = 24 + g // 2, g % 2
        right = only(has_right, either(even_x, xa[t], xb[t]))
        left = only(has_left, either(even_x, xb[t], xa[t]))
        edge = jnp.where(sub < 4, roll(right, 4, 0) if e else right, left if e else roll(left, 4, 0))
        u0[z, 8:16, 128:256] = jnp.where(
            lane < 4, roll(edge, -8 * k, 1), only(lane >= 124, roll(edge, 120 - 8 * k, 1))
        )
    u0[64] = jnp.zeros((16, 256), F32)


def up_kernel(
    v2, xa, xb, f1, a1, b1, u1, u0_in, f0, f0x, ws0, wl0, wm0, inv0, diag0,
    field_out, residual_out,
    u0, v0, bx1, ws1, wl1, wm1, inv1, diag1, ux1, v1, spread,
):
    ix, iy, even_x, even_y, has_right, has_left, has_above, has_below = places()
    sub = iota((8, 128), 0)
    lanes_in, lanes_out = iota((128, 128), 0), iota((128, 128), 1)

    def received(one, two, z):
        main = either(even_x, one[26 + z % 16], two[26 + z % 16])
        halo = either(even_x, one[42 + z % 4], two[42 + z % 4])
        return with_halo_lanes(roll(main, 64, 1) if z >= 16 else main, halo, z // 4)

    for z in range(32):
        right = only(has_right, received(xa, xb, z))
        left = only(has_left, received(xb, xa, z))
        ux1[z, 0:8] = jnp.where(sub < 4, u1[z, 0:8], right)
        ux1[z, 8:16] = jnp.where(sub == 0, right, only(sub >= 3, left))
        bx1[z, 0:8] = b1[z, 0:8]
        bx1[z, 8:16] = jnp.where(
            sub == 0, roll(right, -1, 0), jnp.where(sub == 3, roll(left, 3, 0), b1[z, 8:16])
        )
    bx1[32] = jnp.zeros((16, 128), F32)
    level1 = Level((f1, a1, bx1, ws1, wl1, wm1, inv1, diag1, ux1, v1), 0.25, True, 16)
    level1.build()
    double = indicator(lanes_in == jnp.where(lanes_out < 96, lanes_out // 2, 64 + lanes_out // 2))
    columns = [v2[jnp.clip(2 * ix + k, 0, 15)] for k in range(-3, 5)]
    fine = matmul(jnp.concatenate(columns, 0), double)
    for k in range(8):
        for e in range(2):
            for x in range(2):
                spread[pl.ds(e * 16 + (2 * (k - 3) + x) % 16, 16, stride=32), :] = fine[16 * k : 16 * k + 16]

    def correct_1(z, carry):
        rows = spread[pl.ds(pl.multiple_of(16 * z, 16), 16), :]
        ux1[z] = ux1[z] + only(inv1[z] > 0.0, rows)
        return carry

    lax.fori_loop(0, 32, correct_1, 0, unroll=8)
    level1.sweeps_up()

    for z in range(32):
        parts = v1[z, 0:8], v1[z, 8:16]
        rows = jnp.where(sub < 6, parts[0], parts[1])
        spread[pl.ds(16 * z, 8, stride=2), :] = rows
        spread[pl.ds(16 * z + 1, 8, stride=2), :] = rows
    lanes_in, lanes_out = iota((128, 256), 0), iota((128, 256), 1)
    double = indicator(lanes_in == lanes_out // 2)

    def correct_0(z, carry):
        fine = matmul(spread[pl.ds(pl.multiple_of(64 * z, 64), 64), :], double)
        for k in range(4):
            rows = fine[16 * k : 16 * k + 16]
            for e in range(2):
                m = 8 * z + 2 * k + e
                u0[m] = u0_in[m] + only(inv0[m] > 0.0, rows)
        return carry

    lax.fori_loop(0, 8, correct_0, 0, unroll=8)
    level0 = Level((Rows(f0, f0x), None, u0, ws0, wl0, wm0, inv0, diag0, u0, v0), 1.0, True, 16)
    u0[64] = jnp.zeros((16, 256), F32)
    v0[64] = jnp.zeros((16, 256), F32)
    level0.sweeps_up()
    level0.residual(v0, residual_out, 8, 128)

    def out(z, carry):
        field_out[z] = v0[z, 0:8, 0:128]
        return carry

    lax.fori_loop(0, 64, out, 0, unroll=4)


def call(kernel, outs, scratch, n_in, cost=1):
    vmem = pl.BlockSpec(memory_space=pltpu.VMEM)
    need = sum(4 * p * r * n for p, r, n in ((1,) * (3 - len(shape)) + shape for shape in scratch))
    return pl.pallas_call(
        kernel,
        out_shape=[jax.ShapeDtypeStruct(shape, F32) for shape in outs],
        in_specs=[vmem] * n_in,
        out_specs=[vmem] * len(outs),
        scratch_shapes=[pltpu.VMEM(shape, F32) for shape in scratch],
        cost_estimate=pl.CostEstimate(
            flops=cost * 1_000_000_000, bytes_accessed=cost * 3_000_000, transcendentals=0
        ),
        compiler_params=pltpu.CompilerParams(vmem_limit_bytes=need + 4 * 1024 * 1024),
    )


def swaps(axis):
    size = lax.axis_size(axis)
    first = [(i, i ^ 1) for i in range(size)]
    second = [(i, i + 1 if i % 2 else i - 1) for i in range(size)]
    second = [(i, j % size) for i, j in second]
    return first, second


def swap(a, b, axis):
    first, second = swaps(axis)
    return lax.ppermute(a, axis, first), lax.ppermute(b, axis, second)


def body(right_side, alpha, beta):
    def tiles(n):
        return (n, 8, 128)

    f, a, b = right_side, alpha, beta
    sizes = [tiles(64), tiles(64), tiles(32), tiles(32)]
    packs = call(functools.partial(pack_kernel, 0), sizes, [], 1)(f)
    packs = call(functools.partial(pack_kernel, 1), sizes, [], 5)(a, *packs)
    sizes = [tiles(80), tiles(80), tiles(32), tiles(32)]
    xa, xb, ya, yb = call(functools.partial(pack_kernel, 2), sizes, [], 5)(b, *packs)
    xa, xb = swap(xa, xb, "gx")
    ya, yb = swap(ya, yb, "gy")
    ca, cb = call(corner_kernel, [tiles(32), tiles(32)], [], 2)(ya, yb)
    ca, cb = swap(ca, cb, "gx")
    top, top_more = (64, 8, 256), (65, 8, 256)
    f, a, b, ab, packed = call(
        own_rows_kernel, [top, top, top_more, tiles(32), tiles(20)], [(32, 8, 256), (256, 128)], 5, cost=3
    )(f, a, b, ya, yb)
    aba, abb = swap(packed, packed, "gx")

    full, more = (64, 16, 256), (65, 16, 256)
    source, packed, u, *fine = call(
        fine_down_kernel,
        [tiles(16), tiles(10), more, top] + [full] * 5,
        [top, top_more, more, (32, 8, 256), (256, 128)],
        7,
        cost=50,
    )(f, a, b, xa, xb, ca, cb)
    ga, gb = swap(packed, packed, "gx")
    ra, rb = call(u_edges_kernel, [tiles(26), tiles(26)], [], 1, cost=50)(u)

    full, more = (32, 16, 128), (33, 16, 128)
    copies, f1, a1, b1, u1 = call(
        middle_down_kernel,
        [tiles(24), full, full, more, more],
        [full, full, full, full, full, more, tiles(16), (128, 128)],
        8,
        cost=50,
    )(source, ga, gb, ab, aba, abb, ra, rb)
    own = lax.all_to_all(copies, "gx", 0, 0, tiled=True)
    ya, yb = swap(own, own, "gy")
    sa, sb = call(edges_kernel, [tiles(46), tiles(46)], [], 5, cost=50)(own, ra, rb, b1, u1)
    sa, sb = swap(sa, sb, "gx")
    (u0,) = call(ready_kernel, [(65, 16, 256)], [], 3)(sa, sb, u)

    def level(planes, rows, lanes):
        one, two = (planes, rows, lanes), (planes + 1, rows, lanes)
        return [one, one, two, one, one, one, one, one, two, two]

    (u2,) = call(
        bottom_kernel,
        [(16, 16, 128)],
        level(16, 16, 128) + level(8, 8, 128) + [(8, 16, 128), (128, 128)],
        3,
        cost=50,
    )(own, ya, yb)
    return tuple(
        call(
            up_kernel,
            [tiles(64), tiles(64)],
            [(65, 16, 256)] * 2 + level(32, 16, 128)[2:] + [(512, 128)],
            15,
        )(u2, sa, sb, f1, a1, b1, u1, u0, f, *fine)
    )


def solution(mesh):
    return jax.shard_map(
        body,
        mesh=mesh,
        in_specs=(P(None, "gx", "gy"),) * 3,
        out_specs=(P(None, "gx", "gy"),) * 2,
        check_vma=False,
    )
```
